128 devices in a mesh: rows: 32 (over y, z, core), probe: 4 (over x).
Axes of the slice: x: 4, y: 4, z: 4, core: 2. Of those that a mesh axis runs over, the one named last changes fastest.
Arguments:
- states: bfloat16 [32768, 256], P('rows'), may hold values from -1 to 1
- offsets: int32 [32], P('rows'), may hold values from 0 to 512, as said below
- right_side: float32 [16384, 64], P('rows', 'probe'), may hold values from -6 to 6
Outputs:
- solution_field: float32 [16384, 64], P('rows', 'probe')
- residual: float32 [16384, 64], P('rows', 'probe')
The draws below stay inside these ranges and needn't reach their ends.
Inputs may be any that keep to these rules, and one draw needn't show every extreme that they name: `offsets`: each window of 512 states lies inside its block; some block starts at 0 and some at 512.
All inputs are finite; a program needn't handle non-finite values.
Results may differ from the reference program's by a relative error of at most 0.0056.
Values may be sent and summed in bfloat16 or wider, within the bound.
No kernel may reach another device: no remote copies, remote signals or barrier semaphores. Data moves between devices by JAX's collectives and lax.ppermute only.
A program may use at most 64 MiB of HBM per device.

```python
import math
import jax
import jax.numpy as jnp
from jax import lax

F = 256
P_SIZE = 64
R_DEV = 512
ITERS = 2
STATE_DEV = 1024
STATES = 32768
POINTS = 16384
N_ROWS = 32


def draw_offsets(key, part):
    key = jax.random.fold_in(key, 7)
    first_key, second_key = jax.random.split(key)
    values = jax.random.randint(first_key, (N_ROWS,), 0, R_DEV + 1, dtype=jnp.int32)
    order = jax.random.permutation(second_key, N_ROWS)
    values = values.at[order[0]].set(R_DEV).at[order[1]].set(0)
    return values


def draw_states(key, part):
    key = jax.random.fold_in(key, 11)
    latent_key, slope_key, shift_key, jitter_key = jax.random.split(key, 4)
    drivers = 8
    latent = jax.random.normal(latent_key, (STATES, drivers), jnp.float32)
    jitter = 0.3 * jax.random.normal(jitter_key, (STATES, F), jnp.float32)
    slope = jnp.exp(jax.random.uniform(slope_key, (F,), jnp.float32, math.log(0.5), math.log(2.0)))
    shift = jax.random.uniform(shift_key, (F,), jnp.float32, -1.0, 1.0)
    lifted = jnp.tile(latent, (1, F // drivers))
    return (4.0 / math.sqrt(F) * jnp.tanh(slope[None, :] * lifted + shift[None, :] + jitter)).astype(jnp.bfloat16)


def steps_of(key, shape, cuts, least, top_value):
    def one(axis_at, parts):
        steps = jax.random.uniform(jax.random.fold_in(jax.random.fold_in(key, 6), axis_at), (parts,), jnp.float32, least / len(cuts), top_value / len(cuts))
        return jnp.repeat(jnp.exp(steps), shape[axis_at] // parts).reshape((-1,) + (1,) * (len(shape) - axis_at - 1))

    gain = one(*cuts[0])
    for cut in cuts[1:]:
        gain = gain * one(*cut)
    return gain


def bell_draw(own_key, shape, width, bound, cuts=(), kind=jnp.bfloat16):
    entries = width * jax.random.normal(own_key, shape, jnp.float32)
    if cuts:
        entries = entries * steps_of(own_key, shape, cuts, -0.22, 0.18)
    return jnp.clip(entries, -bound, bound).astype(kind)


def setup_inputs(seed: int = 0) -> dict:
    splits = jax.random.split(jax.random.key(seed), 4)
    states = draw_states(jax.random.fold_in(splits[3], 71), 0)
    offsets = draw_offsets(jax.random.fold_in(splits[3], 71), 0)
    right_side = bell_draw(splits[2], (POINTS, P_SIZE), 1.0, 6.0, ((0, 32), (1, 4)), jnp.float32)
    return {"states": states, "offsets": offsets, "right_side": right_side}


noise_level = 1.0
kernel_rate = 0.5


def reference(states, offsets, right_side):
    blocks = jnp.arange(N_ROWS, dtype=jnp.int32)
    starts = (blocks * STATE_DEV + offsets).astype(jnp.int32)
    index_grid = starts[:, None] + jnp.arange(R_DEV, dtype=jnp.int32)[None, :]
    points = states[index_grid.reshape(-1)]
    norms = jnp.sum(points.astype(jnp.float32) ** 2, axis=1)
    point_blocks = points.reshape(N_ROWS, R_DEV, F)
    norm_blocks = norms.reshape(N_ROWS, R_DEV)

    def apply(direction):
        narrow = direction.astype(jnp.bfloat16)

        def one_block(inputs):
            block_points, block_norms = inputs
            cross = lax.dot_general(block_points, points, (((1,), (1,)), ((), ())), preferred_element_type=jnp.float32)
            dist = block_norms[:, None] + norms[None, :] - 2.0 * cross
            kern = jnp.exp(-kernel_rate * dist).astype(jnp.bfloat16)
            return jnp.dot(kern, narrow, preferred_element_type=jnp.float32)

        image = lax.map(one_block, (point_blocks, norm_blocks)).reshape(POINTS, P_SIZE)
        return image + noise_level * direction

    solution_field = jnp.zeros_like(right_side)
    residual = right_side
    direction = right_side
    norm_now = jnp.sum(residual * residual, axis=0)
    for iteration in range(ITERS):
        image = apply(direction)
        alpha = norm_now / jnp.sum(direction * image, axis=0)
        solution_field = solution_field + alpha * direction
        residual = residual - alpha * image
        if iteration + 1 < ITERS:
            norm_next = jnp.sum(residual * residual, axis=0)
            direction = residual + (norm_next / norm_now) * direction
            norm_now = norm_next
    return solution_field, residual
```

```python
import functools

import jax
import jax.numpy as jnp
from jax import lax
from jax.experimental import pallas as pl
from jax.experimental.pallas import tpu as pltpu
from jax.sharding import Mesh
from jax.sharding import PartitionSpec as P

NY, NZ, NC, NX = 4, 4, 2, 4
LANES = 128

noise_level = 1.0
kernel_rate = 0.5


def shift(value, axis, size, step):
    return lax.ppermute(value, axis, [(i, (i + step) % size) for i in range(size)])


def others(value, axis, size):
    return [shift(value, axis, size, k) for k in range(1, size)]


def prepare_kernel(points_ref, side_ref, out_ref):
    probes = side_ref.shape[1]
    out_ref[:probes, :] = side_ref[...].T
    squares = points_ref[...].astype(jnp.float32) ** 2
    norms = jnp.sum(squares, axis=1, keepdims=True)
    out_ref[probes:, :] = jnp.broadcast_to(norms, (norms.shape[0], 8)).T


def prepare(points, side):
    rows, probes = side.shape
    return pl.pallas_call(
        prepare_kernel,
        out_shape=jax.ShapeDtypeStruct((probes + 8, rows), jnp.float32),
        name="prepare",
    )(points, side)


def tile_kernel(probes, chunk, row_ref, col_ref, field_ref, tile_ref, image_ref, half_ref):
    @pl.when(pl.program_id(0) == 0)
    def _():
        image_ref[...] = jnp.zeros_like(image_ref)
        squares = row_ref[...].astype(jnp.float32) ** 2
        half_ref[...] = -kernel_rate * jnp.sum(squares, axis=1, keepdims=True)

    field = field_ref[:probes, :].astype(jnp.bfloat16)
    col_half = -kernel_rate * field_ref[probes : probes + 1, :]
    for i in range(row_ref.shape[0] // chunk):
        rows = pl.ds(i * chunk, chunk)
        cross = lax.dot_general(
            row_ref[rows, :], col_ref[...], (((1,), (1,)), ((), ())), preferred_element_type=jnp.float32
        )
        kern = jnp.exp(2.0 * kernel_rate * cross + half_ref[rows, :] + col_half).astype(jnp.bfloat16)
        tile_ref[rows, :] = kern
        image_ref[:, rows] += lax.dot_general(
            field, kern, (((1,), (1,)), ((), ())), preferred_element_type=jnp.float32
        )


def build_tile(row_points, col_points, col_field, probes):
    rows, features = row_points.shape
    cols = col_points.shape[0]
    chunk, block = 256, 512
    height = col_field.shape[0]
    return pl.pallas_call(
        functools.partial(tile_kernel, probes, chunk),
        grid=(cols // block,),
        in_specs=[
            pl.BlockSpec((rows, features), lambda j: (0, 0)),
            pl.BlockSpec((block, features), lambda j: (j, 0)),
            pl.BlockSpec((height, block), lambda j: (0, j)),
        ],
        out_specs=[
            pl.BlockSpec((rows, block), lambda j: (0, j)),
            pl.BlockSpec((probes, rows), lambda j: (0, 0)),
        ],
        out_shape=[
            jax.ShapeDtypeStruct((rows, cols), jnp.bfloat16),
            jax.ShapeDtypeStruct((probes, rows), jnp.float32),
        ],
        scratch_shapes=[pltpu.VMEM((rows, 1), jnp.float32)],
        compiler_params=pltpu.CompilerParams(vmem_limit_bytes=24 << 20),
        cost_estimate=pl.CostEstimate(
            flops=2 * rows * cols * (features + 256), bytes_accessed=24 << 20, transcendentals=rows * cols
        ),
        name="build_tile",
    )(row_points, col_points, col_field)


def second_kernel(own, tile_ref, side_r, image_r, side_c, image_c, sums_ref, part_ref, own_ref, out_sums):
    sums = sums_ref[...]
    rr, curve, square = sums[:, 0:1], sums[:, 1:2], sums[:, 2:3]
    alpha = rr / curve
    rr_next = rr - 2.0 * alpha * curve + alpha * alpha * square
    beta = rr_next / rr
    res_r = side_r[...] - alpha * image_r[...]
    dir_r = res_r + beta * side_r[...]
    narrow = dir_r.astype(jnp.bfloat16)
    total = jnp.zeros_like(alpha)
    block = 1024
    for j in range(tile_ref.shape[1] // block):
        cols = pl.ds(j * block, block)
        part = jnp.dot(narrow, tile_ref[:, cols], preferred_element_type=jnp.float32)
        part_ref[:, cols] = part
        res_c = side_c[:, cols] - alpha * image_c[:, cols]
        dir_c = res_c + beta * side_c[:, cols]
        total = total + jnp.sum(part * dir_c, axis=1, keepdims=True)
    own_res, own_dir = res_r[:, :own], dir_r[:, :own]
    own_ref[0] = own_res
    own_ref[1] = own_dir
    own_ref[2] = alpha * side_r[:, :own]
    total = total + noise_level * jnp.sum(own_dir * own_dir, axis=1, keepdims=True)
    rr_own = jnp.sum(own_res * own_res, axis=1, keepdims=True)
    lane = lax.broadcasted_iota(jnp.int32, out_sums.shape, 1)
    out_sums[...] = jnp.where(lane == 0, total, jnp.where(lane == 1, rr_own, 0.0))


def second_product(tile, side_r, image_r, side_c, image_c, sums, own):
    rows, cols = tile.shape
    probes = side_r.shape[0]
    return pl.pallas_call(
        functools.partial(second_kernel, own),
        out_shape=[
            jax.ShapeDtypeStruct((probes, cols), jnp.float32),
            jax.ShapeDtypeStruct((3, probes, own), jnp.float32),
            jax.ShapeDtypeStruct((probes, LANES), jnp.float32),
        ],
        compiler_params=pltpu.CompilerParams(vmem_limit_bytes=24 << 20),
        cost_estimate=pl.CostEstimate(flops=2 * rows * cols * 256, bytes_accessed=20 << 20, transcendentals=0),
        name="second_product",
    )(tile, side_r, image_r, side_c, image_c, sums)


def on_device(states, offsets, right_side):
    own, probes = right_side.shape
    points = lax.dynamic_slice_in_dim(states, offsets[0], own, 0)
    with jax.named_scope("fetch_points"):
        row_points = jnp.concatenate([points] + others(points, "z", NZ), axis=0)
        col_points = jnp.concatenate([points] + others(points, "y", NY), axis=0)
        packed = prepare(points, right_side)
        side = packed[:probes]
        side_r = jnp.concatenate([side] + others(side, "z", NZ), axis=1)
        packed_c = jnp.concatenate([packed] + others(packed, "y", NY), axis=1)
        col_points = jnp.concatenate([col_points, shift(col_points, "c", NC, 1)], axis=0)
        packed_c = jnp.concatenate([packed_c, shift(packed_c, "c", NC, 1)], axis=1)
        side_c = packed_c[:probes]

    tile, part = build_tile(row_points, col_points, packed_c, probes)

    with jax.named_scope("sum_over_z"):
        image_r = part + noise_level * side_r
        for s, other in enumerate(others(part, "z", NZ), 1):
            image_r = image_r + jnp.concatenate([other[:, (NZ - s) * own :], other[:, : (NZ - s) * own]], axis=1)
        sums = jnp.stack(
            [jnp.sum(side_r * side_r, axis=1), jnp.sum(side_r * image_r, axis=1), jnp.sum(image_r * image_r, axis=1)],
            axis=1,
        )
        sums = jnp.pad(sums, ((0, 0), (0, LANES - 3)))

    with jax.named_scope("gather_image"):
        message = jnp.concatenate([image_r[:, :own], sums], axis=1)
        pair = jnp.stack([message, shift(message, "c", NC, 1)])
        every = jnp.stack([pair] + others(pair, "y", NY), axis=1)
        image_c = every[:, :, :, :own].transpose(2, 0, 1, 3).reshape(probes, -1)
        sums = jnp.sum(every[:, :, :, own:], axis=(0, 1))

    part, held, sums = second_product(tile, side_r, image_r, side_c, image_c, sums, own)

    with jax.named_scope("sum_over_yc"):
        half = NY * own
        message = jnp.concatenate([part[:, half:], sums], axis=1)
        message = shift(message, "c", NC, 1)
        mine = part[:, :half] + message[:, :half]
        sums = sums + message[:, half:]
        image = mine[:, :own]
        total = sums
        for m in range(1, NY):
            message = jnp.concatenate([mine[:, m * own : (m + 1) * own], sums], axis=1)
            message = shift(message, "y", NY, -m)
            image = image + message[:, :own]
            total = total + message[:, own:]

    with jax.named_scope("sum_sums_over_z"):
        for other in others(total, "z", NZ):
            total = total + other

    alpha = total[:, 1:2] / total[:, 0:1]
    residual, direction, field = held[0], held[1], held[2]
    image = image + noise_level * direction
    field = field + alpha * direction
    residual = residual - alpha * image
    return field.T, residual.T


def solution(mesh):
    fine = Mesh(mesh.devices.reshape(NY, NZ, NC, NX), ("y", "z", "c", "x"))
    rows = ("y", "z", "c")
    in_specs = (P(rows, None), P(rows), P(rows, "x"))
    out_specs = (P(rows, "x"), P(rows, "x"))
    return jax.shard_map(on_device, mesh=fine, in_specs=in_specs, out_specs=out_specs, check_vma=False)
```

```python
import functools

import jax
import jax.numpy as jnp
from jax import lax
from jax.experimental import pallas as pl
from jax.experimental.pallas import tpu as pltpu
from jax.sharding import Mesh
from jax.sharding import PartitionSpec as P

NY, NZ, NC, NX = 4, 4, 2, 4
LANES = 128
CHUNK = 256
ROWS = (0, 1, 3, 2)
COLS = ((0, 0), (1, 0), (0, 1), (0, 3), (1, 1), (1, 3), (0, 2), (1, 2))

noise_level = 1.0
kernel_rate = 0.5


def shift(value, axis, size, step):
    return lax.ppermute(value, axis, [(i, (i + step) % size) for i in range(size)])


def split_rows(value):
    high = value.astype(jnp.bfloat16).astype(jnp.float32)
    middle = (value - high).astype(jnp.bfloat16).astype(jnp.float32)
    return high, middle, value - high - middle


def pack_kernel(points_ref, side_ref, out_ref):
    own, width = points_ref.shape
    probes = side_ref.shape[0]
    out_ref[:own, :] = points_ref[...]
    norms = jnp.sum(points_ref[...].astype(jnp.float32) ** 2, axis=1, keepdims=True)
    norms = jnp.broadcast_to(norms, (own, LANES)).T[:16, :]
    high, middle, low = split_rows(norms)
    row = lax.broadcasted_iota(jnp.int32, norms.shape, 0)
    norms = jnp.where(row == 0, high, jnp.where(row == 1, middle, jnp.where(row == 2, low, 0.0)))
    high, middle, _ = split_rows(side_ref[...])
    at = own
    for part in (high, middle, norms):
        for j in range(own // width):
            out_ref[at : at + probes, :] = part[:, j * width : (j + 1) * width].astype(jnp.bfloat16)
            at += probes


def pack(points, side):
    own, width = points.shape
    extra = side.shape[0] * 3 * own // width
    return pl.pallas_call(
        pack_kernel,
        out_shape=jax.ShapeDtypeStruct((own + extra, width), jnp.bfloat16),
        name="pack",
    )(points, side)


def unpack_rows(message, probes, own, term):
    width = message.shape[1]
    count = own // width
    at = own + term * count * probes
    return jnp.concatenate([message[at + j * probes : at + (j + 1) * probes] for j in range(count)], axis=1)


def tile_kernel(counts, probes, *refs):
    rows_count, cols_count, known_halves, prior_count, has_side = counts
    refs = list(refs)
    row_refs = [refs.pop(0) for _ in range(rows_count)]
    col_refs = [refs.pop(0) for _ in range(cols_count)]
    half_refs = [refs.pop(0) for _ in range(known_halves)]
    prior_refs = [refs.pop(0) for _ in range(prior_count)]
    side_ref = refs.pop(0) if has_side else None
    tile_ref, image_ref = refs.pop(0), refs.pop(0)
    own = row_refs[0].shape[0]
    if known_halves:
        pieces = []
        for half_ref in half_refs:
            pieces += [half_ref[j * own : (j + 1) * own, :] for j in range(half_ref.shape[0] // own)]
        halves = pieces
    else:
        new_ref = refs.pop(0)
        halves = []
        for i, row_ref in enumerate(row_refs):
            squares = row_ref[...].astype(jnp.float32) ** 2
            halves.append(-kernel_rate * jnp.sum(squares, axis=1, keepdims=True))
            new_ref[i * own : (i + 1) * own, :] = halves[-1]
    if prior_count:
        at = 0
        for prior_ref in prior_refs:
            image_ref[:, at : at + prior_ref.shape[1]] = prior_ref[...]
            at += prior_ref.shape[1]
    else:
        image_ref[...] = jnp.zeros_like(image_ref)
        if has_side:
            image_ref[:, :own] = noise_level * side_ref[...]
    for j, col_ref in enumerate(col_refs):
        field = unpack_rows(col_ref, probes, own, 0)
        norms = unpack_rows(col_ref, probes, own, 2).astype(jnp.float32)
        col_half = -kernel_rate * (norms[0:1] + norms[1:2] + norms[2:3])
        for i, row_ref in enumerate(row_refs):
            for k in range(own // CHUNK):
                part = slice(k * CHUNK, (k + 1) * CHUNK)
                place = slice(i * own + k * CHUNK, i * own + (k + 1) * CHUNK)
                cross = lax.dot_general(
                    row_ref[part, :], col_ref[:own, :], (((1,), (1,)), ((), ())), preferred_element_type=jnp.float32
                )
                kern = jnp.exp(2.0 * kernel_rate * cross + halves[i][part, :] + col_half).astype(jnp.bfloat16)
                tile_ref[place, j * own : (j + 1) * own] = kern
                image_ref[:, place] += lax.dot_general(
                    field, kern, (((1,), (1,)), ((), ())), preferred_element_type=jnp.float32
                )


def build(rows, cols, probes, halves=(), prior=(), side=None):
    own, features = rows[0].shape
    height, width = len(rows) * own, len(cols) * own
    counts = (len(rows), len(cols), len(halves), len(prior), side is not None)
    out_shape = [
        pltpu.VMEM((height, width), jnp.bfloat16),
        jax.ShapeDtypeStruct((probes, height), jnp.float32),
    ]
    if not halves:
        out_shape.append(jax.ShapeDtypeStruct((height, 1), jnp.float32))
    args = [*rows, *cols, *halves, *prior] + ([] if side is None else [side])
    return pl.pallas_call(
        functools.partial(tile_kernel, counts, probes),
        out_shape=out_shape,
        compiler_params=pltpu.CompilerParams(vmem_limit_bytes=16 << 20),
        cost_estimate=pl.CostEstimate(
            flops=2 * height * width * (features + 256), bytes_accessed=1 << 20, transcendentals=height * width
        ),
        name="build_tile",
    )(*args)


def second_kernel(own, tiles, image_r, side_r, image_c, side_c, sums_ref, mine_ref, other_ref, own_ref):
    sums = sums_ref[...]
    rr, curve, square = sums[:, 0:1], sums[:, 1:2], sums[:, 2:3]
    alpha = rr / curve
    rr_next = rr - 2.0 * alpha * curve + alpha * alpha * square
    beta = rr_next / rr
    res_r = side_r[...] - alpha * image_r[...]
    dir_r = res_r + beta * side_r[...]
    narrow = dir_r.astype(jnp.bfloat16)
    total = jnp.zeros_like(alpha)
    for j, (h, m) in enumerate(COLS):
        part = 0.0
        for tile_ref, top, left in tiles:
            at = j * own - left
            if 0 <= at < tile_ref.shape[1]:
                part = part + jnp.dot(
                    narrow[:, top : top + tile_ref.shape[0]],
                    tile_ref[:, at : at + own],
                    preferred_element_type=jnp.float32,
                )
        cols = slice(j * own, (j + 1) * own)
        dir_c = (side_c[:, cols] - alpha * image_c[:, cols]) + beta * side_c[:, cols]
        total = total + jnp.sum(part * dir_c, axis=1, keepdims=True)
        (other_ref if h else mine_ref)[:, m * own : (m + 1) * own] = part
    own_res, own_dir = res_r[:, :own], dir_r[:, :own]
    own_ref[0] = own_res
    own_ref[1] = own_dir
    own_ref[2] = alpha * side_r[:, :own]
    total = total + noise_level * jnp.sum(own_dir * own_dir, axis=1, keepdims=True)
    rr_own = jnp.sum(own_res * own_res, axis=1, keepdims=True)
    lane = lax.broadcasted_iota(jnp.int32, (total.shape[0], LANES), 1)
    out_sums = jnp.where(lane == 0, total, jnp.where(lane == 1, rr_own, 0.0))
    mine_ref[:, NY * own :] = out_sums
    other_ref[:, NY * own :] = out_sums


def second_product(tiles, image_r, side_r, image_c, side_c, sums, own):
    probes, rows = side_r.shape
    cols = side_c.shape[1]
    places = [(top, left) for _, top, left in tiles]

    def kernel(*refs):
        held = [(ref, top, left) for ref, (top, left) in zip(refs, places)]
        second_kernel(own, held, *refs[len(places) :])

    return pl.pallas_call(
        kernel,
        in_specs=[pl.BlockSpec(memory_space=pltpu.VMEM)] * (len(tiles) + 5),
        out_shape=[
            jax.ShapeDtypeStruct((probes, cols // NC + LANES), jnp.float32),
            jax.ShapeDtypeStruct((probes, cols // NC + LANES), jnp.float32),
            jax.ShapeDtypeStruct((3, probes, own), jnp.float32),
        ],
        compiler_params=pltpu.CompilerParams(vmem_limit_bytes=16 << 20),
        cost_estimate=pl.CostEstimate(flops=2 * rows * cols * 256, bytes_accessed=1 << 20, transcendentals=0),
        name="second_product",
    )(*[tile for tile, _, _ in tiles], image_r, side_r, image_c, side_c, sums)


def on_device(states, offsets, right_side):
    own, probes = right_side.shape
    side = right_side.T
    points = lax.dynamic_slice_in_dim(states, offsets[0], own, 0)
    with jax.named_scope("fetch_points"):
        row = {0: points}
        for k in (1, 3, 2):
            row[k] = shift(points, "z", NZ, k)
        message = pack(points, side)
        col = {(0, 0): message, (1, 0): shift(message, "c", NC, 1)}
        for m in (1, 3, 2):
            col[0, m] = shift(message, "y", NY, m)
        for m in (1, 3, 2):
            col[1, m] = shift(col[0, m], "c", NC, 1)
        near = [row[k] for k in ROWS[:3]]
        col = [col[at] for at in COLS]

    with jax.named_scope("build_tiles"):
        tile_a, image, half = build(near, col[:2], probes, side=side)
        tile_b, image = build(near, col[2:4], probes, [half], [image])
        tile_c, image = build(near, col[4:6], probes, [half], [image])
        tile_d, image_far, half_far = build([row[2]], col[:6], probes)
        tile_e, image = build(near + [row[2]], col[6:], probes, [half, half_far], [image, image_far])
        far = 3 * own
        tiles = [
            (tile_a, 0, 0),
            (tile_b, 0, 2 * own),
            (tile_c, 0, 4 * own),
            (tile_d, far, 0),
            (tile_e, 0, 6 * own),
        ]
        side_c = [unpack_rows(one, probes, own, 0) + unpack_rows(one, probes, own, 1).astype(jnp.float32) for one in col]
        side_c = jnp.concatenate(side_c, axis=1)

    with jax.named_scope("sum_over_z"):
        message = jnp.concatenate([image, side], axis=1)
        every = {0: message}
        for s in (1, 3, 2):
            every[s] = shift(message, "z", NZ, s)
        pieces = []
        for p in ROWS:
            piece = 0.0
            for s in range(NZ):
                at = ROWS.index((p - s) % NZ) * own
                piece = piece + every[s][:, at : at + own]
            pieces.append(piece)
        image_r = jnp.concatenate(pieces, axis=1)
        side_r = jnp.concatenate([every[p][:, NZ * own :] for p in ROWS], axis=1)
        sums = jnp.stack(
            [jnp.sum(side_r * side_r, axis=1), jnp.sum(side_r * image_r, axis=1), jnp.sum(image_r * image_r, axis=1)],
            axis=1,
        )
        sums = jnp.pad(sums, ((0, 0), (0, LANES - 3)))

    with jax.named_scope("gather_image"):
        message = jnp.concatenate([image_r[:, :own], sums], axis=1)
        pair = jnp.concatenate([message, shift(message, "c", NC, 1)], axis=0)
        every = {0: pair}
        for m in (1, 3, 2):
            every[m] = shift(pair, "y", NY, m)
        image_c = jnp.concatenate([every[m][h * probes : (h + 1) * probes, :own] for h, m in COLS], axis=1)
        sums = sum(every[m][h * probes : (h + 1) * probes, own:] for h, m in COLS)

    mine, other, held = second_product(tiles, image_r, side_r, image_c, side_c, sums, own)

    with jax.named_scope("sum_over_yc"):
        mine = mine + shift(other, "c", NC, 1)
        image = mine[:, :own]
        sums = mine[:, NY * own :]
        total = sums
        for m in (1, 3, 2):
            message = jnp.concatenate([mine[:, m * own : (m + 1) * own], sums], axis=1)
            message = shift(message, "y", NY, -m)
            image = image + message[:, :own]
            total = total + message[:, own:]

    with jax.named_scope("sum_sums_over_z"):
        sums = total
        for k in (1, 3, 2):
            total = total + shift(sums, "z", NZ, k)

    alpha = total[:, 1:2] / total[:, 0:1]
    residual, direction, field = held[0], held[1], held[2]
    image = image + noise_level * direction
    field = field + alpha * direction
    residual = residual - alpha * image
    return field.T, residual.T


def solution(mesh):
    fine = Mesh(mesh.devices.reshape(NY, NZ, NC, NX), ("y", "z", "c", "x"))
    rows = ("y", "z", "c")
    in_specs = (P(rows, None), P(rows), P(rows, "x"))
    out_specs = (P(rows, "x"), P(rows, "x"))
    return jax.shard_map(on_device, mesh=fine, in_specs=in_specs, out_specs=out_specs, check_vma=False)
```

```python
import functools

import jax
import jax.numpy as jnp
from jax import lax
from jax.experimental import pallas as pl
from jax.experimental.pallas import tpu as pltpu
from jax.sharding import Mesh
from jax.sharding import PartitionSpec as P

NY, NZ, NC, NX = 4, 4, 2, 4
LANES = 128
CHUNK = 256
ROWS = (0, 1, 3, 2)
COLS = ((0, 0), (1, 0), (0, 1), (0, 3), (1, 1), (1, 3), (0, 2), (1, 2))

noise_level = 1.0
kernel_rate = 0.5


def shift(value, axis, size, step):
    return lax.ppermute(value, axis, [(i, (i + step) % size) for i in range(size)])


def split(value):
    high = value.astype(jnp.bfloat16)
    rest = value - high.astype(jnp.float32)
    middle = rest.astype(jnp.bfloat16)
    return high, middle, (rest - middle.astype(jnp.float32)).astype(jnp.bfloat16)


def pack_kernel(points_ref, side_ref, out_ref):
    own, width = points_ref.shape
    probes = side_ref.shape[0]
    out_ref[:own, :] = points_ref[...]
    high, middle, _ = split(points_ref[...].astype(jnp.float32) ** 2)
    ones = jnp.ones((probes, width), jnp.bfloat16)
    norms = 0.0
    for term in (high, middle):
        norms = norms + lax.dot_general(ones, term, (((1,), (1,)), ((), ())), preferred_element_type=jnp.float32)
    high, middle, low = split(norms)
    row = lax.broadcasted_iota(jnp.int32, norms.shape, 0)
    norms = jnp.where(row == 0, high.astype(jnp.float32), jnp.where(row == 1, middle.astype(jnp.float32), low.astype(jnp.float32)))
    high, middle, _ = split(side_ref[...])
    at = own
    for part in (high, middle, norms.astype(jnp.bfloat16)):
        for j in range(own // width):
            out_ref[at : at + probes, :] = part[:, j * width : (j + 1) * width]
            at += probes


def pack(points, side):
    own, width = points.shape
    extra = side.shape[0] * 3 * own // width
    return pl.pallas_call(
        pack_kernel,
        out_shape=jax.ShapeDtypeStruct((own + extra, width), jnp.bfloat16),
        compiler_params=pltpu.CompilerParams(vmem_limit_bytes=8 << 20),
        name="pack",
    )(points, side)


def unpack_side(messages, probes, own):
    terms = [jnp.concatenate([unpack_rows(one, probes, own, t) for one in messages], axis=1) for t in (0, 1)]
    return terms[0].astype(jnp.float32) + terms[1].astype(jnp.float32)


def unpack_rows(message, probes, own, term):
    width = message.shape[1]
    count = own // width
    at = own + term * count * probes
    return jnp.concatenate([message[at + j * probes : at + (j + 1) * probes] for j in range(count)], axis=1)


def tile_kernel(counts, probes, *refs):
    rows_count, cols_count, known_halves, prior_count, has_side = counts
    refs = list(refs)
    row_refs = [refs.pop(0) for _ in range(rows_count)]
    col_refs = [refs.pop(0) for _ in range(cols_count)]
    half_refs = [refs.pop(0) for _ in range(known_halves)]
    prior_refs = [refs.pop(0) for _ in range(prior_count)]
    side_ref = refs.pop(0) if has_side else None
    tile_ref, image_ref = refs.pop(0), refs.pop(0)
    own = tile_ref.shape[0] // rows_count
    if known_halves:
        pieces = []
        for half_ref in half_refs:
            pieces += [half_ref[j * own : (j + 1) * own, :] for j in range(half_ref.shape[0] // own)]
        halves = pieces
    else:
        new_ref = refs.pop(0)
        halves = []
        for i, row_ref in enumerate(row_refs):
            squares = row_ref[:own, :].astype(jnp.float32) ** 2
            halves.append(-kernel_rate * jnp.sum(squares, axis=1, keepdims=True))
            new_ref[i * own : (i + 1) * own, :] = halves[-1]
    if prior_count:
        at = 0
        for prior_ref in prior_refs:
            image_ref[:, at : at + prior_ref.shape[1]] = prior_ref[...]
            at += prior_ref.shape[1]
    else:
        image_ref[...] = jnp.zeros_like(image_ref)
        if has_side:
            image_ref[:, :own] = noise_level * side_ref[...]
    for j, col_ref in enumerate(col_refs):
        field = unpack_rows(col_ref, probes, own, 0)
        norms = unpack_rows(col_ref, probes, own, 2).astype(jnp.float32)
        col_half = -kernel_rate * (norms[0:1] + norms[1:2] + norms[2:3])
        for i, row_ref in enumerate(row_refs):
            for k in range(own // CHUNK):
                part = slice(k * CHUNK, (k + 1) * CHUNK)
                place = slice(i * own + k * CHUNK, i * own + (k + 1) * CHUNK)
                cross = lax.dot_general(
                    row_ref[part, :], col_ref[:own, :], (((1,), (1,)), ((), ())), preferred_element_type=jnp.float32
                )
                kern = jnp.exp(2.0 * kernel_rate * cross + halves[i][part, :] + col_half).astype(jnp.bfloat16)
                tile_ref[place, j * own : (j + 1) * own] = kern
                image_ref[:, place] += lax.dot_general(
                    field, kern, (((1,), (1,)), ((), ())), preferred_element_type=jnp.float32
                )


def build(rows, cols, own, probes, halves=(), prior=(), side=None):
    features = rows[0].shape[1]
    height, width = len(rows) * own, len(cols) * own
    counts = (len(rows), len(cols), len(halves), len(prior), side is not None)
    out_shape = [
        pltpu.VMEM((height, width), jnp.bfloat16),
        jax.ShapeDtypeStruct((probes, height), jnp.float32),
    ]
    if not halves:
        out_shape.append(jax.ShapeDtypeStruct((height, 1), jnp.float32))
    args = [*rows, *cols, *halves, *prior] + ([] if side is None else [side])
    return pl.pallas_call(
        functools.partial(tile_kernel, counts, probes),
        out_shape=out_shape,
        compiler_params=pltpu.CompilerParams(vmem_limit_bytes=16 << 20),
        cost_estimate=pl.CostEstimate(
            flops=height * width * features // 8, bytes_accessed=1 << 10, transcendentals=0
        ),
        name="build_tile",
    )(*args)


def combine_kernel(own, side_ref, *refs):
    parts, (image_ref, message_ref) = refs[:NZ], refs[NZ:]
    side = side_ref[...]
    sums = [0.0, 0.0, 0.0]
    for i, p in enumerate(ROWS):
        piece = 0.0
        for s in range(NZ):
            at = ROWS.index((p - s) % NZ) * own
            piece = piece + parts[s][:, at : at + own]
        here = slice(i * own, (i + 1) * own)
        image_ref[:, here] = piece
        if i == 0:
            message_ref[:, :own] = piece
        known = side[:, here]
        sums[0] = sums[0] + jnp.sum(known * known, axis=1, keepdims=True)
        sums[1] = sums[1] + jnp.sum(known * piece, axis=1, keepdims=True)
        sums[2] = sums[2] + jnp.sum(piece * piece, axis=1, keepdims=True)
    lane = lax.broadcasted_iota(jnp.int32, (side.shape[0], LANES), 1)
    message_ref[:, own:] = jnp.where(lane == 0, sums[0], jnp.where(lane == 1, sums[1], sums[2]))


def combine(side_r, parts, own):
    probes, rows = side_r.shape
    return pl.pallas_call(
        functools.partial(combine_kernel, own),
        out_shape=[
            jax.ShapeDtypeStruct((probes, rows), jnp.float32),
            jax.ShapeDtypeStruct((probes, own + LANES), jnp.float32),
        ],
        compiler_params=pltpu.CompilerParams(vmem_limit_bytes=8 << 20),
        name="combine",
    )(side_r, *parts)


def second_kernel(own, tiles, side_own, image_r, side_r, image_c, side_c, sums_ref, mine_ref, other_ref, own_ref):
    sums = sums_ref[...]
    rr, curve, square = sums[:, 0:1], sums[:, 1:2], sums[:, 2:3]
    alpha = rr / curve
    rr_next = rr - 2.0 * alpha * curve + alpha * alpha * square
    beta = rr_next / rr
    res_r = side_r[...] - alpha * image_r[...]
    dir_r = res_r + beta * side_r[...]
    narrow = dir_r.astype(jnp.bfloat16)
    total = jnp.zeros_like(alpha)
    for j, (h, m) in enumerate(COLS):
        part = 0.0
        for tile_ref, top, left in tiles:
            at = j * own - left
            if 0 <= at < tile_ref.shape[1]:
                part = part + jnp.dot(
                    narrow[:, top : top + tile_ref.shape[0]],
                    tile_ref[:, at : at + own],
                    preferred_element_type=jnp.float32,
                )
        cols = slice(j * own, (j + 1) * own)
        dir_c = (side_c[:, cols] - alpha * image_c[:, cols]) + beta * side_c[:, cols]
        total = total + jnp.sum(part * dir_c, axis=1, keepdims=True)
        (other_ref if h else mine_ref)[:, m * own : (m + 1) * own] = part
    own_res = side_own[...] - alpha * image_r[:, :own]
    own_dir = own_res + beta * side_own[...]
    own_ref[0] = own_res
    own_ref[1] = own_dir
    own_ref[2] = alpha * side_own[...]
    total = total + noise_level * jnp.sum(own_dir * own_dir, axis=1, keepdims=True)
    rr_own = jnp.sum(own_res * own_res, axis=1, keepdims=True)
    lane = lax.broadcasted_iota(jnp.int32, (total.shape[0], LANES), 1)
    out_sums = jnp.where(lane == 0, total, jnp.where(lane == 1, rr_own, 0.0))
    mine_ref[:, NY * own :] = out_sums
    other_ref[:, NY * own :] = out_sums


def second_product(tiles, side, image_r, side_r, image_c, side_c, sums, own):
    probes, rows = side_r.shape
    cols = side_c.shape[1]
    places = [(top, left) for _, top, left in tiles]

    def kernel(*refs):
        held = [(ref, top, left) for ref, (top, left) in zip(refs, places)]
        second_kernel(own, held, *refs[len(places) :])

    return pl.pallas_call(
        kernel,
        in_specs=[pl.BlockSpec(memory_space=pltpu.VMEM)] * (len(tiles) + 6),
        out_shape=[
            jax.ShapeDtypeStruct((probes, cols // NC + LANES), jnp.float32),
            jax.ShapeDtypeStruct((probes, cols // NC + LANES), jnp.float32),
            jax.ShapeDtypeStruct((3, probes, own), jnp.float32),
        ],
        compiler_params=pltpu.CompilerParams(vmem_limit_bytes=16 << 20),
        cost_estimate=pl.CostEstimate(flops=rows * cols * 32, bytes_accessed=1 << 10, transcendentals=0),
        name="second_product",
    )(*[tile for tile, _, _ in tiles], side, image_r, side_r, image_c, side_c, sums)


def on_device(states, offsets, right_side):
    own, probes = right_side.shape
    side = right_side.T
    points = lax.dynamic_slice_in_dim(states, offsets[0], own, 0)
    with jax.named_scope("fetch_points"):
        message = pack(points, side)
        middle = message.shape[0] // 2
        row, col = {0: message}, {(0, 0): message}
        for k in (1, 3):
            col[0, k] = shift(message, "y", NY, k)
            row[k] = shift(message, "z", NZ, k)
        col[1, 0] = shift(message, "c", NC, 1)
        far = []
        for axis, size, ahead, behind in (("z", NZ, row[1], row[3]), ("y", NY, col[0, 1], col[0, 3])):
            far.append((shift(ahead[:middle], axis, size, 1), shift(behind[middle:], axis, size, -1)))
        for k in (1, 3):
            col[1, k] = shift(col[0, k], "c", NC, 1)
        near = [row[k] for k in ROWS[:3]]

    with jax.named_scope("build_tiles"):
        at = [col[k] for k in COLS[:6]]
        tile_a, image, half = build(near, at[:2], own, probes, side=side)
        tile_b, image = build(near, at[2:4], own, probes, [half], [image])
        tile_c, image = build(near, at[4:6], own, probes, [half], [image])
        far, image = lax.optimization_barrier((far, image))
        row[2] = jnp.concatenate(far[0], axis=0)
        col[0, 2] = jnp.concatenate(far[1], axis=0)
        col[1, 2] = shift(col[0, 2], "c", NC, 1)
        tile_d, image_far, half_far = build([row[2]], at, own, probes)
        at = [col[0, 2], col[1, 2]]
        tile_e, image = build(near + [row[2]], at, own, probes, [half, half_far], [image, image_far])
        tiles = [
            (tile_a, 0, 0),
            (tile_b, 0, 2 * own),
            (tile_c, 0, 4 * own),
            (tile_d, 3 * own, 0),
            (tile_e, 0, 6 * own),
        ]
        side_c = unpack_side([col[at] for at in COLS], probes, own)
        side_r = unpack_side([row[k] for k in ROWS], probes, own)

    with jax.named_scope("sum_over_z"):
        parts = [image] + [None] * (NZ - 1)
        for s in (1, 3, 2):
            parts[s] = shift(image, "z", NZ, s)
        image_r, message = combine(side_r, parts, own)

    with jax.named_scope("gather_image"):
        pair = jnp.concatenate([message, shift(message, "c", NC, 1)], axis=0)
        every = {0: pair}
        for m in (1, 3, 2):
            every[m] = shift(pair, "y", NY, m)
        image_c = jnp.concatenate([every[m][h * probes : (h + 1) * probes, :own] for h, m in COLS], axis=1)
        sums = sum(every[m][h * probes : (h + 1) * probes, own:] for h, m in COLS)

    mine, other, held = second_product(tiles, side, image_r, side_r, image_c, side_c, sums, own)

    with jax.named_scope("sum_over_yc"):
        mine = mine + shift(other, "c", NC, 1)
        image = mine[:, :own]
        sums = mine[:, NY * own :]
        total = sums
        for m in (1, 3, 2):
            message = jnp.concatenate([mine[:, m * own : (m + 1) * own], sums], axis=1)
            message = shift(message, "y", NY, -m)
            image = image + message[:, :own]
            total = total + message[:, own:]

    with jax.named_scope("sum_sums_over_z"):
        sums = total
        for k in (1, 3, 2):
            total = total + shift(sums, "z", NZ, k)

    alpha = total[:, 1:2] / total[:, 0:1]
    residual, direction, field = held[0], held[1], held[2]
    image = image + noise_level * direction
    field = field + alpha * direction
    residual = residual - alpha * image
    return field.T, residual.T


def solution(mesh):
    fine = Mesh(mesh.devices.reshape(NY, NZ, NC, NX), ("y", "z", "c", "x"))
    rows = ("y", "z", "c")
    in_specs = (P(rows, None), P(rows), P(rows, "x"))
    out_specs = (P(rows, "x"), P(rows, "x"))
    return jax.shard_map(on_device, mesh=fine, in_specs=in_specs, out_specs=out_specs, check_vma=False)
```

```python
import functools

import jax
import jax.numpy as jnp
from jax import lax
from jax.experimental import pallas as pl
from jax.experimental.pallas import tpu as pltpu
from jax.sharding import Mesh
from jax.sharding import PartitionSpec as P

NY, NZ, NC, NX = 4, 4, 2, 4
LANES = 128
CHUNK = 256
ROWS = (0, 1, 3, 2)
COLS = ((0, 0), (1, 0), (0, 1), (0, 3), (1, 1), (1, 3), (0, 2), (1, 2))

noise_level = 1.0
kernel_rate = 0.5


def shift(value, axis, size, step):
    return lax.ppermute(value, axis, [(i, (i + step) % size) for i in range(size)])


def split(value):
    high = value.astype(jnp.bfloat16)
    rest = value - high.astype(jnp.float32)
    middle = rest.astype(jnp.bfloat16)
    return high, middle, (rest - middle.astype(jnp.float32)).astype(jnp.bfloat16)


def pack_kernel(points_ref, side_ref, out_ref):
    own, width = points_ref.shape
    probes = side_ref.shape[0]
    out_ref[:own, :] = points_ref[...]
    high, middle, _ = split(points_ref[...].astype(jnp.float32) ** 2)
    ones = jnp.ones((probes, width), jnp.bfloat16)
    norms = 0.0
    for term in (high, middle):
        norms = norms + lax.dot_general(ones, term, (((1,), (1,)), ((), ())), preferred_element_type=jnp.float32)
    high, middle, low = split(norms)
    row = lax.broadcasted_iota(jnp.int32, norms.shape, 0)
    norms = jnp.where(row == 0, high.astype(jnp.float32), jnp.where(row == 1, middle.astype(jnp.float32), low.astype(jnp.float32)))
    high, middle, _ = split(side_ref[...])
    at = own
    for part in (high, middle, norms.astype(jnp.bfloat16)):
        for j in range(own // width):
            out_ref[at : at + probes, :] = part[:, j * width : (j + 1) * width]
            at += probes


def pack(points, side):
    own, width = points.shape
    extra = side.shape[0] * 3 * own // width
    return pl.pallas_call(
        pack_kernel,
        out_shape=jax.ShapeDtypeStruct((own + extra, width), jnp.bfloat16),
        compiler_params=pltpu.CompilerParams(vmem_limit_bytes=8 << 20),
        name="pack",
    )(points, side)


def unpack_side(messages, probes, own):
    terms = [jnp.concatenate([unpack_rows(one, probes, own, t) for one in messages], axis=1) for t in (0, 1)]
    return terms[0].astype(jnp.float32) + terms[1].astype(jnp.float32)


def unpack_rows(message, probes, own, term):
    width = message.shape[1]
    count = own // width
    at = own + term * count * probes
    return jnp.concatenate([message[at + j * probes : at + (j + 1) * probes] for j in range(count)], axis=1)


def tile_kernel(counts, probes, *refs):
    rows_count, cols_count, known_halves, prior_count, has_side = counts
    refs = list(refs)
    row_refs = [refs.pop(0) for _ in range(rows_count)]
    col_refs = [refs.pop(0) for _ in range(cols_count)]
    half_refs = [refs.pop(0) for _ in range(known_halves)]
    prior_refs = [refs.pop(0) for _ in range(prior_count)]
    side_ref = refs.pop(0) if has_side else None
    tile_ref, image_ref = refs.pop(0), refs.pop(0)
    own = tile_ref.shape[0] // rows_count
    if known_halves:
        pieces = []
        for half_ref in half_refs:
            pieces += [half_ref[j * own : (j + 1) * own, :] for j in range(half_ref.shape[0] // own)]
        halves = pieces
    else:
        new_ref = refs.pop(0)
        halves = []
        for i, row_ref in enumerate(row_refs):
            squares = row_ref[:own, :].astype(jnp.float32) ** 2
            halves.append(-kernel_rate * jnp.sum(squares, axis=1, keepdims=True))
            new_ref[i * own : (i + 1) * own, :] = halves[-1]
    if prior_count:
        at = 0
        for prior_ref in prior_refs:
            image_ref[:, at : at + prior_ref.shape[1]] = prior_ref[...]
            at += prior_ref.shape[1]
    else:
        image_ref[...] = jnp.zeros_like(image_ref)
        if has_side:
            image_ref[:, :own] = noise_level * side_ref[...]
    for j, col_ref in enumerate(col_refs):
        field = unpack_rows(col_ref, probes, own, 0)
        norms = unpack_rows(col_ref, probes, own, 2).astype(jnp.float32)
        col_half = -kernel_rate * (norms[0:1] + norms[1:2] + norms[2:3])
        for i, row_ref in enumerate(row_refs):
            for k in range(own // CHUNK):
                part = slice(k * CHUNK, (k + 1) * CHUNK)
                place = slice(i * own + k * CHUNK, i * own + (k + 1) * CHUNK)
                cross = lax.dot_general(
                    row_ref[part, :], col_ref[:own, :], (((1,), (1,)), ((), ())), preferred_element_type=jnp.float32
                )
                kern = jnp.exp(2.0 * kernel_rate * cross + halves[i][part, :] + col_half).astype(jnp.bfloat16)
                tile_ref[place, j * own : (j + 1) * own] = kern
                image_ref[:, place] += lax.dot_general(
                    field, kern, (((1,), (1,)), ((), ())), preferred_element_type=jnp.float32
                )


def build(rows, cols, own, probes, halves=(), prior=(), side=None):
    features = rows[0].shape[1]
    height, width = len(rows) * own, len(cols) * own
    counts = (len(rows), len(cols), len(halves), len(prior), side is not None)
    out_shape = [
        pltpu.VMEM((height, width), jnp.bfloat16),
        jax.ShapeDtypeStruct((probes, height), jnp.float32),
    ]
    if not halves:
        out_shape.append(jax.ShapeDtypeStruct((height, 1), jnp.float32))
    args = [*rows, *cols, *halves, *prior] + ([] if side is None else [side])
    return pl.pallas_call(
        functools.partial(tile_kernel, counts, probes),
        out_shape=out_shape,
        compiler_params=pltpu.CompilerParams(vmem_limit_bytes=16 << 20),
        cost_estimate=pl.CostEstimate(
            flops=height * width * features // 8, bytes_accessed=1 << 10, transcendentals=0
        ),
        name="build_tile",
    )(*args)


def combine_kernel(own, side_ref, *refs):
    parts, (image_ref, message_ref) = refs[:NZ], refs[NZ:]
    side = side_ref[...]
    sums = [0.0, 0.0, 0.0]
    for i, p in enumerate(ROWS):
        piece = 0.0
        for s in range(NZ):
            at = ROWS.index((p - s) % NZ) * own
            piece = piece + parts[s][:, at : at + own]
        here = slice(i * own, (i + 1) * own)
        image_ref[:, here] = piece
        if i == 0:
            message_ref[:, :own] = piece
        known = side[:, here]
        sums[0] = sums[0] + jnp.sum(known * known, axis=1, keepdims=True)
        sums[1] = sums[1] + jnp.sum(known * piece, axis=1, keepdims=True)
        sums[2] = sums[2] + jnp.sum(piece * piece, axis=1, keepdims=True)
    lane = lax.broadcasted_iota(jnp.int32, (side.shape[0], LANES), 1)
    message_ref[:, own:] = jnp.where(lane == 0, sums[0], jnp.where(lane == 1, sums[1], sums[2]))


def combine(side_r, parts, own):
    probes, rows = side_r.shape
    return pl.pallas_call(
        functools.partial(combine_kernel, own),
        out_shape=[
            jax.ShapeDtypeStruct((probes, rows), jnp.float32),
            jax.ShapeDtypeStruct((probes, own + LANES), jnp.float32),
        ],
        compiler_params=pltpu.CompilerParams(vmem_limit_bytes=8 << 20),
        name="combine",
    )(side_r, *parts)


def second_kernel(own, tiles, side_own, image_r, side_r, image_c, side_c, sums_ref, mine_ref, other_ref, own_ref):
    sums = sums_ref[...]
    rr, curve, square = sums[:, 0:1], sums[:, 1:2], sums[:, 2:3]
    alpha = rr / curve
    rr_next = rr - 2.0 * alpha * curve + alpha * alpha * square
    beta = rr_next / rr
    res_r = side_r[...] - alpha * image_r[...]
    dir_r = res_r + beta * side_r[...]
    narrow = dir_r.astype(jnp.bfloat16)
    total = jnp.zeros_like(alpha)
    for j, (h, m) in enumerate(COLS):
        part = 0.0
        for tile_ref, top, left in tiles:
            at = j * own - left
            if 0 <= at < tile_ref.shape[1]:
                part = part + jnp.dot(
                    narrow[:, top : top + tile_ref.shape[0]],
                    tile_ref[:, at : at + own],
                    preferred_element_type=jnp.float32,
                )
        cols = slice(j * own, (j + 1) * own)
        dir_c = (side_c[:, cols] - alpha * image_c[:, cols]) + beta * side_c[:, cols]
        total = total + jnp.sum(part * dir_c, axis=1, keepdims=True)
        (other_ref if h else mine_ref)[:, m * own : (m + 1) * own] = part
    own_res = side_own[...] - alpha * image_r[:, :own]
    own_dir = own_res + beta * side_own[...]
    own_ref[0] = own_res
    own_ref[1] = own_dir
    own_ref[2] = alpha * side_own[...]
    total = total + noise_level * jnp.sum(own_dir * own_dir, axis=1, keepdims=True)
    rr_own = jnp.sum(own_res * own_res, axis=1, keepdims=True)
    lane = lax.broadcasted_iota(jnp.int32, (total.shape[0], LANES), 1)
    out_sums = jnp.where(lane == 0, total, jnp.where(lane == 1, rr_own, 0.0))
    mine_ref[:, NY * own :] = out_sums
    other_ref[:, NY * own :] = out_sums


def second_product(tiles, side, image_r, side_r, image_c, side_c, sums, own):
    probes, rows = side_r.shape
    cols = side_c.shape[1]
    places = [(top, left) for _, top, left in tiles]

    def kernel(*refs):
        held = [(ref, top, left) for ref, (top, left) in zip(refs, places)]
        second_kernel(own, held, *refs[len(places) :])

    return pl.pallas_call(
        kernel,
        in_specs=[pl.BlockSpec(memory_space=pltpu.VMEM)] * (len(tiles) + 6),
        out_shape=[
            jax.ShapeDtypeStruct((probes, cols // NC + LANES), jnp.float32),
            jax.ShapeDtypeStruct((probes, cols // NC + LANES), jnp.float32),
            jax.ShapeDtypeStruct((3, probes, own), jnp.float32),
        ],
        compiler_params=pltpu.CompilerParams(vmem_limit_bytes=16 << 20),
        cost_estimate=pl.CostEstimate(flops=rows * cols * 32, bytes_accessed=1 << 10, transcendentals=0),
        name="second_product",
    )(*[tile for tile, _, _ in tiles], side, image_r, side_r, image_c, side_c, sums)


def on_device(states, offsets, right_side):
    own, probes = right_side.shape
    side = right_side.T
    points = lax.dynamic_slice_in_dim(states, offsets[0], own, 0)
    with jax.named_scope("fetch_points"):
        message = pack(points, side)
        middle = message.shape[0] // 2
        row, col = {0: message}, {(0, 0): message}
        for k in (1, 3):
            row[k] = shift(message, "z", NZ, k)
        col[1, 0] = shift(message, "c", NC, 1)
        for k in (1, 3):
            col[0, k] = shift(message, "y", NY, k)
        near = [row[k] for k in ROWS[:3]]

    with jax.named_scope("build_tiles"):
        at = [col[0, 0], col[1, 0]]
        tile_a, image, half = build(near, at, own, probes, side=side)
        ring = {"z": (row[1], row[3]), "y": (col[0, 1], col[0, 3])}
        ring, image = lax.optimization_barrier((ring, image))
        far = {}
        for axis, size in (("z", NZ), ("y", NY)):
            ahead, behind = ring[axis]
            far[axis] = shift(ahead[:middle], axis, size, 1), shift(behind[middle:], axis, size, -1)
        tile_b, image = build(near, [ring["y"][0]], own, probes, [half], [image])
        other, image = lax.optimization_barrier((ring["y"][0], image))
        col[1, 1] = shift(other, "c", NC, 1)
        tile_c, image = build(near, [ring["y"][1]], own, probes, [half], [image])
        other, image = lax.optimization_barrier((ring["y"][1], image))
        col[1, 3] = shift(other, "c", NC, 1)
        tile_d, image = build(near, [col[1, 1]], own, probes, [half], [image])
        tile_e, image = build(near, [col[1, 3]], own, probes, [half], [image])
        far, image = lax.optimization_barrier((far, image))
        row[2] = jnp.concatenate(far["z"], axis=0)
        col[0, 2] = jnp.concatenate(far["y"], axis=0)
        col[1, 2] = shift(col[0, 2], "c", NC, 1)
        at = [col[k] for k in COLS[:6]]
        tile_f, image_far, half_far = build([row[2]], at, own, probes)
        at = [col[0, 2], col[1, 2]]
        tile_g, image = build(near + [row[2]], at, own, probes, [half, half_far], [image, image_far])
        tiles = [
            (tile_a, 0, 0),
            (tile_b, 0, 2 * own),
            (tile_c, 0, 3 * own),
            (tile_d, 0, 4 * own),
            (tile_e, 0, 5 * own),
            (tile_f, 3 * own, 0),
            (tile_g, 0, 6 * own),
        ]
        side_c = unpack_side([col[at] for at in COLS], probes, own)
        side_r = unpack_side([row[k] for k in ROWS], probes, own)

    with jax.named_scope("sum_over_z"):
        parts = [image] + [None] * (NZ - 1)
        for s in (1, 3, 2):
            parts[s] = shift(image, "z", NZ, s)
        image_r, message = combine(side_r, parts, own)

    with jax.named_scope("gather_image"):
        every = {0: message}
        for m in (1, 3, 2):
            every[m] = shift(message, "y", NY, m)
        line = jnp.concatenate([every[m] for m in range(NY)], axis=1)
        pair = line, shift(line, "c", NC, 1)
        width = own + LANES
        image_c = jnp.concatenate([pair[h][:, m * width : m * width + own] for h, m in COLS], axis=1)
        sums = sum(pair[h][:, m * width + own : (m + 1) * width] for h, m in COLS)

    mine, other, held = second_product(tiles, side, image_r, side_r, image_c, side_c, sums, own)

    with jax.named_scope("sum_over_yc"):
        mine = mine + shift(other, "c", NC, 1)
        image = mine[:, :own]
        sums = mine[:, NY * own :]
        total = sums
        for m in (1, 3, 2):
            message = jnp.concatenate([mine[:, m * own : (m + 1) * own], sums], axis=1)
            message = shift(message, "y", NY, -m)
            image = image + message[:, :own]
            total = total + message[:, own:]

    with jax.named_scope("sum_sums_over_z"):
        sums = total
        for k in (1, 3, 2):
            total = total + shift(sums, "z", NZ, k)

    alpha = total[:, 1:2] / total[:, 0:1]
    residual, direction, field = held[0], held[1], held[2]
    image = image + noise_level * direction
    field = field + alpha * direction
    residual = residual - alpha * image
    return field.T, residual.T


def solution(mesh):
    fine = Mesh(mesh.devices.reshape(NY, NZ, NC, NX), ("y", "z", "c", "x"))
    rows = ("y", "z", "c")
    in_specs = (P(rows, None), P(rows), P(rows, "x"))
    out_specs = (P(rows, "x"), P(rows, "x"))
    return jax.shard_map(on_device, mesh=fine, in_specs=in_specs, out_specs=out_specs, check_vma=False)
```

```python
import functools

import jax
import jax.numpy as jnp
from jax import lax
from jax.experimental import pallas as pl
from jax.experimental.pallas import tpu as pltpu
from jax.sharding import Mesh
from jax.sharding import PartitionSpec as P

NY, NZ, NC, NX = 4, 4, 2, 4
LANES = 128
CHUNK = 256
ROWS = (0, 1, 3, 2)
COLS = ((0, 0), (1, 0), (0, 1), (0, 3), (1, 1), (1, 3), (0, 2), (1, 2))

noise_level = 1.0
kernel_rate = 0.5


def shift(value, axis, size, step):
    return lax.ppermute(value, axis, [(i, (i + step) % size) for i in range(size)])


def split(value):
    high = value.astype(jnp.bfloat16)
    rest = value - high.astype(jnp.float32)
    middle = rest.astype(jnp.bfloat16)
    return high, middle, (rest - middle.astype(jnp.float32)).astype(jnp.bfloat16)


def pack_kernel(points_ref, side_ref, out_ref):
    own, width = points_ref.shape
    probes = side_ref.shape[0]
    out_ref[:own, :] = points_ref[...]
    high, middle, _ = split(points_ref[...].astype(jnp.float32) ** 2)
    ones = jnp.ones((probes, width), jnp.bfloat16)
    norms = 0.0
    for term in (high, middle):
        norms = norms + lax.dot_general(ones, term, (((1,), (1,)), ((), ())), preferred_element_type=jnp.float32)
    high, middle, low = split(norms)
    row = lax.broadcasted_iota(jnp.int32, norms.shape, 0)
    norms = jnp.where(row == 0, high.astype(jnp.float32), jnp.where(row == 1, middle.astype(jnp.float32), low.astype(jnp.float32)))
    high, middle, _ = split(side_ref[...])
    at = own
    for part in (high, middle, norms.astype(jnp.bfloat16)):
        for j in range(own // width):
            out_ref[at : at + probes, :] = part[:, j * width : (j + 1) * width]
            at += probes


def pack(points, side):
    own, width = points.shape
    extra = side.shape[0] * 3 * own // width
    return pl.pallas_call(
        pack_kernel,
        out_shape=jax.ShapeDtypeStruct((own + extra, width), jnp.bfloat16),
        compiler_params=pltpu.CompilerParams(vmem_limit_bytes=8 << 20),
        name="pack",
    )(points, side)


def unpack_side(messages, probes, own):
    terms = [jnp.concatenate([unpack_rows(one, probes, own, t) for one in messages], axis=1) for t in (0, 1)]
    return terms[0].astype(jnp.float32) + terms[1].astype(jnp.float32)


def unpack_rows(message, probes, own, term):
    width = message.shape[1]
    count = own // width
    at = own + term * count * probes
    return jnp.concatenate([message[at + j * probes : at + (j + 1) * probes] for j in range(count)], axis=1)


def tile_kernel(counts, probes, *refs):
    rows_count, cols_count, known_halves, prior_count, has_side = counts
    refs = list(refs)
    row_refs = [refs.pop(0) for _ in range(rows_count)]
    col_refs = [refs.pop(0) for _ in range(cols_count)]
    half_refs = [refs.pop(0) for _ in range(known_halves)]
    prior_refs = [refs.pop(0) for _ in range(prior_count)]
    side_ref = refs.pop(0) if has_side else None
    tile_ref, image_ref = refs.pop(0), refs.pop(0)
    own = tile_ref.shape[0] // rows_count
    if known_halves:
        pieces = []
        for half_ref in half_refs:
            pieces += [half_ref[j * own : (j + 1) * own, :] for j in range(half_ref.shape[0] // own)]
        halves = pieces
    else:
        new_ref = refs.pop(0)
        halves = []
        for i, row_ref in enumerate(row_refs):
            squares = row_ref[:own, :].astype(jnp.float32) ** 2
            halves.append(-kernel_rate * jnp.sum(squares, axis=1, keepdims=True))
            new_ref[i * own : (i + 1) * own, :] = halves[-1]
    if prior_count:
        at = 0
        for prior_ref in prior_refs:
            image_ref[:, at : at + prior_ref.shape[1]] = prior_ref[...]
            at += prior_ref.shape[1]
    else:
        image_ref[...] = jnp.zeros_like(image_ref)
        if has_side:
            image_ref[:, :own] = noise_level * side_ref[...]
    for j, col_ref in enumerate(col_refs):
        field = unpack_rows(col_ref, probes, own, 0)
        norms = unpack_rows(col_ref, probes, own, 2).astype(jnp.float32)
        col_half = -kernel_rate * (norms[0:1] + norms[1:2] + norms[2:3])
        for i, row_ref in enumerate(row_refs):
            for k in range(own // CHUNK):
                part = slice(k * CHUNK, (k + 1) * CHUNK)
                place = slice(i * own + k * CHUNK, i * own + (k + 1) * CHUNK)
                cross = lax.dot_general(
                    row_ref[part, :], col_ref[:own, :], (((1,), (1,)), ((), ())), preferred_element_type=jnp.float32
                )
                kern = jnp.exp(2.0 * kernel_rate * cross + halves[i][part, :] + col_half).astype(jnp.bfloat16)
                tile_ref[place, j * own : (j + 1) * own] = kern
                image_ref[:, place] += lax.dot_general(
                    field, kern, (((1,), (1,)), ((), ())), preferred_element_type=jnp.float32
                )


def build(rows, cols, own, probes, halves=(), prior=(), side=None):
    features = rows[0].shape[1]
    height, width = len(rows) * own, len(cols) * own
    counts = (len(rows), len(cols), len(halves), len(prior), side is not None)
    out_shape = [
        pltpu.VMEM((height, width), jnp.bfloat16),
        jax.ShapeDtypeStruct((probes, height), jnp.float32),
    ]
    if not halves:
        out_shape.append(jax.ShapeDtypeStruct((height, 1), jnp.float32))
    args = [*rows, *cols, *halves, *prior] + ([] if side is None else [side])
    return pl.pallas_call(
        functools.partial(tile_kernel, counts, probes),
        out_shape=out_shape,
        compiler_params=pltpu.CompilerParams(vmem_limit_bytes=16 << 20),
        cost_estimate=pl.CostEstimate(
            flops=height * width * features // 8, bytes_accessed=1 << 10, transcendentals=0
        ),
        name="build_tile",
    )(*args)


def combine_kernel(own, side_ref, *refs):
    parts, (image_ref, message_ref) = refs[:NZ], refs[NZ:]
    side = side_ref[...]
    sums = [0.0, 0.0, 0.0]
    for i, p in enumerate(ROWS):
        piece = 0.0
        for s in range(NZ):
            at = ROWS.index((p - s) % NZ) * own
            piece = piece + parts[s][:, at : at + own]
        here = slice(i * own, (i + 1) * own)
        image_ref[:, here] = piece
        if i == 0:
            message_ref[:, :own] = piece
        known = side[:, here]
        sums[0] = sums[0] + jnp.sum(known * known, axis=1, keepdims=True)
        sums[1] = sums[1] + jnp.sum(known * piece, axis=1, keepdims=True)
        sums[2] = sums[2] + jnp.sum(piece * piece, axis=1, keepdims=True)
    lane = lax.broadcasted_iota(jnp.int32, (side.shape[0], LANES), 1)
    message_ref[:, own:] = jnp.where(lane == 0, sums[0], jnp.where(lane == 1, sums[1], sums[2]))


def combine(side_r, parts, own):
    probes, rows = side_r.shape
    return pl.pallas_call(
        functools.partial(combine_kernel, own),
        out_shape=[
            jax.ShapeDtypeStruct((probes, rows), jnp.float32),
            jax.ShapeDtypeStruct((probes, own + LANES), jnp.float32),
        ],
        compiler_params=pltpu.CompilerParams(vmem_limit_bytes=8 << 20),
        name="combine",
    )(side_r, *parts)


def second_kernel(own, tiles, side_own, image_r, side_r, image_c, side_c, sums_ref, mine_ref, other_ref, own_ref):
    sums = sums_ref[...]
    rr, curve, square = sums[:, 0:1], sums[:, 1:2], sums[:, 2:3]
    alpha = rr / curve
    rr_next = rr - 2.0 * alpha * curve + alpha * alpha * square
    beta = rr_next / rr
    res_r = side_r[...] - alpha * image_r[...]
    dir_r = res_r + beta * side_r[...]
    narrow = dir_r.astype(jnp.bfloat16)
    total = jnp.zeros_like(alpha)
    for j, (h, m) in enumerate(COLS):
        part = 0.0
        for tile_ref, top, left in tiles:
            at = j * own - left
            if 0 <= at < tile_ref.shape[1]:
                part = part + jnp.dot(
                    narrow[:, top : top + tile_ref.shape[0]],
                    tile_ref[:, at : at + own],
                    preferred_element_type=jnp.float32,
                )
        cols = slice(j * own, (j + 1) * own)
        dir_c = (side_c[:, cols] - alpha * image_c[:, cols]) + beta * side_c[:, cols]
        total = total + jnp.sum(part * dir_c, axis=1, keepdims=True)
        (other_ref if h else mine_ref)[:, m * own : (m + 1) * own] = part
    own_res = side_own[...] - alpha * image_r[:, :own]
    own_dir = own_res + beta * side_own[...]
    own_ref[0] = own_res
    own_ref[1] = own_dir
    own_ref[2] = alpha * side_own[...]
    total = total + noise_level * jnp.sum(own_dir * own_dir, axis=1, keepdims=True)
    rr_own = jnp.sum(own_res * own_res, axis=1, keepdims=True)
    lane = lax.broadcasted_iota(jnp.int32, (total.shape[0], LANES), 1)
    out_sums = jnp.where(lane == 0, total, jnp.where(lane == 1, rr_own, 0.0))
    mine_ref[:, NY * own :] = out_sums
    other_ref[:, NY * own :] = out_sums


def second_product(tiles, side, image_r, side_r, image_c, side_c, sums, own):
    probes, rows = side_r.shape
    cols = side_c.shape[1]
    places = [(top, left) for _, top, left in tiles]

    def kernel(*refs):
        held = [(ref, top, left) for ref, (top, left) in zip(refs, places)]
        second_kernel(own, held, *refs[len(places) :])

    return pl.pallas_call(
        kernel,
        in_specs=[pl.BlockSpec(memory_space=pltpu.VMEM)] * (len(tiles) + 6),
        out_shape=[
            jax.ShapeDtypeStruct((probes, cols // NC + LANES), jnp.float32),
            jax.ShapeDtypeStruct((probes, cols // NC + LANES), jnp.float32),
            jax.ShapeDtypeStruct((3, probes, own), jnp.float32),
        ],
        compiler_params=pltpu.CompilerParams(vmem_limit_bytes=16 << 20),
        cost_estimate=pl.CostEstimate(flops=rows * cols * 32, bytes_accessed=1 << 10, transcendentals=0),
        name="second_product",
    )(*[tile for tile, _, _ in tiles], side, image_r, side_r, image_c, side_c, sums)


def on_device(states, offsets, right_side):
    own, probes = right_side.shape
    side = right_side.T
    points = lax.dynamic_slice_in_dim(states, offsets[0], own, 0)
    with jax.named_scope("fetch_points"):
        message = pack(points, side)
        middle = message.shape[0] // 2
        row, col = {0: message}, {(0, 0): message}
        for k in (1, 3):
            col[0, k] = shift(message, "y", NY, k)
            row[k] = shift(message, "z", NZ, k)
        col[1, 0] = shift(message, "c", NC, 1)
        far = []
        for axis, size, ahead, behind in (("z", NZ, row[1], row[3]), ("y", NY, col[0, 1], col[0, 3])):
            far.append((shift(ahead[:middle], axis, size, 1), shift(behind[middle:], axis, size, -1)))
        pair = shift(jnp.concatenate([col[0, 1], col[0, 3]], axis=0), "c", NC, 1)
        col[1, 1], col[1, 3] = pair[: 2 * middle], pair[2 * middle :]
        near = [row[k] for k in ROWS[:3]]

    with jax.named_scope("build_tiles"):
        at = [col[k] for k in COLS[:6]]
        tile_a, image, half = build(near, at[:2], own, probes, side=side)
        tile_b, image = build(near, at[2:4], own, probes, [half], [image])
        tile_c, image = build(near, at[4:6], own, probes, [half], [image])
        far, image = lax.optimization_barrier((far, image))
        row[2] = jnp.concatenate(far[0], axis=0)
        col[0, 2] = jnp.concatenate(far[1], axis=0)
        col[1, 2] = shift(col[0, 2], "c", NC, 1)
        tile_d, image_far, half_far = build([row[2]], at, own, probes)
        at = [col[0, 2], col[1, 2]]
        tile_e, image = build(near + [row[2]], at, own, probes, [half, half_far], [image, image_far])
        tiles = [
            (tile_a, 0, 0),
            (tile_b, 0, 2 * own),
            (tile_c, 0, 4 * own),
            (tile_d, 3 * own, 0),
            (tile_e, 0, 6 * own),
        ]
        side_c = unpack_side([col[at] for at in COLS], probes, own)
        side_r = unpack_side([row[k] for k in ROWS], probes, own)

    with jax.named_scope("sum_over_z"):
        parts = [image] + [None] * (NZ - 1)
        for s in (1, 3, 2):
            parts[s] = shift(image, "z", NZ, s)
        image_r, message = combine(side_r, parts, own)

    with jax.named_scope("gather_image"):
        pair = jnp.concatenate([message, shift(message, "c", NC, 1)], axis=0)
        every = {0: pair}
        for m in (1, 3, 2):
            every[m] = shift(pair, "y", NY, m)
        image_c = jnp.concatenate([every[m][h * probes : (h + 1) * probes, :own] for h, m in COLS], axis=1)
        sums = sum(every[m][h * probes : (h + 1) * probes, own:] for h, m in COLS)

    mine, other, held = second_product(tiles, side, image_r, side_r, image_c, side_c, sums, own)

    with jax.named_scope("sum_over_yc"):
        mine = mine + shift(other, "c", NC, 1)
        image = mine[:, :own]
        sums = mine[:, NY * own :]
        total = sums
        for m in (1, 3, 2):
            message = jnp.concatenate([mine[:, m * own : (m + 1) * own], sums], axis=1)
            message = shift(message, "y", NY, -m)
            image = image + message[:, :own]
            total = total + message[:, own:]

    with jax.named_scope("sum_sums_over_z"):
        sums = total
        for k in (1, 3, 2):
            total = total + shift(sums, "z", NZ, k)

    alpha = total[:, 1:2] / total[:, 0:1]
    residual, direction, field = held[0], held[1], held[2]
    image = image + noise_level * direction
    field = field + alpha * direction
    residual = residual - alpha * image
    return field.T, residual.T


def solution(mesh):
    fine = Mesh(mesh.devices.reshape(NY, NZ, NC, NX), ("y", "z", "c", "x"))
    rows = ("y", "z", "c")
    in_specs = (P(rows, None), P(rows), P(rows, "x"))
    out_specs = (P(rows, "x"), P(rows, "x"))
    return jax.shard_map(on_device, mesh=fine, in_specs=in_specs, out_specs=out_specs, check_vma=False)
```

```python
import functools

import jax
import jax.numpy as jnp
from jax import lax
from jax.experimental import pallas as pl
from jax.experimental.pallas import tpu as pltpu
from jax.sharding import Mesh
from jax.sharding import PartitionSpec as P

NY, NZ, NC, NX = 4, 4, 2, 4
LANES = 128
CHUNK = 256
ROWS = (0, 1, 3, 2)
COLS = ((0, 0), (1, 0), (0, 1), (0, 3), (1, 1), (1, 3), (0, 2), (1, 2))

noise_level = 1.0
kernel_rate = 0.5
STEP = 1.0 / (1.0 + noise_level)


def shift(value, axis, size, step):
    return lax.ppermute(value, axis, [(i, (i + step) % size) for i in range(size)])


def split(value):
    high = value.astype(jnp.bfloat16)
    rest = value - high.astype(jnp.float32)
    middle = rest.astype(jnp.bfloat16)
    return high, middle, (rest - middle.astype(jnp.float32)).astype(jnp.bfloat16)


def pack_kernel(points_ref, side_ref, out_ref):
    own, width = points_ref.shape
    probes = side_ref.shape[0]
    out_ref[:own, :] = points_ref[...]
    high, middle, _ = split(points_ref[...].astype(jnp.float32) ** 2)
    ones = jnp.ones((probes, width), jnp.bfloat16)
    norms = 0.0
    for term in (high, middle):
        norms = norms + lax.dot_general(ones, term, (((1,), (1,)), ((), ())), preferred_element_type=jnp.float32)
    high, middle, low = split(norms)
    row = lax.broadcasted_iota(jnp.int32, norms.shape, 0)
    norms = jnp.where(row == 0, high.astype(jnp.float32), jnp.where(row == 1, middle.astype(jnp.float32), low.astype(jnp.float32)))
    at = own
    for part in (side_ref[...].astype(jnp.bfloat16), norms.astype(jnp.bfloat16)):
        for j in range(own // width):
            out_ref[at : at + probes, :] = part[:, j * width : (j + 1) * width]
            at += probes


def pack(points, side):
    own, width = points.shape
    extra = side.shape[0] * 2 * own // width
    return pl.pallas_call(
        pack_kernel,
        out_shape=jax.ShapeDtypeStruct((own + extra, width), jnp.bfloat16),
        compiler_params=pltpu.CompilerParams(vmem_limit_bytes=8 << 20),
        name="pack",
    )(points, side)


def unpack_rows(message, probes, own, term):
    width = message.shape[1]
    count = own // width
    at = own + term * count * probes
    return jnp.concatenate([message[at + j * probes : at + (j + 1) * probes] for j in range(count)], axis=1)


def tile_kernel(counts, probes, *refs):
    rows_count, cols_count, known_halves, prior_count, has_side = counts
    refs = list(refs)
    row_refs = [refs.pop(0) for _ in range(rows_count)]
    col_refs = [refs.pop(0) for _ in range(cols_count)]
    half_refs = [refs.pop(0) for _ in range(known_halves)]
    prior_refs = [refs.pop(0) for _ in range(prior_count)]
    side_ref = refs.pop(0) if has_side else None
    tile_ref, image_ref = refs.pop(0), refs.pop(0)
    own = tile_ref.shape[0] // rows_count
    if known_halves:
        pieces = []
        for half_ref in half_refs:
            pieces += [half_ref[j * own : (j + 1) * own, :] for j in range(half_ref.shape[0] // own)]
        halves = pieces
    else:
        new_ref = refs.pop(0)
        halves = []
        for i, row_ref in enumerate(row_refs):
            squares = row_ref[:own, :].astype(jnp.float32) ** 2
            halves.append(-kernel_rate * jnp.sum(squares, axis=1, keepdims=True))
            new_ref[i * own : (i + 1) * own, :] = halves[-1]
    if prior_count:
        at = 0
        for prior_ref in prior_refs:
            image_ref[:, at : at + prior_ref.shape[1]] = prior_ref[...]
            at += prior_ref.shape[1]
    else:
        image_ref[...] = jnp.zeros_like(image_ref)
        if has_side:
            image_ref[:, :own] = (noise_level - 1.0 / STEP) * side_ref[...]
    for j, col_ref in enumerate(col_refs):
        field = unpack_rows(col_ref, probes, own, 0)
        norms = unpack_rows(col_ref, probes, own, 1).astype(jnp.float32)
        col_half = -kernel_rate * (norms[0:1] + norms[1:2] + norms[2:3])
        for i, row_ref in enumerate(row_refs):
            for k in range(own // CHUNK):
                part = slice(k * CHUNK, (k + 1) * CHUNK)
                place = slice(i * own + k * CHUNK, i * own + (k + 1) * CHUNK)
                cross = lax.dot_general(
                    row_ref[part, :], col_ref[:own, :], (((1,), (1,)), ((), ())), preferred_element_type=jnp.float32
                )
                kern = jnp.exp(2.0 * kernel_rate * cross + halves[i][part, :] + col_half).astype(jnp.bfloat16)
                tile_ref[place, j * own : (j + 1) * own] = kern
                image_ref[:, place] += lax.dot_general(
                    field, kern, (((1,), (1,)), ((), ())), preferred_element_type=jnp.float32
                )


def build(rows, cols, own, probes, halves=(), prior=(), side=None):
    features = rows[0].shape[1]
    height, width = len(rows) * own, len(cols) * own
    counts = (len(rows), len(cols), len(halves), len(prior), side is not None)
    out_shape = [
        pltpu.VMEM((height, width), jnp.bfloat16),
        jax.ShapeDtypeStruct((probes, height), jnp.float32),
    ]
    if not halves:
        out_shape.append(jax.ShapeDtypeStruct((height, 1), jnp.float32))
    args = [*rows, *cols, *halves, *prior] + ([] if side is None else [side])
    return pl.pallas_call(
        functools.partial(tile_kernel, counts, probes),
        out_shape=out_shape,
        compiler_params=pltpu.CompilerParams(vmem_limit_bytes=16 << 20),
        cost_estimate=pl.CostEstimate(
            flops=height * width * features // 8, bytes_accessed=1 << 10, transcendentals=0
        ),
        name="build_tile",
    )(*args)


def second_kernel(own, places, *refs):
    parts, refs = refs[:NZ], refs[NZ:]
    tiles, (mine_ref, other_ref, rho_ref) = refs[: len(places)], refs[len(places) :]
    probes = rho_ref.shape[0]
    pieces = []
    for p in ROWS:
        piece = 0.0
        for s in range(NZ):
            at = ROWS.index((p - s) % NZ) * own
            piece = piece + parts[s][:, at : at + own]
        pieces.append(-STEP * piece)
    rho_ref[...] = pieces[0]
    rho = jnp.concatenate(pieces, axis=1)
    high, low, _ = split(rho)
    narrow = jnp.concatenate([high, low], axis=0)
    for j, (h, m) in enumerate(COLS):
        part = 0.0
        for tile_ref, (top, left) in zip(tiles, places):
            at = j * own - left
            if 0 <= at < tile_ref.shape[1]:
                part = part + jnp.dot(
                    narrow[:, top : top + tile_ref.shape[0]],
                    tile_ref[:, at : at + own],
                    preferred_element_type=jnp.float32,
                )
        (other_ref if h else mine_ref)[:, m * own : (m + 1) * own] = part[:probes] + part[probes:]


def second_product(tiles, parts, own):
    probes, rows = parts[0].shape
    cols = len(COLS) * own
    places = [(top, left) for _, top, left in tiles]
    return pl.pallas_call(
        functools.partial(second_kernel, own, places),
        in_specs=[pl.BlockSpec(memory_space=pltpu.VMEM)] * (NZ + len(tiles)),
        out_shape=[
            jax.ShapeDtypeStruct((probes, cols // NC), jnp.float32),
            jax.ShapeDtypeStruct((probes, cols // NC), jnp.float32),
            jax.ShapeDtypeStruct((probes, own), jnp.float32),
        ],
        compiler_params=pltpu.CompilerParams(vmem_limit_bytes=16 << 20),
        cost_estimate=pl.CostEstimate(flops=rows * cols * 32, bytes_accessed=1 << 10, transcendentals=0),
        name="second_product",
    )(*parts, *[tile for tile, _, _ in tiles])


def sums_kernel(side_ref, rho_ref, *refs):
    shares, (image_ref, sums_ref) = refs[:NY], refs[NY:]
    side, rho = side_ref[...], rho_ref[...]
    image = noise_level * rho
    for share in shares:
        image = image + share[...]
    image_ref[...] = image
    total = lambda a, b: jnp.sum(a * b, axis=1, keepdims=True)
    lane = lax.broadcasted_iota(jnp.int32, (side.shape[0], LANES), 1)
    sums = 0.0
    for k, one in enumerate((total(side, side), total(side, rho), total(rho, rho), total(rho, image))):
        sums = jnp.where(lane == k, one, sums)
    sums_ref[...] = jnp.pad(sums.T[:8], ((0, 0), (0, LANES - side.shape[0])))


def local_sums(side, rho, shares):
    return pl.pallas_call(
        sums_kernel,
        out_shape=[
            jax.ShapeDtypeStruct(side.shape, jnp.float32),
            jax.ShapeDtypeStruct((8, LANES), jnp.float32),
        ],
        compiler_params=pltpu.CompilerParams(vmem_limit_bytes=4 << 20),
        name="local_sums",
    )(side, rho, *shares)


def finish_kernel(side_ref, rho_ref, image_ref, sums_ref, field_ref, residual_ref):
    side, rho, image = side_ref[...], rho_ref[...], image_ref[...]
    sums = jnp.sum(sums_ref[...], axis=0).T[: side.shape[0]]
    rr, side_rho, rho_rho, rho_image = (sums[:, k : k + 1] for k in range(4))
    curve = (rr - side_rho) / STEP
    alpha = rr / curve
    turn = alpha / STEP
    rest = 1.0 - turn
    rr_next = rest * rest * rr + 2.0 * rest * turn * side_rho + turn * turn * rho_rho
    gain = rest + rr_next / rr
    cross = (side_rho - rho_rho) / STEP
    curve = gain * gain * curve + 2.0 * gain * turn * cross + turn * turn * rho_image
    alpha_next = rr_next / curve
    direction = gain * side + turn * rho
    field_ref[...] = alpha * side + alpha_next * direction
    residual_ref[...] = rest * side + turn * rho - alpha_next * (gain / STEP * (side - rho) + turn * image)


def finish(side, rho, image, sums):
    return pl.pallas_call(
        finish_kernel,
        out_shape=[jax.ShapeDtypeStruct(side.shape, jnp.float32)] * 2,
        compiler_params=pltpu.CompilerParams(vmem_limit_bytes=4 << 20),
        name="finish",
    )(side, rho, image, sums)


def on_device(states, offsets, right_side):
    own, probes = right_side.shape
    side = right_side.T
    points = lax.dynamic_slice_in_dim(states, offsets[0], own, 0)
    with jax.named_scope("fetch_points"):
        message = pack(points, side)
        row, col = {0: points}, {(0, 0): message}
        for k in (1, 3):
            col[0, k] = shift(message, "y", NY, k)
            row[k] = shift(points, "z", NZ, k)
        col[1, 0] = shift(message, "c", NC, 1)
        row[1], row[3], col[0, 1], col[0, 3] = lax.optimization_barrier((row[1], row[3], col[0, 1], col[0, 3]))
        far = []
        for axis, size, ahead, behind in (("z", NZ, row[1], row[3]), ("y", NY, col[0, 1], col[0, 3])):
            middle = ahead.shape[0] // 2
            far.append((shift(ahead[:middle], axis, size, 1), shift(behind[middle:], axis, size, -1)))
        pair = shift(jnp.concatenate([col[0, 1], col[0, 3]], axis=0), "c", NC, 1)
        col[1, 1], col[1, 3] = pair[: message.shape[0]], pair[message.shape[0] :]
        near = [row[k] for k in ROWS[:3]]

    with jax.named_scope("build_tiles"):
        at = [col[k] for k in COLS[:6]]
        tile_a, image, half = build(near, at[:2], own, probes, side=side)
        tile_b, image = build(near, at[2:4], own, probes, [half], [image])
        tile_c, image = build(near, at[4:6], own, probes, [half], [image])
        far, image = lax.optimization_barrier((far, image))
        row[2] = jnp.concatenate(far[0], axis=0)
        col[0, 2] = jnp.concatenate(far[1], axis=0)
        col[1, 2] = shift(col[0, 2], "c", NC, 1)
        tile_d, image_far, half_far = build([row[2]], at, own, probes)
        at = [col[0, 2], col[1, 2]]
        tile_e, image = build(near + [row[2]], at, own, probes, [half, half_far], [image, image_far])
        tiles = [
            (tile_a, 0, 0),
            (tile_b, 0, 2 * own),
            (tile_c, 0, 4 * own),
            (tile_d, 3 * own, 0),
            (tile_e, 0, 6 * own),
        ]

    with jax.named_scope("sum_over_z"):
        parts = [image] + [None] * (NZ - 1)
        for k in (1, 3, 2):
            parts[k] = shift(image, "z", NZ, k)

    mine, other, rho = second_product(tiles, parts, own)

    with jax.named_scope("sum_over_yc"):
        mine = mine + shift(other, "c", NC, 1)
        shares = [mine[:, :own]]
        for m in (1, 3, 2):
            shares.append(shift(mine[:, m * own : (m + 1) * own], "y", NY, -m))

    with jax.named_scope("final_sums"):
        image, sums = local_sums(side, rho, shares)
        sums = jnp.broadcast_to(sums, (NY * NZ * NC, 8, LANES))
        sums = lax.all_to_all(sums, ("y", "z", "c"), 0, 0, tiled=True)

    field, residual = finish(side, rho, image, sums)
    return field.T, residual.T


def solution(mesh):
    fine = Mesh(mesh.devices.reshape(NY, NZ, NC, NX), ("y", "z", "c", "x"))
    rows = ("y", "z", "c")
    in_specs = (P(rows, None), P(rows), P(rows, "x"))
    out_specs = (P(rows, "x"), P(rows, "x"))
    return jax.shard_map(on_device, mesh=fine, in_specs=in_specs, out_specs=out_specs, check_vma=False)
```

```python
import functools

import jax
import jax.numpy as jnp
from jax import lax
from jax.experimental import pallas as pl
from jax.experimental.pallas import tpu as pltpu
from jax.sharding import Mesh
from jax.sharding import PartitionSpec as P

NY, NZ, NC, NX = 4, 4, 2, 4
LANES = 128
CHUNK = 256
ROWS = (0, 1, 3, 2)
COLS = ((0, 0), (1, 0), (0, 1), (0, 3), (1, 1), (1, 3), (0, 2), (1, 2))

noise_level = 1.0
kernel_rate = 0.5
STEP = 1.0 / (1.0 + noise_level)


def shift(value, axis, size, step):
    return lax.ppermute(value, axis, [(i, (i + step) % size) for i in range(size)])


def hand_on(behind, ahead, axis, size):
    value = jnp.where(lax.axis_index("c") == 0, behind, ahead)
    pairs = []
    for i in range(size):
        pairs += [(i * NC, (i + 1) % size * NC), (i * NC + 1, (i - 1) % size * NC + 1)]
    return lax.ppermute(value, (axis, "c"), pairs)


def split(value):
    high = value.astype(jnp.bfloat16)
    rest = value - high.astype(jnp.float32)
    middle = rest.astype(jnp.bfloat16)
    return high, middle, (rest - middle.astype(jnp.float32)).astype(jnp.bfloat16)


def pack_kernel(points_ref, side_ref, out_ref):
    own, width = points_ref.shape
    probes = side_ref.shape[0]
    out_ref[:own, :] = points_ref[...]
    high, middle, _ = split(points_ref[...].astype(jnp.float32) ** 2)
    ones = jnp.ones((probes, width), jnp.bfloat16)
    norms = 0.0
    for term in (high, middle):
        norms = norms + lax.dot_general(ones, term, (((1,), (1,)), ((), ())), preferred_element_type=jnp.float32)
    high, middle, low = split(norms)
    row = lax.broadcasted_iota(jnp.int32, norms.shape, 0)
    norms = jnp.where(row == 0, high.astype(jnp.float32), jnp.where(row == 1, middle.astype(jnp.float32), low.astype(jnp.float32)))
    at = own
    for part in (side_ref[...].astype(jnp.bfloat16), norms.astype(jnp.bfloat16)):
        for j in range(own // width):
            out_ref[at : at + probes, :] = part[:, j * width : (j + 1) * width]
            at += probes


def pack(points, side):
    own, width = points.shape
    extra = side.shape[0] * 2 * own // width
    return pl.pallas_call(
        pack_kernel,
        out_shape=jax.ShapeDtypeStruct((own + extra, width), jnp.bfloat16),
        compiler_params=pltpu.CompilerParams(vmem_limit_bytes=8 << 20),
        name="pack",
    )(points, side)


def unpack_rows(message, probes, own, term):
    width = message.shape[1]
    count = own // width
    at = own + term * count * probes
    return jnp.concatenate([message[at + j * probes : at + (j + 1) * probes] for j in range(count)], axis=1)


def tile_kernel(counts, probes, *refs):
    rows_count, cols_count, known_halves, prior_count, has_side = counts
    refs = list(refs)
    row_refs = [refs.pop(0) for _ in range(rows_count)]
    col_refs = [refs.pop(0) for _ in range(cols_count)]
    half_refs = [refs.pop(0) for _ in range(known_halves)]
    prior_refs = [refs.pop(0) for _ in range(prior_count)]
    side_ref = refs.pop(0) if has_side else None
    tile_ref, image_ref = refs.pop(0), refs.pop(0)
    own = tile_ref.shape[0] // rows_count
    if known_halves:
        pieces = []
        for half_ref in half_refs:
            pieces += [half_ref[j * own : (j + 1) * own, :] for j in range(half_ref.shape[0] // own)]
        halves = pieces
    else:
        new_ref = refs.pop(0)
        halves = []
        for i, row_ref in enumerate(row_refs):
            squares = row_ref[:own, :].astype(jnp.float32) ** 2
            halves.append(-kernel_rate * jnp.sum(squares, axis=1, keepdims=True))
            new_ref[i * own : (i + 1) * own, :] = halves[-1]
    if prior_count:
        at = 0
        for prior_ref in prior_refs:
            image_ref[:, at : at + prior_ref.shape[1]] = prior_ref[...]
            at += prior_ref.shape[1]
    else:
        image_ref[...] = jnp.zeros_like(image_ref)
        if has_side:
            image_ref[:, :own] = (noise_level - 1.0 / STEP) * side_ref[...]
    for j, col_ref in enumerate(col_refs):
        field = unpack_rows(col_ref, probes, own, 0)
        norms = unpack_rows(col_ref, probes, own, 1).astype(jnp.float32)
        col_half = -kernel_rate * (norms[0:1] + norms[1:2] + norms[2:3])
        for i, row_ref in enumerate(row_refs):
            for k in range(own // CHUNK):
                part = slice(k * CHUNK, (k + 1) * CHUNK)
                place = slice(i * own + k * CHUNK, i * own + (k + 1) * CHUNK)
                cross = lax.dot_general(
                    row_ref[part, :], col_ref[:own, :], (((1,), (1,)), ((), ())), preferred_element_type=jnp.float32
                )
                kern = jnp.exp(2.0 * kernel_rate * cross + halves[i][part, :] + col_half).astype(jnp.bfloat16)
                tile_ref[place, j * own : (j + 1) * own] = kern
                image_ref[:, place] += lax.dot_general(
                    field, kern, (((1,), (1,)), ((), ())), preferred_element_type=jnp.float32
                )


def build(rows, cols, own, probes, halves=(), prior=(), side=None):
    features = rows[0].shape[1]
    height, width = len(rows) * own, len(cols) * own
    counts = (len(rows), len(cols), len(halves), len(prior), side is not None)
    out_shape = [
        pltpu.VMEM((height, width), jnp.bfloat16),
        jax.ShapeDtypeStruct((probes, height), jnp.float32),
    ]
    if not halves:
        out_shape.append(jax.ShapeDtypeStruct((height, 1), jnp.float32))
    args = [*rows, *cols, *halves, *prior] + ([] if side is None else [side])
    return pl.pallas_call(
        functools.partial(tile_kernel, counts, probes),
        out_shape=out_shape,
        compiler_params=pltpu.CompilerParams(vmem_limit_bytes=16 << 20),
        cost_estimate=pl.CostEstimate(
            flops=height * width * features // 8, bytes_accessed=1 << 10, transcendentals=0
        ),
        name="build_tile",
    )(*args)


def second_kernel(own, places, *refs):
    parts, refs = refs[:NZ], refs[NZ:]
    tiles, (mine_ref, other_ref, rho_ref) = refs[: len(places)], refs[len(places) :]
    probes = rho_ref.shape[0]
    pieces = []
    for p in ROWS:
        piece = 0.0
        for s in range(NZ):
            at = ROWS.index((p - s) % NZ) * own
            piece = piece + parts[s][:, at : at + own]
        pieces.append(-STEP * piece)
    rho_ref[...] = pieces[0]
    rho = jnp.concatenate(pieces, axis=1)
    high, low, _ = split(rho)
    narrow = jnp.concatenate([high, low], axis=0)
    for j, (h, m) in enumerate(COLS):
        part = 0.0
        for tile_ref, (top, left) in zip(tiles, places):
            at = j * own - left
            if 0 <= at < tile_ref.shape[1]:
                part = part + jnp.dot(
                    narrow[:, top : top + tile_ref.shape[0]],
                    tile_ref[:, at : at + own],
                    preferred_element_type=jnp.float32,
                )
        (other_ref if h else mine_ref)[:, m * own : (m + 1) * own] = part[:probes] + part[probes:]


def second_product(tiles, parts, own):
    probes, rows = parts[0].shape
    cols = len(COLS) * own
    places = [(top, left) for _, top, left in tiles]
    return pl.pallas_call(
        functools.partial(second_kernel, own, places),
        in_specs=[pl.BlockSpec(memory_space=pltpu.VMEM)] * (NZ + len(tiles)),
        out_shape=[
            jax.ShapeDtypeStruct((probes, cols // NC), jnp.float32),
            jax.ShapeDtypeStruct((probes, cols // NC), jnp.float32),
            jax.ShapeDtypeStruct((probes, own), jnp.float32),
        ],
        compiler_params=pltpu.CompilerParams(vmem_limit_bytes=16 << 20),
        cost_estimate=pl.CostEstimate(flops=rows * cols * 32, bytes_accessed=1 << 10, transcendentals=0),
        name="second_product",
    )(*parts, *[tile for tile, _, _ in tiles])


def sums_kernel(side_ref, rho_ref, *refs):
    shares, (image_ref, sums_ref) = refs[:NY], refs[NY:]
    side, rho = side_ref[...], rho_ref[...]
    image = noise_level * rho
    for share in shares:
        image = image + share[...]
    image_ref[...] = image
    total = lambda a, b: jnp.sum(a * b, axis=1, keepdims=True)
    lane = lax.broadcasted_iota(jnp.int32, (side.shape[0], LANES), 1)
    sums = 0.0
    for k, one in enumerate((total(side, side), total(side, rho), total(rho, rho), total(rho, image))):
        sums = jnp.where(lane == k, one, sums)
    sums_ref[...] = jnp.pad(sums.T[:8], ((0, 0), (0, LANES - side.shape[0])))


def local_sums(side, rho, shares):
    return pl.pallas_call(
        sums_kernel,
        out_shape=[
            jax.ShapeDtypeStruct(side.shape, jnp.float32),
            jax.ShapeDtypeStruct((8, LANES), jnp.float32),
        ],
        compiler_params=pltpu.CompilerParams(vmem_limit_bytes=4 << 20),
        name="local_sums",
    )(side, rho, *shares)


def finish_kernel(side_ref, rho_ref, image_ref, sums_ref, field_ref, residual_ref):
    side, rho, image = side_ref[...], rho_ref[...], image_ref[...]
    sums = jnp.sum(sums_ref[...], axis=0).T[: side.shape[0]]
    rr, side_rho, rho_rho, rho_image = (sums[:, k : k + 1] for k in range(4))
    curve = (rr - side_rho) / STEP
    alpha = rr / curve
    turn = alpha / STEP
    rest = 1.0 - turn
    rr_next = rest * rest * rr + 2.0 * rest * turn * side_rho + turn * turn * rho_rho
    gain = rest + rr_next / rr
    cross = (side_rho - rho_rho) / STEP
    curve = gain * gain * curve + 2.0 * gain * turn * cross + turn * turn * rho_image
    alpha_next = rr_next / curve
    direction = gain * side + turn * rho
    field_ref[...] = alpha * side + alpha_next * direction
    residual_ref[...] = rest * side + turn * rho - alpha_next * (gain / STEP * (side - rho) + turn * image)


def finish(side, rho, image, sums):
    return pl.pallas_call(
        finish_kernel,
        out_shape=[jax.ShapeDtypeStruct(side.shape, jnp.float32)] * 2,
        compiler_params=pltpu.CompilerParams(vmem_limit_bytes=4 << 20),
        name="finish",
    )(side, rho, image, sums)


def on_device(states, offsets, right_side):
    own, probes = right_side.shape
    side = right_side.T
    points = lax.dynamic_slice_in_dim(states, offsets[0], own, 0)
    with jax.named_scope("fetch_points"):
        message = pack(points, side)
        row, col = {0: points}, {(0, 0): message}
        for k in (1, 3):
            col[0, k] = shift(message, "y", NY, k)
            row[k] = shift(points, "z", NZ, k)
        col[1, 0] = shift(message, "c", NC, 1)
        first = [col[0, 0], col[1, 0]]
        tile_a, image_a, half_a = build([points], first, own, probes, side=side)
        tile_b, image_b, half_b = build([row[1]], first, own, probes)
        near = row[1], row[3], col[0, 1], col[0, 3]
        near, image_a, image_b = lax.optimization_barrier((near, image_a, image_b))
        row[1], row[3], col[0, 1], col[0, 3] = near
        row[2] = hand_on(row[1], row[3], "z", NZ)
        col[0, 2] = hand_on(col[0, 1], col[0, 3], "y", NY)
        pair = shift(jnp.concatenate([col[0, 1], col[0, 3]], axis=0), "c", NC, 1)
        col[1, 1], col[1, 3] = pair[: message.shape[0]], pair[message.shape[0] :]

    with jax.named_scope("build_tiles"):
        near = [points, row[1], row[3]]
        tile_c, image_c, half_c = build([row[3]], first, own, probes)
        half = [half_a, half_b, half_c]
        tile_d, image = build(near, [col[0, 1], col[0, 3]], own, probes, half, [image_a, image_b, image_c])
        tile_e, image = build(near, [col[1, 1], col[1, 3]], own, probes, half, [image])
        far, image = lax.optimization_barrier(((row[2], col[0, 2]), image))
        row[2], col[0, 2] = far
        col[1, 2] = shift(col[0, 2], "c", NC, 1)
        at = [col[k] for k in COLS[:6]]
        tile_f, image_far, half_far = build([row[2]], at, own, probes)
        at = [col[0, 2], col[1, 2]]
        tile_g, image = build(near + [row[2]], at, own, probes, half + [half_far], [image, image_far])
        tiles = [
            (tile_a, 0, 0),
            (tile_b, own, 0),
            (tile_c, 2 * own, 0),
            (tile_d, 0, 2 * own),
            (tile_e, 0, 4 * own),
            (tile_f, 3 * own, 0),
            (tile_g, 0, 6 * own),
        ]

    with jax.named_scope("sum_over_z"):
        parts = [image] + [None] * (NZ - 1)
        for k in (1, 3, 2):
            parts[k] = shift(image, "z", NZ, k)

    mine, other, rho = second_product(tiles, parts, own)

    with jax.named_scope("sum_over_yc"):
        mine = mine + shift(other, "c", NC, 1)
        shares = [mine[:, :own]]
        for m in (1, 3, 2):
            shares.append(shift(mine[:, m * own : (m + 1) * own], "y", NY, -m))

    with jax.named_scope("final_sums"):
        image, sums = local_sums(side, rho, shares)
        sums = jnp.broadcast_to(sums, (NY * NZ * NC, 8, LANES))
        sums = lax.all_to_all(sums, ("y", "z", "c"), 0, 0, tiled=True)

    field, residual = finish(side, rho, image, sums)
    return field.T, residual.T


def solution(mesh):
    fine = Mesh(mesh.devices.reshape(NY, NZ, NC, NX), ("y", "z", "c", "x"))
    rows = ("y", "z", "c")
    in_specs = (P(rows, None), P(rows), P(rows, "x"))
    out_specs = (P(rows, "x"), P(rows, "x"))
    return jax.shard_map(on_device, mesh=fine, in_specs=in_specs, out_specs=out_specs, check_vma=False)
```

```python
import functools

import jax
import jax.numpy as jnp
from jax import lax
from jax.experimental import pallas as pl
from jax.experimental.pallas import tpu as pltpu
from jax.sharding import Mesh
from jax.sharding import PartitionSpec as P

NY, NZ, NC, NX = 4, 4, 2, 4
LANES = 128
CHUNK = 256
ROWS = (0, 1, 3, 2)
COLS = ((0, 0), (1, 0), (0, 1), (0, 3), (1, 1), (1, 3), (0, 2), (1, 2))

noise_level = 1.0
kernel_rate = 0.5
STEP = 1.0 / (1.0 + noise_level)


def shift(value, axis, size, step):
    return lax.ppermute(value, axis, [(i, (i + step) % size) for i in range(size)])


def hand_on(behind, ahead, axis, size):
    value = jnp.where(lax.axis_index("c") == 0, behind, ahead)
    pairs = []
    for i in range(size):
        pairs += [(i * NC, (i + 1) % size * NC), (i * NC + 1, (i - 1) % size * NC + 1)]
    return lax.ppermute(value, (axis, "c"), pairs)


def split(value):
    high = value.astype(jnp.bfloat16)
    rest = value - high.astype(jnp.float32)
    middle = rest.astype(jnp.bfloat16)
    return high, middle, (rest - middle.astype(jnp.float32)).astype(jnp.bfloat16)


def pack_kernel(points_ref, side_ref, out_ref):
    own, width = points_ref.shape
    probes = side_ref.shape[0]
    out_ref[:own, :] = points_ref[...]
    high, middle, _ = split(points_ref[...].astype(jnp.float32) ** 2)
    ones = jnp.ones((probes, width), jnp.bfloat16)
    norms = 0.0
    for term in (high, middle):
        norms = norms + lax.dot_general(ones, term, (((1,), (1,)), ((), ())), preferred_element_type=jnp.float32)
    high, middle, low = split(norms)
    row = lax.broadcasted_iota(jnp.int32, norms.shape, 0)
    norms = jnp.where(row == 0, high.astype(jnp.float32), jnp.where(row == 1, middle.astype(jnp.float32), low.astype(jnp.float32)))
    at = own
    for part in (side_ref[...].astype(jnp.bfloat16), norms.astype(jnp.bfloat16)):
        for j in range(own // width):
            out_ref[at : at + probes, :] = part[:, j * width : (j + 1) * width]
            at += probes


def pack(points, side):
    own, width = points.shape
    extra = side.shape[0] * 2 * own // width
    return pl.pallas_call(
        pack_kernel,
        out_shape=jax.ShapeDtypeStruct((own + extra, width), jnp.bfloat16),
        compiler_params=pltpu.CompilerParams(vmem_limit_bytes=8 << 20),
        name="pack",
    )(points, side)


def unpack_rows(message, probes, own, term):
    width = message.shape[1]
    count = own // width
    at = own + term * count * probes
    return jnp.concatenate([message[at + j * probes : at + (j + 1) * probes] for j in range(count)], axis=1)


def tile_kernel(counts, probes, *refs):
    rows_count, cols_count, known_halves, prior_count, has_side = counts
    refs = list(refs)
    row_refs = [refs.pop(0) for _ in range(rows_count)]
    col_refs = [refs.pop(0) for _ in range(cols_count)]
    half_refs = [refs.pop(0) for _ in range(known_halves)]
    prior_refs = [refs.pop(0) for _ in range(prior_count)]
    side_ref = refs.pop(0) if has_side else None
    tile_ref, image_ref = refs.pop(0), refs.pop(0)
    own = tile_ref.shape[0] // rows_count
    if known_halves:
        pieces = []
        for half_ref in half_refs:
            pieces += [half_ref[j * own : (j + 1) * own, :] for j in range(half_ref.shape[0] // own)]
        halves = pieces
    else:
        new_ref = refs.pop(0)
        halves = []
        for i, row_ref in enumerate(row_refs):
            squares = row_ref[:own, :].astype(jnp.float32) ** 2
            halves.append(-kernel_rate * jnp.sum(squares, axis=1, keepdims=True))
            new_ref[i * own : (i + 1) * own, :] = halves[-1]
    if prior_count:
        at = 0
        for prior_ref in prior_refs:
            image_ref[:, at : at + prior_ref.shape[1]] = prior_ref[...]
            at += prior_ref.shape[1]
    else:
        image_ref[...] = jnp.zeros_like(image_ref)
        if has_side:
            image_ref[:, :own] = (noise_level - 1.0 / STEP) * side_ref[...]
    for j, col_ref in enumerate(col_refs):
        field = unpack_rows(col_ref, probes, own, 0)
        norms = unpack_rows(col_ref, probes, own, 1).astype(jnp.float32)
        col_half = -kernel_rate * (norms[0:1] + norms[1:2] + norms[2:3])
        for i, row_ref in enumerate(row_refs):
            for k in range(own // CHUNK):
                part = slice(k * CHUNK, (k + 1) * CHUNK)
                place = slice(i * own + k * CHUNK, i * own + (k + 1) * CHUNK)
                cross = lax.dot_general(
                    row_ref[part, :], col_ref[:own, :], (((1,), (1,)), ((), ())), preferred_element_type=jnp.float32
                )
                kern = jnp.exp(2.0 * kernel_rate * cross + halves[i][part, :] + col_half).astype(jnp.bfloat16)
                tile_ref[place, j * own : (j + 1) * own] = kern
                image_ref[:, place] += lax.dot_general(
                    field, kern, (((1,), (1,)), ((), ())), preferred_element_type=jnp.float32
                )


def build(rows, cols, own, probes, halves=(), prior=(), side=None):
    features = rows[0].shape[1]
    height, width = len(rows) * own, len(cols) * own
    counts = (len(rows), len(cols), len(halves), len(prior), side is not None)
    out_shape = [
        pltpu.VMEM((height, width), jnp.bfloat16),
        jax.ShapeDtypeStruct((probes, height), jnp.float32),
    ]
    if not halves:
        out_shape.append(jax.ShapeDtypeStruct((height, 1), jnp.float32))
    args = [*rows, *cols, *halves, *prior] + ([] if side is None else [side])
    return pl.pallas_call(
        functools.partial(tile_kernel, counts, probes),
        out_shape=out_shape,
        compiler_params=pltpu.CompilerParams(vmem_limit_bytes=8 << 20),
        cost_estimate=pl.CostEstimate(
            flops=height * width * features // 8, bytes_accessed=1 << 10, transcendentals=0
        ),
        name="build_tile",
    )(*args)


def second_kernel(own, places, *refs):
    parts, refs = refs[:NZ], refs[NZ:]
    tiles, (mine_ref, other_ref, rho_ref) = refs[: len(places)], refs[len(places) :]
    probes = rho_ref.shape[0]
    pieces = []
    for p in ROWS:
        piece = 0.0
        for s in range(NZ):
            at = ROWS.index((p - s) % NZ) * own
            piece = piece + parts[s][:, at : at + own]
        pieces.append(-STEP * piece)
    rho_ref[...] = pieces[0]
    rho = jnp.concatenate(pieces, axis=1)
    high, low, _ = split(rho)
    narrow = jnp.concatenate([high, low], axis=0)
    for j, (h, m) in enumerate(COLS):
        part = 0.0
        for tile_ref, (top, left) in zip(tiles, places):
            at = j * own - left
            if 0 <= at < tile_ref.shape[1]:
                part = part + jnp.dot(
                    narrow[:, top : top + tile_ref.shape[0]],
                    tile_ref[:, at : at + own],
                    preferred_element_type=jnp.float32,
                )
        (other_ref if h else mine_ref)[:, m * own : (m + 1) * own] = part[:probes] + part[probes:]


def second_product(tiles, parts, own):
    probes, rows = parts[0].shape
    cols = len(COLS) * own
    places = [(top, left) for _, top, left in tiles]
    return pl.pallas_call(
        functools.partial(second_kernel, own, places),
        in_specs=[pl.BlockSpec(memory_space=pltpu.VMEM)] * (NZ + len(tiles)),
        out_shape=[
            jax.ShapeDtypeStruct((probes, cols // NC), jnp.float32),
            jax.ShapeDtypeStruct((probes, cols // NC), jnp.float32),
            jax.ShapeDtypeStruct((probes, own), jnp.float32),
        ],
        compiler_params=pltpu.CompilerParams(vmem_limit_bytes=8 << 20),
        cost_estimate=pl.CostEstimate(flops=rows * cols * 32, bytes_accessed=1 << 10, transcendentals=0),
        name="second_product",
    )(*parts, *[tile for tile, _, _ in tiles])


def sums_kernel(side_ref, rho_ref, *refs):
    shares, (image_ref, sums_ref) = refs[:NY], refs[NY:]
    side, rho = side_ref[...], rho_ref[...]
    image = noise_level * rho
    for share in shares:
        image = image + share[...]
    image_ref[...] = image
    total = lambda a, b: jnp.sum(a * b, axis=1, keepdims=True)
    lane = lax.broadcasted_iota(jnp.int32, (side.shape[0], LANES), 1)
    sums = 0.0
    for k, one in enumerate((total(side, side), total(side, rho), total(rho, rho), total(rho, image))):
        sums = jnp.where(lane == k, one, sums)
    sums_ref[...] = jnp.pad(sums.T[:8], ((0, 0), (0, LANES - side.shape[0])))


def local_sums(side, rho, shares):
    return pl.pallas_call(
        sums_kernel,
        out_shape=[
            jax.ShapeDtypeStruct(side.shape, jnp.float32),
            jax.ShapeDtypeStruct((8, LANES), jnp.float32),
        ],
        compiler_params=pltpu.CompilerParams(vmem_limit_bytes=4 << 20),
        name="local_sums",
    )(side, rho, *shares)


def finish_kernel(side_ref, rho_ref, image_ref, sums_ref, field_ref, residual_ref):
    side, rho, image = side_ref[...], rho_ref[...], image_ref[...]
    sums = jnp.sum(sums_ref[...], axis=0).T[: side.shape[0]]
    rr, side_rho, rho_rho, rho_image = (sums[:, k : k + 1] for k in range(4))
    curve = (rr - side_rho) / STEP
    alpha = rr / curve
    turn = alpha / STEP
    rest = 1.0 - turn
    rr_next = rest * rest * rr + 2.0 * rest * turn * side_rho + turn * turn * rho_rho
    gain = rest + rr_next / rr
    cross = (side_rho - rho_rho) / STEP
    curve = gain * gain * curve + 2.0 * gain * turn * cross + turn * turn * rho_image
    alpha_next = rr_next / curve
    direction = gain * side + turn * rho
    field_ref[...] = alpha * side + alpha_next * direction
    residual_ref[...] = rest * side + turn * rho - alpha_next * (gain / STEP * (side - rho) + turn * image)


def finish(side, rho, image, sums):
    return pl.pallas_call(
        finish_kernel,
        out_shape=[jax.ShapeDtypeStruct(side.shape, jnp.float32)] * 2,
        compiler_params=pltpu.CompilerParams(vmem_limit_bytes=4 << 20),
        name="finish",
    )(side, rho, image, sums)


def on_device(states, offsets, right_side):
    own, probes = right_side.shape
    side = right_side.T
    points = lax.dynamic_slice_in_dim(states, offsets[0], own, 0)
    with jax.named_scope("fetch_points"):
        message = pack(points, side)
        row, col = {0: points}, {(0, 0): message}
        for k in (1, 3):
            col[0, k] = shift(message, "y", NY, k)
            row[k] = shift(points, "z", NZ, k)
        col[1, 0] = shift(message, "c", NC, 1)
        first = [col[0, 0], col[1, 0]]
        tile_a, image_a, half_a = build([points], first, own, probes, side=side)
        tile_b, image_b, half_b = build([row[1]], first, own, probes)
        near = row[1], row[3], col[0, 1], col[0, 3]
        near, image_a, image_b = lax.optimization_barrier((near, image_a, image_b))
        row[1], row[3], col[0, 1], col[0, 3] = near
        row[2] = hand_on(row[1], row[3], "z", NZ)
        col[0, 2] = hand_on(col[0, 1], col[0, 3], "y", NY)
        for k in (1, 3):
            col[1, k] = shift(col[0, k], "c", NC, 1)

    with jax.named_scope("build_tiles"):
        near = [points, row[1], row[3]]
        tile_c, image_c, half_c = build([row[3]], first, own, probes)
        half = [half_a, half_b, half_c]
        tile_d, image = build(near, [col[0, 1], col[0, 3]], own, probes, half, [image_a, image_b, image_c])
        tile_e, image = build(near, [col[1, 1], col[1, 3]], own, probes, half, [image])
        at = [col[k] for k in COLS[:6]]
        row[2], image = lax.optimization_barrier((row[2], image))
        tile_f, image_far, half_far = build([row[2]], at, own, probes)
        col[0, 2], image_far = lax.optimization_barrier((col[0, 2], image_far))
        col[1, 2] = shift(col[0, 2], "c", NC, 1)
        near.append(row[2])
        half.append(half_far)
        tile_g, image = build(near, [col[0, 2]], own, probes, half, [image, image_far])
        tile_h, image = build(near, [col[1, 2]], own, probes, half, [image])
        tiles = [
            (tile_a, 0, 0),
            (tile_b, own, 0),
            (tile_c, 2 * own, 0),
            (tile_d, 0, 2 * own),
            (tile_e, 0, 4 * own),
            (tile_f, 3 * own, 0),
            (tile_g, 0, 6 * own),
            (tile_h, 0, 7 * own),
        ]

    with jax.named_scope("sum_over_z"):
        parts = [image] + [None] * (NZ - 1)
        for k in (1, 3, 2):
            parts[k] = shift(image, "z", NZ, k)

    mine, other, rho = second_product(tiles, parts, own)

    with jax.named_scope("sum_over_yc"):
        mine = mine + shift(other, "c", NC, 1)
        shares = [mine[:, :own]]
        for m in (1, 3, 2):
            shares.append(shift(mine[:, m * own : (m + 1) * own], "y", NY, -m))

    with jax.named_scope("final_sums"):
        image, sums = local_sums(side, rho, shares)
        sums = jnp.broadcast_to(sums, (NY * NZ * NC, 8, LANES))
        sums = lax.all_to_all(sums, ("y", "z", "c"), 0, 0, tiled=True)

    field, residual = finish(side, rho, image, sums)
    return field.T, residual.T


def solution(mesh):
    fine = Mesh(mesh.devices.reshape(NY, NZ, NC, NX), ("y", "z", "c", "x"))
    rows = ("y", "z", "c")
    in_specs = (P(rows, None), P(rows), P(rows, "x"))
    out_specs = (P(rows, "x"), P(rows, "x"))
    return jax.shard_map(on_device, mesh=fine, in_specs=in_specs, out_specs=out_specs, check_vma=False)
```

```python
import functools

import jax
import jax.numpy as jnp
from jax import lax
from jax.experimental import pallas as pl
from jax.experimental.pallas import tpu as pltpu
from jax.sharding import Mesh
from jax.sharding import PartitionSpec as P

NY, NZ, NC, NX = 4, 4, 2, 4
LANES = 128
CHUNK = 256
HERE = (0, 0)
ROWS = (HERE, (3, 0), (0, 3), (3, 3))
SQUARE = (HERE, (1, 0), (0, 1), (1, 1))
COLS = ((0, 0), (1, 0), (0, 1), (0, 2), (1, 1), (1, 2), (0, 3), (1, 3))

noise_level = 1.0
kernel_rate = 0.5
STEP = 1.0 / (1.0 + noise_level)


def swap(value, offset):
    pairs = []
    for y in range(NY):
        for z in range(NZ):
            pairs.append((y * NZ + z, (y ^ offset[0]) * NZ + (z ^ offset[1])))
    return lax.ppermute(value, ("y", "z"), pairs)


def swap_core(value):
    return lax.ppermute(value, "c", [(0, 1), (1, 0)])


def split(value):
    high = value.astype(jnp.bfloat16)
    rest = value - high.astype(jnp.float32)
    middle = rest.astype(jnp.bfloat16)
    return high, middle, (rest - middle.astype(jnp.float32)).astype(jnp.bfloat16)


def pack_kernel(points_ref, side_ref, out_ref):
    own, width = points_ref.shape
    probes = side_ref.shape[0]
    out_ref[:own, :] = points_ref[...]
    high, middle, _ = split(points_ref[...].astype(jnp.float32) ** 2)
    ones = jnp.ones((probes, width), jnp.bfloat16)
    norms = 0.0
    for term in (high, middle):
        norms = norms + lax.dot_general(ones, term, (((1,), (1,)), ((), ())), preferred_element_type=jnp.float32)
    high, middle, low = split(norms)
    row = lax.broadcasted_iota(jnp.int32, norms.shape, 0)
    norms = jnp.where(row == 0, high.astype(jnp.float32), jnp.where(row == 1, middle.astype(jnp.float32), low.astype(jnp.float32)))
    at = own
    for part in (side_ref[...].astype(jnp.bfloat16), norms.astype(jnp.bfloat16)):
        for j in range(own // width):
            out_ref[at : at + probes, :] = part[:, j * width : (j + 1) * width]
            at += probes


def pack(points, side):
    own, width = points.shape
    extra = side.shape[0] * 2 * own // width
    return pl.pallas_call(
        pack_kernel,
        out_shape=jax.ShapeDtypeStruct((own + extra, width), jnp.bfloat16),
        compiler_params=pltpu.CompilerParams(vmem_limit_bytes=8 << 20),
        name="pack",
    )(points, side)


def unpack_rows(message, probes, own, term):
    width = message.shape[1]
    count = own // width
    at = own + term * count * probes
    return jnp.concatenate([message[at + j * probes : at + (j + 1) * probes] for j in range(count)], axis=1)


def tile_kernel(counts, probes, *refs):
    rows_count, cols_count, known_halves, prior_count, has_side = counts
    refs = list(refs)
    row_refs = [refs.pop(0) for _ in range(rows_count)]
    col_refs = [refs.pop(0) for _ in range(cols_count)]
    half_refs = [refs.pop(0) for _ in range(known_halves)]
    prior_refs = [refs.pop(0) for _ in range(prior_count)]
    side_ref = refs.pop(0) if has_side else None
    tile_ref, image_ref = refs.pop(0), refs.pop(0)
    own = tile_ref.shape[0] // rows_count
    if known_halves:
        pieces = []
        for half_ref in half_refs:
            pieces += [half_ref[j * own : (j + 1) * own, :] for j in range(half_ref.shape[0] // own)]
        halves = pieces
    else:
        new_ref = refs.pop(0)
        halves = []
        for i, row_ref in enumerate(row_refs):
            squares = row_ref[:own, :].astype(jnp.float32) ** 2
            halves.append(-kernel_rate * jnp.sum(squares, axis=1, keepdims=True))
            new_ref[i * own : (i + 1) * own, :] = halves[-1]
    if prior_count:
        at = 0
        for prior_ref in prior_refs:
            image_ref[:, at : at + prior_ref.shape[1]] = prior_ref[...]
            at += prior_ref.shape[1]
    else:
        image_ref[...] = jnp.zeros_like(image_ref)
        if has_side:
            image_ref[:, :own] = (noise_level - 1.0 / STEP) * side_ref[...]
    for j, col_ref in enumerate(col_refs):
        field = unpack_rows(col_ref, probes, own, 0)
        norms = unpack_rows(col_ref, probes, own, 1).astype(jnp.float32)
        col_half = -kernel_rate * (norms[0:1] + norms[1:2] + norms[2:3])
        for i, row_ref in enumerate(row_refs):
            for k in range(own // CHUNK):
                part = slice(k * CHUNK, (k + 1) * CHUNK)
                place = slice(i * own + k * CHUNK, i * own + (k + 1) * CHUNK)
                cross = lax.dot_general(
                    row_ref[part, :], col_ref[:own, :], (((1,), (1,)), ((), ())), preferred_element_type=jnp.float32
                )
                kern = jnp.exp(2.0 * kernel_rate * cross + halves[i][part, :] + col_half).astype(jnp.bfloat16)
                tile_ref[place, j * own : (j + 1) * own] = kern
                image_ref[:, place] += lax.dot_general(
                    field, kern, (((1,), (1,)), ((), ())), preferred_element_type=jnp.float32
                )


def build(rows, cols, own, probes, halves=(), prior=(), side=None):
    features = rows[0].shape[1]
    height, width = len(rows) * own, len(cols) * own
    counts = (len(rows), len(cols), len(halves), len(prior), side is not None)
    out_shape = [
        pltpu.VMEM((height, width), jnp.bfloat16),
        jax.ShapeDtypeStruct((probes, height), jnp.float32),
    ]
    if not halves:
        out_shape.append(jax.ShapeDtypeStruct((height, 1), jnp.float32))
    args = [*rows, *cols, *halves, *prior] + ([] if side is None else [side])
    return pl.pallas_call(
        functools.partial(tile_kernel, counts, probes),
        out_shape=out_shape,
        compiler_params=pltpu.CompilerParams(vmem_limit_bytes=8 << 20),
        cost_estimate=pl.CostEstimate(
            flops=height * width * features // 8, bytes_accessed=1 << 10, transcendentals=0
        ),
        name="build_tile",
    )(*args)


def second_kernel(own, places, *refs):
    parts, refs = refs[: len(ROWS)], refs[len(ROWS) :]
    tiles, (mine_ref, other_ref, rho_ref) = refs[: len(places)], refs[len(places) :]
    probes = rho_ref.shape[0]
    pieces = []
    for p in ROWS:
        piece = 0.0
        for s, part in zip(ROWS, parts):
            at = ROWS.index((p[0] ^ s[0], p[1] ^ s[1])) * own
            piece = piece + part[:, at : at + own]
        pieces.append(-STEP * piece)
    rho_ref[...] = pieces[0]
    rho = jnp.concatenate(pieces, axis=1)
    high, low, _ = split(rho)
    narrow = jnp.concatenate([high, low], axis=0)
    for j, (h, m) in enumerate(COLS):
        part = 0.0
        for tile_ref, (top, left) in zip(tiles, places):
            at = j * own - left
            if 0 <= at < tile_ref.shape[1]:
                part = part + jnp.dot(
                    narrow[:, top : top + tile_ref.shape[0]],
                    tile_ref[:, at : at + own],
                    preferred_element_type=jnp.float32,
                )
        (other_ref if h else mine_ref)[:, m * own : (m + 1) * own] = part[:probes] + part[probes:]


def second_product(tiles, parts, own):
    probes, rows = parts[0].shape
    cols = len(COLS) * own
    places = [(top, left) for _, top, left in tiles]
    return pl.pallas_call(
        functools.partial(second_kernel, own, places),
        in_specs=[pl.BlockSpec(memory_space=pltpu.VMEM)] * (len(ROWS) + len(tiles)),
        out_shape=[
            jax.ShapeDtypeStruct((probes, cols // NC), jnp.float32),
            jax.ShapeDtypeStruct((probes, cols // NC), jnp.float32),
            jax.ShapeDtypeStruct((probes, own), jnp.float32),
        ],
        compiler_params=pltpu.CompilerParams(vmem_limit_bytes=8 << 20),
        cost_estimate=pl.CostEstimate(flops=rows * cols * 32, bytes_accessed=1 << 10, transcendentals=0),
        name="second_product",
    )(*parts, *[tile for tile, _, _ in tiles])


def sums_kernel(side_ref, rho_ref, *refs):
    shares, (image_ref, sums_ref) = refs[: len(SQUARE)], refs[len(SQUARE) :]
    side, rho = side_ref[...], rho_ref[...]
    image = noise_level * rho
    for share in shares:
        image = image + share[...]
    image_ref[...] = image
    total = lambda a, b: jnp.sum(a * b, axis=1, keepdims=True)
    lane = lax.broadcasted_iota(jnp.int32, (side.shape[0], LANES), 1)
    sums = 0.0
    for k, one in enumerate((total(side, side), total(side, rho), total(rho, rho), total(rho, image))):
        sums = jnp.where(lane == k, one, sums)
    sums_ref[...] = jnp.pad(sums.T[:8], ((0, 0), (0, LANES - side.shape[0])))


def local_sums(side, rho, shares):
    return pl.pallas_call(
        sums_kernel,
        out_shape=[
            jax.ShapeDtypeStruct(side.shape, jnp.float32),
            jax.ShapeDtypeStruct((8, LANES), jnp.float32),
        ],
        compiler_params=pltpu.CompilerParams(vmem_limit_bytes=4 << 20),
        name="local_sums",
    )(side, rho, *shares)


def finish_kernel(side_ref, rho_ref, image_ref, sums_ref, field_ref, residual_ref):
    side, rho, image = side_ref[...], rho_ref[...], image_ref[...]
    sums = jnp.sum(sums_ref[...], axis=0).T[: side.shape[0]]
    rr, side_rho, rho_rho, rho_image = (sums[:, k : k + 1] for k in range(4))
    curve = (rr - side_rho) / STEP
    alpha = rr / curve
    turn = alpha / STEP
    rest = 1.0 - turn
    rr_next = rest * rest * rr + 2.0 * rest * turn * side_rho + turn * turn * rho_rho
    gain = rest + rr_next / rr
    cross = (side_rho - rho_rho) / STEP
    curve = gain * gain * curve + 2.0 * gain * turn * cross + turn * turn * rho_image
    alpha_next = rr_next / curve
    direction = gain * side + turn * rho
    field_ref[...] = alpha * side + alpha_next * direction
    residual_ref[...] = rest * side + turn * rho - alpha_next * (gain / STEP * (side - rho) + turn * image)


def finish(side, rho, image, sums):
    return pl.pallas_call(
        finish_kernel,
        out_shape=[jax.ShapeDtypeStruct(side.shape, jnp.float32)] * 2,
        compiler_params=pltpu.CompilerParams(vmem_limit_bytes=4 << 20),
        name="finish",
    )(side, rho, image, sums)


def on_device(states, offsets, right_side):
    own, probes = right_side.shape
    side = right_side.T
    points = lax.dynamic_slice_in_dim(states, offsets[0], own, 0)
    with jax.named_scope("fetch_points"):
        message = pack(points, side)
        rows = [points] + [swap(points, offset) for offset in ROWS[1:]]
        cols = [message] + [swap(message, offset) for offset in SQUARE[1:]]
        first = [message, swap_core(message)]
        tile_a, image_a, half_a = build([points], first, own, probes, side=side)
        (rows[1], rows[2], cols[1], cols[2]), image_a = lax.optimization_barrier(
            ((rows[1], rows[2], cols[1], cols[2]), image_a)
        )
        others = [swap_core(cols[1]), swap_core(cols[2])]

    with jax.named_scope("build_tiles"):
        tile_b, image_b, half_b = build(rows[1:3], first, own, probes)
        half = [half_a, half_b]
        tile_d, image = build(rows[:3], cols[1:3], own, probes, half, [image_a, image_b])
        tile_e, image = build(rows[:3], others, own, probes, half, [image])
        rows[3], image = lax.optimization_barrier((rows[3], image))
        tile_f, image_far, half_far = build([rows[3]], first + cols[1:3] + others, own, probes)
        cols[3], image_far = lax.optimization_barrier((cols[3], image_far))
        last = swap_core(cols[3])
        half.append(half_far)
        tile_g, image = build(rows, [cols[3]], own, probes, half, [image, image_far])
        tile_h, image = build(rows, [last], own, probes, half, [image])
        tiles = [
            (tile_a, 0, 0),
            (tile_b, own, 0),
            (tile_d, 0, 2 * own),
            (tile_e, 0, 4 * own),
            (tile_f, 3 * own, 0),
            (tile_g, 0, 6 * own),
            (tile_h, 0, 7 * own),
        ]

    with jax.named_scope("sum_over_rows"):
        parts = [image] + [swap(image, offset) for offset in ROWS[1:]]

    mine, other, rho = second_product(tiles, parts, own)

    with jax.named_scope("sum_over_columns"):
        mine = mine + swap_core(other)
        shares = [mine[:, :own]]
        for m, offset in enumerate(SQUARE[1:], 1):
            shares.append(swap(mine[:, m * own : (m + 1) * own], offset))

    with jax.named_scope("final_sums"):
        image, sums = local_sums(side, rho, shares)
        sums = jnp.broadcast_to(sums, (NY * NZ * NC, 8, LANES))
        sums = lax.all_to_all(sums, ("y", "z", "c"), 0, 0, tiled=True)

    field, residual = finish(side, rho, image, sums)
    return field.T, residual.T


def solution(mesh):
    fine = Mesh(mesh.devices.reshape(NY, NZ, NC, NX), ("y", "z", "c", "x"))
    rows = ("y", "z", "c")
    in_specs = (P(rows, None), P(rows), P(rows, "x"))
    out_specs = (P(rows, "x"), P(rows, "x"))
    return jax.shard_map(on_device, mesh=fine, in_specs=in_specs, out_specs=out_specs, check_vma=False)
```

```python
import functools

import jax
import jax.numpy as jnp
from jax import lax
from jax.experimental import pallas as pl
from jax.experimental.pallas import tpu as pltpu
from jax.sharding import Mesh
from jax.sharding import PartitionSpec as P

NY, NZ, NC, NX = 4, 4, 2, 4
LANES = 128
CHUNK = 256
HERE = (0, 0)
ROWS = (HERE, (3, 0), (0, 3), (3, 3))
SQUARE = (HERE, (1, 0), (0, 1), (1, 1))
COLS = ((0, 0), (1, 0), (0, 1), (0, 2), (1, 1), (1, 2), (0, 3), (1, 3))

noise_level = 1.0
kernel_rate = 0.5
STEP = 1.0 / (1.0 + noise_level)


def swap(value, offset):
    pairs = []
    for y in range(NY):
        for z in range(NZ):
            pairs.append((y * NZ + z, (y ^ offset[0]) * NZ + (z ^ offset[1])))
    return lax.ppermute(value, ("y", "z"), pairs)


def swap_each(values, offsets):
    received = [swap(value, offset) for value, offset in reversed(list(zip(values, offsets)))]
    return received[::-1]


def hand_on(along_y, along_z, step):
    value = jnp.where(lax.axis_index("c") == 0, along_z, along_y)
    pairs = []
    for y in range(NY):
        for z in range(NZ):
            here = (y * NZ + z) * NC
            pairs += [(here, ((y ^ step) * NZ + z) * NC), (here + 1, (y * NZ + (z ^ step)) * NC + 1)]
    return lax.ppermute(value, ("y", "z", "c"), pairs)


def swap_core(value):
    return lax.ppermute(value, "c", [(0, 1), (1, 0)])


def split(value):
    high = value.astype(jnp.bfloat16)
    rest = value - high.astype(jnp.float32)
    middle = rest.astype(jnp.bfloat16)
    return high, middle, (rest - middle.astype(jnp.float32)).astype(jnp.bfloat16)


def pack_kernel(points_ref, side_ref, out_ref):
    own, width = points_ref.shape
    probes = side_ref.shape[0]
    out_ref[:own, :] = points_ref[...]
    high, middle, _ = split(points_ref[...].astype(jnp.float32) ** 2)
    ones = jnp.ones((probes, width), jnp.bfloat16)
    norms = 0.0
    for term in (high, middle):
        norms = norms + lax.dot_general(ones, term, (((1,), (1,)), ((), ())), preferred_element_type=jnp.float32)
    high, middle, low = split(norms)
    row = lax.broadcasted_iota(jnp.int32, norms.shape, 0)
    norms = jnp.where(row == 0, high.astype(jnp.float32), jnp.where(row == 1, middle.astype(jnp.float32), low.astype(jnp.float32)))
    at = own
    for part in (side_ref[...].astype(jnp.bfloat16), norms.astype(jnp.bfloat16)):
        for j in range(own // width):
            out_ref[at : at + probes, :] = part[:, j * width : (j + 1) * width]
            at += probes


def pack(points, side):
    own, width = points.shape
    extra = side.shape[0] * 2 * own // width
    return pl.pallas_call(
        pack_kernel,
        out_shape=jax.ShapeDtypeStruct((own + extra, width), jnp.bfloat16),
        compiler_params=pltpu.CompilerParams(vmem_limit_bytes=8 << 20),
        name="pack",
    )(points, side)


def unpack_rows(message, probes, own, term):
    width = message.shape[1]
    count = own // width
    at = own + term * count * probes
    return jnp.concatenate([message[at + j * probes : at + (j + 1) * probes] for j in range(count)], axis=1)


def tile_kernel(counts, probes, *refs):
    rows_count, cols_count, known_halves, prior_count, has_side = counts
    refs = list(refs)
    row_refs = [refs.pop(0) for _ in range(rows_count)]
    col_refs = [refs.pop(0) for _ in range(cols_count)]
    half_refs = [refs.pop(0) for _ in range(known_halves)]
    prior_refs = [refs.pop(0) for _ in range(prior_count)]
    side_ref = refs.pop(0) if has_side else None
    tile_ref, image_ref = refs.pop(0), refs.pop(0)
    own = tile_ref.shape[0] // rows_count
    if known_halves:
        pieces = []
        for half_ref in half_refs:
            pieces += [half_ref[j * own : (j + 1) * own, :] for j in range(half_ref.shape[0] // own)]
        halves = pieces
    else:
        new_ref = refs.pop(0)
        halves = []
        for i, row_ref in enumerate(row_refs):
            squares = row_ref[:own, :].astype(jnp.float32) ** 2
            halves.append(-kernel_rate * jnp.sum(squares, axis=1, keepdims=True))
            new_ref[i * own : (i + 1) * own, :] = halves[-1]
    if prior_count:
        at = 0
        for prior_ref in prior_refs:
            image_ref[:, at : at + prior_ref.shape[1]] = prior_ref[...]
            at += prior_ref.shape[1]
    else:
        image_ref[...] = jnp.zeros_like(image_ref)
        if has_side:
            image_ref[:, :own] = (noise_level - 1.0 / STEP) * side_ref[...]
    for j, col_ref in enumerate(col_refs):
        field = unpack_rows(col_ref, probes, own, 0)
        norms = unpack_rows(col_ref, probes, own, 1).astype(jnp.float32)
        col_half = -kernel_rate * (norms[0:1] + norms[1:2] + norms[2:3])
        for i, row_ref in enumerate(row_refs):
            for k in range(own // CHUNK):
                part = slice(k * CHUNK, (k + 1) * CHUNK)
                place = slice(i * own + k * CHUNK, i * own + (k + 1) * CHUNK)
                cross = lax.dot_general(
                    row_ref[part, :], col_ref[:own, :], (((1,), (1,)), ((), ())), preferred_element_type=jnp.float32
                )
                kern = jnp.exp(2.0 * kernel_rate * cross + halves[i][part, :] + col_half).astype(jnp.bfloat16)
                tile_ref[place, j * own : (j + 1) * own] = kern
                image_ref[:, place] += lax.dot_general(
                    field, kern, (((1,), (1,)), ((), ())), preferred_element_type=jnp.float32
                )


def build(rows, cols, own, probes, halves=(), prior=(), side=None):
    features = rows[0].shape[1]
    height, width = len(rows) * own, len(cols) * own
    counts = (len(rows), len(cols), len(halves), len(prior), side is not None)
    out_shape = [
        pltpu.VMEM((height, width), jnp.bfloat16),
        jax.ShapeDtypeStruct((probes, height), jnp.float32),
    ]
    if not halves:
        out_shape.append(jax.ShapeDtypeStruct((height, 1), jnp.float32))
    args = [*rows, *cols, *halves, *prior] + ([] if side is None else [side])
    return pl.pallas_call(
        functools.partial(tile_kernel, counts, probes),
        out_shape=out_shape,
        compiler_params=pltpu.CompilerParams(vmem_limit_bytes=8 << 20),
        cost_estimate=pl.CostEstimate(
            flops=height * width * features // 8, bytes_accessed=1 << 10, transcendentals=0
        ),
        name="build_tile",
    )(*args)


def share_kernel(own, image_ref, *out_refs):
    probes = image_ref.shape[0]
    for k, out_ref in enumerate(out_refs, 1):
        for i in range(len(ROWS)):
            high, middle, _ = split(image_ref[:, i * own : (i + 1) * own])
            out_ref[i * probes : (i + 1) * probes, :] = high
            if i == k:
                out_ref[len(ROWS) * probes :, :] = middle


def share(image, own):
    probes = image.shape[0]
    height = (len(ROWS) + 1) * probes
    return pl.pallas_call(
        functools.partial(share_kernel, own),
        out_shape=[jax.ShapeDtypeStruct((height, own), jnp.bfloat16)] * (len(ROWS) - 1),
        compiler_params=pltpu.CompilerParams(vmem_limit_bytes=4 << 20),
        name="share",
    )(image)


def second_kernel(own, places, *refs):
    parts, refs = refs[: len(ROWS)], refs[len(ROWS) :]
    tiles, (mine_ref, other_ref, rho_ref) = refs[: len(places)], refs[len(places) :]
    probes = rho_ref.shape[0]
    pieces = []
    for p in ROWS:
        at = ROWS.index(p) * own
        piece = parts[0][:, at : at + own]
        for s, part in zip(ROWS[1:], parts[1:]):
            at = ROWS.index((p[0] ^ s[0], p[1] ^ s[1])) * probes
            piece = piece + part[at : at + probes, :].astype(jnp.float32)
            if p == HERE:
                piece = piece + part[len(ROWS) * probes :, :].astype(jnp.float32)
        pieces.append(-STEP * piece)
    rho_ref[...] = pieces[0]
    rho = jnp.concatenate(pieces, axis=1)
    high, low, _ = split(rho)
    narrow = jnp.concatenate([high, low], axis=0)
    for j, (h, m) in enumerate(COLS):
        part = 0.0
        for tile_ref, (top, left) in zip(tiles, places):
            at = j * own - left
            if 0 <= at < tile_ref.shape[1]:
                part = part + jnp.dot(
                    narrow[:, top : top + tile_ref.shape[0]],
                    tile_ref[:, at : at + own],
                    preferred_element_type=jnp.float32,
                )
        (other_ref if h else mine_ref)[:, m * own : (m + 1) * own] = part[:probes] + part[probes:]


def second_product(tiles, parts, own):
    probes, rows = parts[0].shape
    cols = len(COLS) * own
    places = [(top, left) for _, top, left in tiles]
    return pl.pallas_call(
        functools.partial(second_kernel, own, places),
        in_specs=[pl.BlockSpec(memory_space=pltpu.VMEM)] * (len(ROWS) + len(tiles)),
        out_shape=[
            jax.ShapeDtypeStruct((probes, cols // NC), jnp.float32),
            jax.ShapeDtypeStruct((probes, cols // NC), jnp.float32),
            jax.ShapeDtypeStruct((probes, own), jnp.float32),
        ],
        compiler_params=pltpu.CompilerParams(vmem_limit_bytes=8 << 20),
        cost_estimate=pl.CostEstimate(flops=rows * cols * 32, bytes_accessed=1 << 10, transcendentals=0),
        name="second_product",
    )(*parts, *[tile for tile, _, _ in tiles])


def sums_kernel(side_ref, rho_ref, *refs):
    shares, (image_ref, sums_ref) = refs[: len(SQUARE)], refs[len(SQUARE) :]
    side, rho = side_ref[...], rho_ref[...]
    image = noise_level * rho
    for share in shares:
        image = image + share[...]
    image_ref[...] = image
    total = lambda a, b: jnp.sum(a * b, axis=1, keepdims=True)
    lane = lax.broadcasted_iota(jnp.int32, (side.shape[0], LANES), 1)
    sums = 0.0
    for k, one in enumerate((total(side, side), total(side, rho), total(rho, rho), total(rho, image))):
        sums = jnp.where(lane == k, one, sums)
    sums_ref[...] = jnp.pad(sums.T[:8], ((0, 0), (0, LANES - side.shape[0])))


def local_sums(side, rho, shares):
    return pl.pallas_call(
        sums_kernel,
        out_shape=[
            jax.ShapeDtypeStruct(side.shape, jnp.float32),
            jax.ShapeDtypeStruct((8, LANES), jnp.float32),
        ],
        compiler_params=pltpu.CompilerParams(vmem_limit_bytes=4 << 20),
        name="local_sums",
    )(side, rho, *shares)


def finish_kernel(side_ref, rho_ref, image_ref, sums_ref, field_ref, residual_ref):
    side, rho, image = side_ref[...], rho_ref[...], image_ref[...]
    sums = jnp.sum(sums_ref[...], axis=0).T[: side.shape[0]]
    rr, side_rho, rho_rho, rho_image = (sums[:, k : k + 1] for k in range(4))
    curve = (rr - side_rho) / STEP
    alpha = rr / curve
    turn = alpha / STEP
    rest = 1.0 - turn
    rr_next = rest * rest * rr + 2.0 * rest * turn * side_rho + turn * turn * rho_rho
    gain = rest + rr_next / rr
    cross = (side_rho - rho_rho) / STEP
    curve = gain * gain * curve + 2.0 * gain * turn * cross + turn * turn * rho_image
    alpha_next = rr_next / curve
    direction = gain * side + turn * rho
    field_ref[...] = alpha * side + alpha_next * direction
    residual_ref[...] = rest * side + turn * rho - alpha_next * (gain / STEP * (side - rho) + turn * image)


def finish(side, rho, image, sums):
    return pl.pallas_call(
        finish_kernel,
        out_shape=[jax.ShapeDtypeStruct(side.shape, jnp.float32)] * 2,
        compiler_params=pltpu.CompilerParams(vmem_limit_bytes=4 << 20),
        name="finish",
    )(side, rho, image, sums)


def on_device(states, offsets, right_side):
    own, probes = right_side.shape
    side = right_side.T
    points = lax.dynamic_slice_in_dim(states, offsets[0], own, 0)
    with jax.named_scope("fetch_points"):
        message = pack(points, side)
        rows = [points] + [swap(points, offset) for offset in ROWS[1:3]]
        cols = [message] + [swap(message, offset) for offset in SQUARE[1:3]]
        first = [message, swap_core(message)]
        tile_a, image_a, half_a = build([points], first, own, probes, side=side)
        (rows[1], rows[2], cols[1], cols[2]), image_a = lax.optimization_barrier(
            ((rows[1], rows[2], cols[1], cols[2]), image_a)
        )
        rows.append(hand_on(rows[1], rows[2], 3))
        cols.append(hand_on(cols[1], cols[2], 1))
        others = [swap_core(cols[1]), swap_core(cols[2])]

    with jax.named_scope("build_tiles"):
        tile_b, image_b, half_b = build(rows[1:3], first, own, probes)
        half = [half_a, half_b]
        tile_d, image = build(rows[:3], cols[1:3], own, probes, half, [image_a, image_b])
        tile_e, image = build(rows[:3], others, own, probes, half, [image])
        rows[3], image = lax.optimization_barrier((rows[3], image))
        tile_f, image_far, half_far = build([rows[3]], first + cols[1:3] + others, own, probes)
        cols[3], image_far = lax.optimization_barrier((cols[3], image_far))
        last = swap_core(cols[3])
        half.append(half_far)
        tile_g, image = build(rows, [cols[3]], own, probes, half, [image, image_far])
        tile_h, image = build(rows, [last], own, probes, half, [image])
        tiles = [
            (tile_a, 0, 0),
            (tile_b, own, 0),
            (tile_d, 0, 2 * own),
            (tile_e, 0, 4 * own),
            (tile_f, 3 * own, 0),
            (tile_g, 0, 6 * own),
            (tile_h, 0, 7 * own),
        ]

    with jax.named_scope("sum_over_rows"):
        parts = [image] + swap_each(share(image, own), ROWS[1:])

    mine, other, rho = second_product(tiles, parts, own)

    with jax.named_scope("sum_over_columns"):
        mine = mine + swap_core(other)
        blocks = [mine[:, m * own : (m + 1) * own] for m in range(len(SQUARE))]
        shares = blocks[:1] + swap_each(blocks[1:], SQUARE[1:])

    with jax.named_scope("final_sums"):
        image, sums = local_sums(side, rho, shares)
        sums = jnp.broadcast_to(sums, (NY * NZ * NC, 8, LANES))
        sums = lax.all_to_all(sums, ("y", "z", "c"), 0, 0, tiled=True)

    field, residual = finish(side, rho, image, sums)
    return field.T, residual.T


def solution(mesh):
    fine = Mesh(mesh.devices.reshape(NY, NZ, NC, NX), ("y", "z", "c", "x"))
    rows = ("y", "z", "c")
    in_specs = (P(rows, None), P(rows), P(rows, "x"))
    out_specs = (P(rows, "x"), P(rows, "x"))
    return jax.shard_map(on_device, mesh=fine, in_specs=in_specs, out_specs=out_specs, check_vma=False)
```

```python
import functools

import jax
import jax.numpy as jnp
from jax import lax
from jax.experimental import pallas as pl
from jax.experimental.pallas import tpu as pltpu
from jax.sharding import Mesh
from jax.sharding import PartitionSpec as P

NY, NZ, NC, NX = 4, 4, 2, 4
LANES = 128
CHUNK = 256
HERE = (0, 0)
ROWS = (HERE, (1, 0), (0, 1), (1, 1))
SQUARE = (HERE, (3, 0), (0, 3), (3, 3))
COLS = ((0, 0), (1, 0), (0, 1), (0, 2), (1, 1), (1, 2), (0, 3), (1, 3))

noise_level = 1.0
kernel_rate = 0.5
STEP = 1.0 / (1.0 + noise_level)


def swap(value, offset):
    pairs = []
    for y in range(NY):
        for z in range(NZ):
            pairs.append((y * NZ + z, (y ^ offset[0]) * NZ + (z ^ offset[1])))
    return lax.ppermute(value, ("y", "z"), pairs)


def swap_each(values, offsets):
    received = [swap(value, offset) for value, offset in reversed(list(zip(values, offsets)))]
    return received[::-1]


def hand_on(along_y, along_z, step):
    value = jnp.where(lax.axis_index("c") == 0, along_z, along_y)
    pairs = []
    for y in range(NY):
        for z in range(NZ):
            here = (y * NZ + z) * NC
            pairs += [(here, ((y ^ step) * NZ + z) * NC), (here + 1, (y * NZ + (z ^ step)) * NC + 1)]
    return lax.ppermute(value, ("y", "z", "c"), pairs)


def swap_core(value):
    return lax.ppermute(value, "c", [(0, 1), (1, 0)])


def split(value):
    high = value.astype(jnp.bfloat16)
    rest = value - high.astype(jnp.float32)
    middle = rest.astype(jnp.bfloat16)
    return high, middle, (rest - middle.astype(jnp.float32)).astype(jnp.bfloat16)


def pack_kernel(points_ref, side_ref, out_ref):
    own, width = points_ref.shape
    probes = side_ref.shape[0]
    out_ref[:own, :] = points_ref[...]
    high, middle, _ = split(points_ref[...].astype(jnp.float32) ** 2)
    ones = jnp.ones((probes, width), jnp.bfloat16)
    norms = 0.0
    for term in (high, middle):
        norms = norms + lax.dot_general(ones, term, (((1,), (1,)), ((), ())), preferred_element_type=jnp.float32)
    high, middle, low = split(norms)
    row = lax.broadcasted_iota(jnp.int32, norms.shape, 0)
    norms = jnp.where(row == 0, high.astype(jnp.float32), jnp.where(row == 1, middle.astype(jnp.float32), low.astype(jnp.float32)))
    at = own
    for part in (side_ref[...].astype(jnp.bfloat16), norms.astype(jnp.bfloat16)):
        for j in range(own // width):
            out_ref[at : at + probes, :] = part[:, j * width : (j + 1) * width]
            at += probes


def pack(points, side):
    own, width = points.shape
    extra = side.shape[0] * 2 * own // width
    return pl.pallas_call(
        pack_kernel,
        out_shape=jax.ShapeDtypeStruct((own + extra, width), jnp.bfloat16),
        compiler_params=pltpu.CompilerParams(vmem_limit_bytes=8 << 20),
        name="pack",
    )(points, side)


def unpack_rows(message, probes, own, term):
    width = message.shape[1]
    count = own // width
    at = own + term * count * probes
    return jnp.concatenate([message[at + j * probes : at + (j + 1) * probes] for j in range(count)], axis=1)


def tile_kernel(counts, probes, *refs):
    rows_count, cols_count, known_halves, prior_count, has_side = counts
    refs = list(refs)
    row_refs = [refs.pop(0) for _ in range(rows_count)]
    col_refs = [refs.pop(0) for _ in range(cols_count)]
    half_refs = [refs.pop(0) for _ in range(known_halves)]
    prior_refs = [refs.pop(0) for _ in range(prior_count)]
    side_ref = refs.pop(0) if has_side else None
    tile_ref, image_ref = refs.pop(0), refs.pop(0)
    own = tile_ref.shape[0] // rows_count
    if known_halves:
        pieces = []
        for half_ref in half_refs:
            pieces += [half_ref[j * own : (j + 1) * own, :] for j in range(half_ref.shape[0] // own)]
        halves = pieces
    else:
        new_ref = refs.pop(0)
        halves = []
        for i, row_ref in enumerate(row_refs):
            squares = row_ref[:own, :].astype(jnp.float32) ** 2
            halves.append(-kernel_rate * jnp.sum(squares, axis=1, keepdims=True))
            new_ref[i * own : (i + 1) * own, :] = halves[-1]
    if prior_count:
        at = 0
        for prior_ref in prior_refs:
            image_ref[:, at : at + prior_ref.shape[1]] = prior_ref[...]
            at += prior_ref.shape[1]
    else:
        image_ref[...] = jnp.zeros_like(image_ref)
        if has_side:
            image_ref[:, :own] = (noise_level - 1.0 / STEP) * side_ref[...]
    for j, col_ref in enumerate(col_refs):
        field = unpack_rows(col_ref, probes, own, 0)
        norms = unpack_rows(col_ref, probes, own, 1).astype(jnp.float32)
        col_half = -kernel_rate * (norms[0:1] + norms[1:2] + norms[2:3])
        for i, row_ref in enumerate(row_refs):
            for k in range(own // CHUNK):
                part = slice(k * CHUNK, (k + 1) * CHUNK)
                place = slice(i * own + k * CHUNK, i * own + (k + 1) * CHUNK)
                cross = lax.dot_general(
                    row_ref[part, :], col_ref[:own, :], (((1,), (1,)), ((), ())), preferred_element_type=jnp.float32
                )
                kern = jnp.exp(2.0 * kernel_rate * cross + halves[i][part, :] + col_half).astype(jnp.bfloat16)
                tile_ref[place, j * own : (j + 1) * own] = kern
                image_ref[:, place] += lax.dot_general(
                    field, kern, (((1,), (1,)), ((), ())), preferred_element_type=jnp.float32
                )


def build(rows, cols, own, probes, halves=(), prior=(), side=None):
    features = rows[0].shape[1]
    height, width = len(rows) * own, len(cols) * own
    counts = (len(rows), len(cols), len(halves), len(prior), side is not None)
    out_shape = [
        pltpu.VMEM((height, width), jnp.bfloat16),
        jax.ShapeDtypeStruct((probes, height), jnp.float32),
    ]
    if not halves:
        out_shape.append(jax.ShapeDtypeStruct((height, 1), jnp.float32))
    args = [*rows, *cols, *halves, *prior] + ([] if side is None else [side])
    return pl.pallas_call(
        functools.partial(tile_kernel, counts, probes),
        out_shape=out_shape,
        compiler_params=pltpu.CompilerParams(vmem_limit_bytes=8 << 20),
        cost_estimate=pl.CostEstimate(
            flops=height * width * features // 8, bytes_accessed=1 << 10, transcendentals=0
        ),
        name="build_tile",
    )(*args)


def share_kernel(own, image_ref, *out_refs):
    probes = image_ref.shape[0]
    for k, out_ref in enumerate(out_refs, 1):
        for i in range(len(ROWS)):
            high, middle, _ = split(image_ref[:, i * own : (i + 1) * own])
            out_ref[i * probes : (i + 1) * probes, :] = high
            if i == k:
                out_ref[len(ROWS) * probes :, :] = middle


def share(image, own):
    probes = image.shape[0]
    height = (len(ROWS) + 1) * probes
    return pl.pallas_call(
        functools.partial(share_kernel, own),
        out_shape=[jax.ShapeDtypeStruct((height, own), jnp.bfloat16)] * (len(ROWS) - 1),
        compiler_params=pltpu.CompilerParams(vmem_limit_bytes=4 << 20),
        name="share",
    )(image)


def second_kernel(own, places, *refs):
    parts, refs = refs[: len(ROWS)], refs[len(ROWS) :]
    tiles, (mine_ref, other_ref, rho_ref) = refs[: len(places)], refs[len(places) :]
    probes = rho_ref.shape[0]
    pieces = []
    for p in ROWS:
        at = ROWS.index(p) * own
        piece = parts[0][:, at : at + own]
        for s, part in zip(ROWS[1:], parts[1:]):
            at = ROWS.index((p[0] ^ s[0], p[1] ^ s[1])) * probes
            piece = piece + part[at : at + probes, :].astype(jnp.float32)
            if p == HERE:
                piece = piece + part[len(ROWS) * probes :, :].astype(jnp.float32)
        pieces.append(-STEP * piece)
    rho_ref[...] = pieces[0]
    rho = jnp.concatenate(pieces, axis=1)
    high, low, _ = split(rho)
    narrow = jnp.concatenate([high, low], axis=0)
    for j, (h, m) in enumerate(COLS):
        part = 0.0
        for tile_ref, (top, left) in zip(tiles, places):
            at = j * own - left
            if 0 <= at < tile_ref.shape[1]:
                part = part + jnp.dot(
                    narrow[:, top : top + tile_ref.shape[0]],
                    tile_ref[:, at : at + own],
                    preferred_element_type=jnp.float32,
                )
        (other_ref if h else mine_ref)[:, m * own : (m + 1) * own] = part[:probes] + part[probes:]


def second_product(tiles, parts, own):
    probes, rows = parts[0].shape
    cols = len(COLS) * own
    places = [(top, left) for _, top, left in tiles]
    return pl.pallas_call(
        functools.partial(second_kernel, own, places),
        in_specs=[pl.BlockSpec(memory_space=pltpu.VMEM)] * (len(ROWS) + len(tiles)),
        out_shape=[
            jax.ShapeDtypeStruct((probes, cols // NC), jnp.float32),
            jax.ShapeDtypeStruct((probes, cols // NC), jnp.float32),
            jax.ShapeDtypeStruct((probes, own), jnp.float32),
        ],
        compiler_params=pltpu.CompilerParams(vmem_limit_bytes=8 << 20),
        cost_estimate=pl.CostEstimate(flops=rows * cols * 32, bytes_accessed=1 << 10, transcendentals=0),
        name="second_product",
    )(*parts, *[tile for tile, _, _ in tiles])


def sums_kernel(side_ref, rho_ref, *refs):
    shares, (image_ref, sums_ref) = refs[: len(SQUARE)], refs[len(SQUARE) :]
    side, rho = side_ref[...], rho_ref[...]
    image = noise_level * rho
    for share in shares:
        image = image + share[...]
    image_ref[...] = image
    total = lambda a, b: jnp.sum(a * b, axis=1, keepdims=True)
    lane = lax.broadcasted_iota(jnp.int32, (side.shape[0], LANES), 1)
    sums = 0.0
    for k, one in enumerate((total(side, side), total(side, rho), total(rho, rho), total(rho, image))):
        sums = jnp.where(lane == k, one, sums)
    sums_ref[...] = jnp.pad(sums.T[:8], ((0, 0), (0, LANES - side.shape[0])))


def local_sums(side, rho, shares):
    return pl.pallas_call(
        sums_kernel,
        out_shape=[
            jax.ShapeDtypeStruct(side.shape, jnp.float32),
            jax.ShapeDtypeStruct((8, LANES), jnp.float32),
        ],
        compiler_params=pltpu.CompilerParams(vmem_limit_bytes=4 << 20),
        name="local_sums",
    )(side, rho, *shares)


def finish_kernel(side_ref, rho_ref, image_ref, sums_ref, field_ref, residual_ref):
    side, rho, image = side_ref[...], rho_ref[...], image_ref[...]
    sums = jnp.sum(sums_ref[...], axis=0).T[: side.shape[0]]
    rr, side_rho, rho_rho, rho_image = (sums[:, k : k + 1] for k in range(4))
    curve = (rr - side_rho) / STEP
    alpha = rr / curve
    turn = alpha / STEP
    rest = 1.0 - turn
    rr_next = rest * rest * rr + 2.0 * rest * turn * side_rho + turn * turn * rho_rho
    gain = rest + rr_next / rr
    cross = (side_rho - rho_rho) / STEP
    curve = gain * gain * curve + 2.0 * gain * turn * cross + turn * turn * rho_image
    alpha_next = rr_next / curve
    direction = gain * side + turn * rho
    field_ref[...] = alpha * side + alpha_next * direction
    residual_ref[...] = rest * side + turn * rho - alpha_next * (gain / STEP * (side - rho) + turn * image)


def finish(side, rho, image, sums):
    return pl.pallas_call(
        finish_kernel,
        out_shape=[jax.ShapeDtypeStruct(side.shape, jnp.float32)] * 2,
        compiler_params=pltpu.CompilerParams(vmem_limit_bytes=4 << 20),
        name="finish",
    )(side, rho, image, sums)


def on_device(states, offsets, right_side):
    own, probes = right_side.shape
    side = right_side.T
    points = lax.dynamic_slice_in_dim(states, offsets[0], own, 0)
    with jax.named_scope("fetch_points"):
        message = pack(points, side)
        rows = [points] + [swap(points, offset) for offset in ROWS[1:3]]
        cols = [message] + [swap(message, offset) for offset in SQUARE[1:3]]
        first = [message, swap_core(message)]
        tile_a, image_a, half_a = build([points], first, own, probes, side=side)
        (rows[1], rows[2], cols[1], cols[2]), image_a = lax.optimization_barrier(
            ((rows[1], rows[2], cols[1], cols[2]), image_a)
        )
        rows.append(hand_on(rows[1], rows[2], 1))
        cols.append(hand_on(cols[1], cols[2], 3))
        others = [swap_core(cols[1]), swap_core(cols[2])]

    with jax.named_scope("build_tiles"):
        tile_b, image_b, half_b = build(rows[1:3], first, own, probes)
        half = [half_a, half_b]
        tile_d, image = build(rows[:3], cols[1:3], own, probes, half, [image_a, image_b])
        tile_e, image = build(rows[:3], others, own, probes, half, [image])
        rows[3], image = lax.optimization_barrier((rows[3], image))
        tile_f, image_far, half_far = build([rows[3]], first + cols[1:3] + others, own, probes)
        cols[3], image_far = lax.optimization_barrier((cols[3], image_far))
        last = swap_core(cols[3])
        half.append(half_far)
        tile_g, image = build(rows, [cols[3]], own, probes, half, [image, image_far])
        tile_h, image = build(rows, [last], own, probes, half, [image])
        tiles = [
            (tile_a, 0, 0),
            (tile_b, own, 0),
            (tile_d, 0, 2 * own),
            (tile_e, 0, 4 * own),
            (tile_f, 3 * own, 0),
            (tile_g, 0, 6 * own),
            (tile_h, 0, 7 * own),
        ]

    with jax.named_scope("sum_over_rows"):
        parts = [image] + swap_each(share(image, own), ROWS[1:])

    mine, other, rho = second_product(tiles, parts, own)

    with jax.named_scope("sum_over_columns"):
        mine = mine + swap_core(other)
        blocks = [mine[:, m * own : (m + 1) * own] for m in range(len(SQUARE))]
        shares = blocks[:1] + swap_each(blocks[1:], SQUARE[1:])

    with jax.named_scope("final_sums"):
        image, sums = local_sums(side, rho, shares)
        sums = jnp.broadcast_to(sums, (NY * NZ * NC, 8, LANES))
        sums = lax.all_to_all(sums, ("y", "z", "c"), 0, 0, tiled=True)

    field, residual = finish(side, rho, image, sums)
    return field.T, residual.T


def solution(mesh):
    fine = Mesh(mesh.devices.reshape(NY, NZ, NC, NX), ("y", "z", "c", "x"))
    rows = ("y", "z", "c")
    in_specs = (P(rows, None), P(rows), P(rows, "x"))
    out_specs = (P(rows, "x"), P(rows, "x"))
    return jax.shard_map(on_device, mesh=fine, in_specs=in_specs, out_specs=out_specs, check_vma=False)
```

```python
import functools

import jax
import jax.numpy as jnp
from jax import lax
from jax.experimental import pallas as pl
from jax.experimental.pallas import tpu as pltpu
from jax.sharding import Mesh
from jax.sharding import PartitionSpec as P

NY, NZ, NC, NX = 4, 4, 2, 4
LANES = 128
CHUNK = 256
HERE = (0, 0)
ROWS = (HERE, (1, 0), (0, 1), (1, 1))
SQUARE = (HERE, (3, 0), (0, 3), (3, 3))
COLS = ((0, 0), (1, 0), (0, 1), (0, 2), (1, 1), (1, 2), (0, 3), (1, 3))

noise_level = 1.0
kernel_rate = 0.5
STEP = 1.0 / (1.0 + noise_level)


def swap(value, offset):
    pairs = []
    for y in range(NY):
        for z in range(NZ):
            pairs.append((y * NZ + z, (y ^ offset[0]) * NZ + (z ^ offset[1])))
    return lax.ppermute(value, ("y", "z"), pairs)


def swap_each(values, offsets):
    received = [swap(value, offset) for value, offset in reversed(list(zip(values, offsets)))]
    return received[::-1]


def hand_on(along_y, along_z, step):
    value = jnp.where(lax.axis_index("c") == 0, along_z, along_y)
    pairs = []
    for y in range(NY):
        for z in range(NZ):
            here = (y * NZ + z) * NC
            pairs += [(here, ((y ^ step) * NZ + z) * NC), (here + 1, (y * NZ + (z ^ step)) * NC + 1)]
    return lax.ppermute(value, ("y", "z", "c"), pairs)


def swap_core(value):
    return lax.ppermute(value, "c", [(0, 1), (1, 0)])


def split(value):
    high = value.astype(jnp.bfloat16)
    rest = value - high.astype(jnp.float32)
    middle = rest.astype(jnp.bfloat16)
    return high, middle, (rest - middle.astype(jnp.float32)).astype(jnp.bfloat16)


def pack_kernel(points_ref, side_ref, out_ref):
    own, width = points_ref.shape
    probes = side_ref.shape[0]
    out_ref[:own, :] = points_ref[...]
    high, middle, _ = split(points_ref[...].astype(jnp.float32) ** 2)
    ones = jnp.ones((probes, width), jnp.bfloat16)
    norms = 0.0
    for term in (high, middle):
        norms = norms + lax.dot_general(ones, term, (((1,), (1,)), ((), ())), preferred_element_type=jnp.float32)
    high, middle, low = split(norms)
    row = lax.broadcasted_iota(jnp.int32, norms.shape, 0)
    norms = jnp.where(row == 0, high.astype(jnp.float32), jnp.where(row == 1, middle.astype(jnp.float32), low.astype(jnp.float32)))
    at = own
    for part in (side_ref[...], norms.astype(jnp.bfloat16)):
        for j in range(own // width):
            out_ref[at : at + probes, :] = part[:, j * width : (j + 1) * width]
            at += probes


def pack(points, side):
    own, width = points.shape
    extra = side.shape[0] * 2 * own // width
    return pl.pallas_call(
        pack_kernel,
        out_shape=jax.ShapeDtypeStruct((own + extra, width), jnp.bfloat16),
        compiler_params=pltpu.CompilerParams(vmem_limit_bytes=8 << 20),
        name="pack",
    )(points, side)


def unpack_rows(message, probes, own, term):
    width = message.shape[1]
    count = own // width
    at = own + term * count * probes
    return jnp.concatenate([message[at + j * probes : at + (j + 1) * probes] for j in range(count)], axis=1)


def tile_kernel(counts, probes, *refs):
    rows_count, cols_count, known_halves, prior_count, has_side = counts
    refs = list(refs)
    row_refs = [refs.pop(0) for _ in range(rows_count)]
    col_refs = [refs.pop(0) for _ in range(cols_count)]
    half_refs = [refs.pop(0) for _ in range(known_halves)]
    prior_refs = [refs.pop(0) for _ in range(prior_count)]
    side_ref = refs.pop(0) if has_side else None
    tile_ref, image_ref = refs.pop(0), refs.pop(0)
    own = tile_ref.shape[0] // rows_count
    if known_halves:
        pieces = []
        for half_ref in half_refs:
            pieces += [half_ref[j * own : (j + 1) * own, :] for j in range(half_ref.shape[0] // own)]
        halves = pieces
    else:
        new_ref = refs.pop(0)
        halves = []
        for i, row_ref in enumerate(row_refs):
            squares = row_ref[:own, :].astype(jnp.float32) ** 2
            halves.append(-kernel_rate * jnp.sum(squares, axis=1, keepdims=True))
            new_ref[i * own : (i + 1) * own, :] = halves[-1]
    if prior_count:
        at = 0
        for prior_ref in prior_refs:
            image_ref[:, at : at + prior_ref.shape[1]] = prior_ref[...]
            at += prior_ref.shape[1]
    else:
        image_ref[...] = jnp.zeros_like(image_ref)
        if has_side:
            image_ref[:, :own] = (noise_level - 1.0 / STEP) * side_ref[...]
    for j, col_ref in enumerate(col_refs):
        field = unpack_rows(col_ref, probes, own, 0)
        norms = unpack_rows(col_ref, probes, own, 1).astype(jnp.float32)
        col_half = -kernel_rate * (norms[0:1] + norms[1:2] + norms[2:3])
        for i, row_ref in enumerate(row_refs):
            for k in range(own // CHUNK):
                part = slice(k * CHUNK, (k + 1) * CHUNK)
                place = slice(i * own + k * CHUNK, i * own + (k + 1) * CHUNK)
                cross = lax.dot_general(
                    row_ref[part, :], col_ref[:own, :], (((1,), (1,)), ((), ())), preferred_element_type=jnp.float32
                )
                kern = jnp.exp(2.0 * kernel_rate * cross + halves[i][part, :] + col_half).astype(jnp.bfloat16)
                tile_ref[place, j * own : (j + 1) * own] = kern
                image_ref[:, place] += lax.dot_general(
                    field, kern, (((1,), (1,)), ((), ())), preferred_element_type=jnp.float32
                )


def build(rows, cols, own, probes, halves=(), prior=(), side=None):
    features = rows[0].shape[1]
    height, width = len(rows) * own, len(cols) * own
    counts = (len(rows), len(cols), len(halves), len(prior), side is not None)
    out_shape = [
        pltpu.VMEM((height, width), jnp.bfloat16),
        jax.ShapeDtypeStruct((probes, height), jnp.float32),
    ]
    if not halves:
        out_shape.append(jax.ShapeDtypeStruct((height, 1), jnp.float32))
    args = [*rows, *cols, *halves, *prior] + ([] if side is None else [side])
    return pl.pallas_call(
        functools.partial(tile_kernel, counts, probes),
        out_shape=out_shape,
        compiler_params=pltpu.CompilerParams(vmem_limit_bytes=8 << 20),
        cost_estimate=pl.CostEstimate(
            flops=height * width * features // 8, bytes_accessed=1 << 10, transcendentals=0
        ),
        name="build_tile",
    )(*args)


def share_kernel(own, image_ref, *out_refs):
    probes = image_ref.shape[0]
    for k, out_ref in enumerate(out_refs, 1):
        for i in range(len(ROWS)):
            high, middle, _ = split(image_ref[:, i * own : (i + 1) * own])
            out_ref[i * probes : (i + 1) * probes, :] = high
            if i == k:
                out_ref[len(ROWS) * probes :, :] = middle


def share(image, own):
    probes = image.shape[0]
    height = (len(ROWS) + 1) * probes
    return pl.pallas_call(
        functools.partial(share_kernel, own),
        out_shape=[jax.ShapeDtypeStruct((height, own), jnp.bfloat16)] * (len(ROWS) - 1),
        compiler_params=pltpu.CompilerParams(vmem_limit_bytes=4 << 20),
        name="share",
    )(image)


def rho_kernel(own, *refs):
    parts, (rho_ref, narrow_ref) = refs[: len(ROWS)], refs[len(ROWS) :]
    probes = rho_ref.shape[0]
    for j, p in enumerate(ROWS):
        at = j * own
        piece = parts[0][:, at : at + own]
        for s, part in zip(ROWS[1:], parts[1:]):
            at = ROWS.index((p[0] ^ s[0], p[1] ^ s[1])) * probes
            piece = piece + part[at : at + probes, :].astype(jnp.float32)
            if p == HERE:
                piece = piece + part[len(ROWS) * probes :, :].astype(jnp.float32)
        rho = -STEP * piece
        if p == HERE:
            rho_ref[...] = rho
        high, low, _ = split(rho)
        narrow_ref[:probes, j * own : (j + 1) * own] = high
        narrow_ref[probes:, j * own : (j + 1) * own] = low


def sum_rows(parts, own):
    probes, rows = parts[0].shape
    return pl.pallas_call(
        functools.partial(rho_kernel, own),
        out_shape=[
            jax.ShapeDtypeStruct((probes, own), jnp.float32),
            jax.ShapeDtypeStruct((2 * probes, rows), jnp.bfloat16),
        ],
        compiler_params=pltpu.CompilerParams(vmem_limit_bytes=4 << 20),
        name="sum_rows",
    )(*parts)


def second_kernel(own, half, places, narrow_ref, *refs):
    tiles, out_ref = refs[: len(places)], refs[len(places)]
    probes = out_ref.shape[0]
    for j, (h, m) in enumerate(COLS):
        if h != half:
            continue
        part = 0.0
        for tile_ref, (top, left) in zip(tiles, places):
            at = j * own - left
            if 0 <= at < tile_ref.shape[1]:
                part = part + jnp.dot(
                    narrow_ref[:, top : top + tile_ref.shape[0]],
                    tile_ref[:, at : at + own],
                    preferred_element_type=jnp.float32,
                )
        out_ref[:, m * own : (m + 1) * own] = part[:probes] + part[probes:]


def second_product(tiles, narrow, own, half):
    height, rows = narrow.shape
    cols = len(SQUARE) * own
    places = [(top, left) for _, top, left in tiles]
    return pl.pallas_call(
        functools.partial(second_kernel, own, half, places),
        in_specs=[pl.BlockSpec(memory_space=pltpu.VMEM)] * (1 + len(tiles)),
        out_shape=jax.ShapeDtypeStruct((height // 2, cols), jnp.float32),
        compiler_params=pltpu.CompilerParams(vmem_limit_bytes=8 << 20),
        cost_estimate=pl.CostEstimate(flops=rows * cols * 32, bytes_accessed=1 << 10, transcendentals=0),
        name="second_product",
    )(narrow, *[tile for tile, _, _ in tiles])


def merge_kernel(own, mine_ref, other_ref, *out_refs):
    for m, out_ref in enumerate(out_refs):
        here = slice(m * own, (m + 1) * own)
        out_ref[...] = mine_ref[:, here] + other_ref[:, here]


def merge(mine, other, own):
    return pl.pallas_call(
        functools.partial(merge_kernel, own),
        out_shape=[jax.ShapeDtypeStruct((mine.shape[0], own), jnp.float32)] * len(SQUARE),
        compiler_params=pltpu.CompilerParams(vmem_limit_bytes=4 << 20),
        name="merge",
    )(mine, other)


def sums_kernel(side_ref, rho_ref, *refs):
    shares, (image_ref, sums_ref) = refs[: len(SQUARE)], refs[len(SQUARE) :]
    side, rho = side_ref[...], rho_ref[...]
    image = noise_level * rho
    for share in shares:
        image = image + share[...]
    image_ref[...] = image
    total = lambda a, b: jnp.sum(a * b, axis=1, keepdims=True)
    lane = lax.broadcasted_iota(jnp.int32, (side.shape[0], LANES), 1)
    sums = 0.0
    for k, one in enumerate((total(side, side), total(side, rho), total(rho, rho), total(rho, image))):
        sums = jnp.where(lane == k, one, sums)
    sums_ref[...] = jnp.pad(sums.T[:8], ((0, 0), (0, LANES - side.shape[0])))


def local_sums(side, rho, shares):
    return pl.pallas_call(
        sums_kernel,
        out_shape=[
            jax.ShapeDtypeStruct(side.shape, jnp.float32),
            jax.ShapeDtypeStruct((8, LANES), jnp.float32),
        ],
        compiler_params=pltpu.CompilerParams(vmem_limit_bytes=4 << 20),
        name="local_sums",
    )(side, rho, *shares)


def finish_kernel(side_ref, rho_ref, image_ref, sums_ref, field_ref, residual_ref):
    side, rho, image = side_ref[...], rho_ref[...], image_ref[...]
    sums = jnp.sum(sums_ref[...], axis=0).T[: side.shape[0]]
    rr, side_rho, rho_rho, rho_image = (sums[:, k : k + 1] for k in range(4))
    curve = (rr - side_rho) / STEP
    alpha = rr / curve
    turn = alpha / STEP
    rest = 1.0 - turn
    rr_next = rest * rest * rr + 2.0 * rest * turn * side_rho + turn * turn * rho_rho
    gain = rest + rr_next / rr
    cross = (side_rho - rho_rho) / STEP
    curve = gain * gain * curve + 2.0 * gain * turn * cross + turn * turn * rho_image
    alpha_next = rr_next / curve
    direction = gain * side + turn * rho
    field_ref[...] = alpha * side + alpha_next * direction
    residual_ref[...] = rest * side + turn * rho - alpha_next * (gain / STEP * (side - rho) + turn * image)


def finish(side, rho, image, sums):
    return pl.pallas_call(
        finish_kernel,
        out_shape=[jax.ShapeDtypeStruct(side.shape, jnp.float32)] * 2,
        compiler_params=pltpu.CompilerParams(vmem_limit_bytes=4 << 20),
        name="finish",
    )(side, rho, image, sums)


def on_device(states, offsets, right_side):
    own, probes = right_side.shape
    side = right_side.T
    points = lax.dynamic_slice_in_dim(states, offsets[0], own, 0)
    with jax.named_scope("fetch_points"):
        message = pack(points, side.astype(jnp.bfloat16))
        rows = [points] + [swap(points, offset) for offset in ROWS[1:3]]
        cols = [message] + [swap(message, offset) for offset in SQUARE[1:3]]
        first = [message, swap_core(message)]
        tile_a, image_a, half_a = build([points], first, own, probes, side=side)
        (rows[1], rows[2], cols[1], cols[2]), image_a = lax.optimization_barrier(
            ((rows[1], rows[2], cols[1], cols[2]), image_a)
        )
        rows.append(hand_on(rows[1], rows[2], 1))
        cols.append(hand_on(cols[1], cols[2], 3))

    with jax.named_scope("build_tiles"):
        tile_b, image_b, half_b = build(rows[1:3], first, own, probes)
        half = [half_a, half_b]
        others = [swap_core(cols[1]), swap_core(cols[2])]
        tile_d, image = build(rows[:3], cols[1:3], own, probes, half, [image_a, image_b])
        tile_e, image = build(rows[:3], others, own, probes, half, [image])
        rows[3], image = lax.optimization_barrier((rows[3], image))
        tile_f, image_far, half_far = build([rows[3]], first + cols[1:3] + others, own, probes)
        cols[3], image_far = lax.optimization_barrier((cols[3], image_far))
        last = swap_core(cols[3])
        half.append(half_far)
        tile_g, image = build(rows, [cols[3]], own, probes, half, [image, image_far])
        tile_h, image = build(rows, [last], own, probes, half, [image])
        tiles = [
            (tile_a, 0, 0),
            (tile_b, own, 0),
            (tile_d, 0, 2 * own),
            (tile_e, 0, 4 * own),
            (tile_f, 3 * own, 0),
            (tile_g, 0, 6 * own),
            (tile_h, 0, 7 * own),
        ]

    with jax.named_scope("sum_over_rows"):
        parts = [image] + swap_each(share(image, own), ROWS[1:])

    rho, narrow = sum_rows(parts, own)
    other = second_product(tiles, narrow, own, 1)
    narrow, other = lax.optimization_barrier((narrow, other))
    mine = second_product(tiles, narrow, own, 0)

    with jax.named_scope("sum_over_columns"):
        blocks = merge(mine, swap_core(other), own)
        shares = [blocks[0]] + swap_each(blocks[1:], SQUARE[1:])

    with jax.named_scope("final_sums"):
        image, sums = local_sums(side, rho, shares)
        sums = jnp.broadcast_to(sums, (NY * NZ * NC, 8, LANES))
        sums = lax.all_to_all(sums, ("y", "z", "c"), 0, 0, tiled=True)

    field, residual = finish(side, rho, image, sums)
    return field.T, residual.T


def solution(mesh):
    fine = Mesh(mesh.devices.reshape(NY, NZ, NC, NX), ("y", "z", "c", "x"))
    rows = ("y", "z", "c")
    in_specs = (P(rows, None), P(rows), P(rows, "x"))
    out_specs = (P(rows, "x"), P(rows, "x"))
    return jax.shard_map(on_device, mesh=fine, in_specs=in_specs, out_specs=out_specs, check_vma=False)
```

```python
import functools

import jax
import jax.numpy as jnp
from jax import lax
from jax.experimental import pallas as pl
from jax.experimental.pallas import tpu as pltpu
from jax.sharding import Mesh
from jax.sharding import PartitionSpec as P

NY, NZ, NC, NX = 4, 4, 2, 4
LANES = 128
CHUNK = 256
HERE = (0, 0)
ROWS = (HERE, (1, 0), (0, 1), (1, 1))
SQUARE = (HERE, (3, 0), (0, 3), (3, 3))
COLS = ((0, 0), (1, 0), (0, 1), (0, 2), (1, 1), (1, 2), (0, 3), (1, 3))

noise_level = 1.0
kernel_rate = 0.5
STEP = 1.0 / (1.0 + noise_level)


def swap(value, offset):
    pairs = []
    for y in range(NY):
        for z in range(NZ):
            pairs.append((y * NZ + z, (y ^ offset[0]) * NZ + (z ^ offset[1])))
    return lax.ppermute(value, ("y", "z"), pairs)


def swap_each(values, offsets):
    received = [swap(value, offset) for value, offset in reversed(list(zip(values, offsets)))]
    return received[::-1]


def hand_on(along_y, along_z, offset):
    value = jnp.where(lax.axis_index("c") == 0, along_z, along_y)
    pairs = []
    for y in range(NY):
        for z in range(NZ):
            here = (y * NZ + z) * NC
            pairs += [(here, ((y ^ offset[0]) * NZ + z) * NC), (here + 1, (y * NZ + (z ^ offset[1])) * NC + 1)]
    return lax.ppermute(value, ("y", "z", "c"), pairs)


def swap_core(value):
    return lax.ppermute(value, "c", [(0, 1), (1, 0)])


def split(value):
    high = value.astype(jnp.bfloat16)
    rest = value - high.astype(jnp.float32)
    middle = rest.astype(jnp.bfloat16)
    return high, middle, (rest - middle.astype(jnp.float32)).astype(jnp.bfloat16)


def pack_kernel(points_ref, side_ref, out_ref):
    own, width = points_ref.shape
    probes = side_ref.shape[0]
    out_ref[:own, :] = points_ref[...]
    high, middle, _ = split(points_ref[...].astype(jnp.float32) ** 2)
    ones = jnp.ones((probes, width), jnp.bfloat16)
    norms = 0.0
    for term in (high, middle):
        norms = norms + lax.dot_general(ones, term, (((1,), (1,)), ((), ())), preferred_element_type=jnp.float32)
    high, middle, low = split(norms)
    row = lax.broadcasted_iota(jnp.int32, norms.shape, 0)
    norms = jnp.where(row == 0, high.astype(jnp.float32), jnp.where(row == 1, middle.astype(jnp.float32), low.astype(jnp.float32)))
    at = own
    for part in (side_ref[...], norms.astype(jnp.bfloat16)):
        for j in range(own // width):
            out_ref[at : at + probes, :] = part[:, j * width : (j + 1) * width]
            at += probes


def pack(points, side):
    own, width = points.shape
    extra = side.shape[0] * 2 * own // width
    return pl.pallas_call(
        pack_kernel,
        out_shape=jax.ShapeDtypeStruct((own + extra, width), jnp.bfloat16),
        compiler_params=pltpu.CompilerParams(vmem_limit_bytes=8 << 20),
        name="pack",
    )(points, side)


def unpack_rows(message, probes, own, term):
    width = message.shape[1]
    count = own // width
    at = own + term * count * probes
    return jnp.concatenate([message[at + j * probes : at + (j + 1) * probes] for j in range(count)], axis=1)


def tile_kernel(counts, probes, *refs):
    rows_count, cols_count, known_halves, prior_count, has_side = counts
    refs = list(refs)
    row_refs = [refs.pop(0) for _ in range(rows_count)]
    col_refs = [refs.pop(0) for _ in range(cols_count)]
    half_refs = [refs.pop(0) for _ in range(known_halves)]
    prior_refs = [refs.pop(0) for _ in range(prior_count)]
    side_ref = refs.pop(0) if has_side else None
    tile_ref, image_ref = refs.pop(0), refs.pop(0)
    own = tile_ref.shape[0] // rows_count
    if known_halves:
        pieces = []
        for half_ref in half_refs:
            pieces += [half_ref[j * own : (j + 1) * own, :] for j in range(half_ref.shape[0] // own)]
        halves = pieces
    else:
        new_ref = refs.pop(0)
        halves = []
        for i, row_ref in enumerate(row_refs):
            squares = row_ref[:own, :].astype(jnp.float32) ** 2
            halves.append(-kernel_rate * jnp.sum(squares, axis=1, keepdims=True))
            new_ref[i * own : (i + 1) * own, :] = halves[-1]
    if prior_count:
        at = 0
        for prior_ref in prior_refs:
            image_ref[:, at : at + prior_ref.shape[1]] = prior_ref[...]
            at += prior_ref.shape[1]
    else:
        image_ref[...] = jnp.zeros_like(image_ref)
        if has_side:
            image_ref[:, :own] = (noise_level - 1.0 / STEP) * side_ref[...]
    for j, col_ref in enumerate(col_refs):
        field = unpack_rows(col_ref, probes, own, 0)
        norms = unpack_rows(col_ref, probes, own, 1).astype(jnp.float32)
        col_half = -kernel_rate * (norms[0:1] + norms[1:2] + norms[2:3])
        for i, row_ref in enumerate(row_refs):
            for k in range(own // CHUNK):
                part = slice(k * CHUNK, (k + 1) * CHUNK)
                place = slice(i * own + k * CHUNK, i * own + (k + 1) * CHUNK)
                cross = lax.dot_general(
                    row_ref[part, :], col_ref[:own, :], (((1,), (1,)), ((), ())), preferred_element_type=jnp.float32
                )
                kern = jnp.exp(2.0 * kernel_rate * cross + halves[i][part, :] + col_half).astype(jnp.bfloat16)
                tile_ref[place, j * own : (j + 1) * own] = kern
                image_ref[:, place] += lax.dot_general(
                    field, kern, (((1,), (1,)), ((), ())), preferred_element_type=jnp.float32
                )


def build(rows, cols, own, probes, halves=(), prior=(), side=None):
    features = rows[0].shape[1]
    height, width = len(rows) * own, len(cols) * own
    counts = (len(rows), len(cols), len(halves), len(prior), side is not None)
    out_shape = [
        pltpu.VMEM((height, width), jnp.bfloat16),
        jax.ShapeDtypeStruct((probes, height), jnp.float32),
    ]
    if not halves:
        out_shape.append(jax.ShapeDtypeStruct((height, 1), jnp.float32))
    args = [*rows, *cols, *halves, *prior] + ([] if side is None else [side])
    return pl.pallas_call(
        functools.partial(tile_kernel, counts, probes),
        out_shape=out_shape,
        compiler_params=pltpu.CompilerParams(vmem_limit_bytes=8 << 20),
        cost_estimate=pl.CostEstimate(
            flops=height * width * features // 8, bytes_accessed=1 << 10, transcendentals=0
        ),
        name="build_tile",
    )(*args)


def share_kernel(own, image_ref, *out_refs):
    probes = image_ref.shape[0]
    for k, out_ref in enumerate(out_refs, 1):
        for i in range(len(ROWS)):
            high, middle, _ = split(image_ref[:, i * own : (i + 1) * own])
            out_ref[i * probes : (i + 1) * probes, :] = high
            if i == k:
                out_ref[len(ROWS) * probes :, :] = middle


def share(image, own):
    probes = image.shape[0]
    height = (len(ROWS) + 1) * probes
    return pl.pallas_call(
        functools.partial(share_kernel, own),
        out_shape=[jax.ShapeDtypeStruct((height, own), jnp.bfloat16)] * (len(ROWS) - 1),
        compiler_params=pltpu.CompilerParams(vmem_limit_bytes=4 << 20),
        name="share",
    )(image)


def rho_kernel(own, *refs):
    parts, (rho_ref, narrow_ref) = refs[: len(ROWS)], refs[len(ROWS) :]
    probes = rho_ref.shape[0]
    for j, p in enumerate(ROWS):
        at = j * own
        piece = parts[0][:, at : at + own]
        for s, part in zip(ROWS[1:], parts[1:]):
            at = ROWS.index((p[0] ^ s[0], p[1] ^ s[1])) * probes
            piece = piece + part[at : at + probes, :].astype(jnp.float32)
            if p == HERE:
                piece = piece + part[len(ROWS) * probes :, :].astype(jnp.float32)
        rho = -STEP * piece
        if p == HERE:
            rho_ref[...] = rho
        high, low, _ = split(rho)
        narrow_ref[:probes, j * own : (j + 1) * own] = high
        narrow_ref[probes:, j * own : (j + 1) * own] = low


def sum_rows(parts, own):
    probes, rows = parts[0].shape
    return pl.pallas_call(
        functools.partial(rho_kernel, own),
        out_shape=[
            jax.ShapeDtypeStruct((probes, own), jnp.float32),
            jax.ShapeDtypeStruct((2 * probes, rows), jnp.bfloat16),
        ],
        compiler_params=pltpu.CompilerParams(vmem_limit_bytes=4 << 20),
        name="sum_rows",
    )(*parts)


def second_kernel(own, half, places, narrow_ref, *refs):
    tiles, out_ref = refs[: len(places)], refs[len(places)]
    probes = out_ref.shape[0]
    for j, (h, m) in enumerate(COLS):
        if h != half:
            continue
        part = 0.0
        for tile_ref, (top, left) in zip(tiles, places):
            at = j * own - left
            if 0 <= at < tile_ref.shape[1]:
                part = part + jnp.dot(
                    narrow_ref[:, top : top + tile_ref.shape[0]],
                    tile_ref[:, at : at + own],
                    preferred_element_type=jnp.float32,
                )
        out_ref[:, m * own : (m + 1) * own] = part[:probes] + part[probes:]


def second_product(tiles, narrow, own, half):
    height, rows = narrow.shape
    cols = len(SQUARE) * own
    places = [(top, left) for _, top, left in tiles]
    return pl.pallas_call(
        functools.partial(second_kernel, own, half, places),
        in_specs=[pl.BlockSpec(memory_space=pltpu.VMEM)] * (1 + len(tiles)),
        out_shape=jax.ShapeDtypeStruct((height // 2, cols), jnp.float32),
        compiler_params=pltpu.CompilerParams(vmem_limit_bytes=8 << 20),
        cost_estimate=pl.CostEstimate(flops=rows * cols * 32, bytes_accessed=1 << 10, transcendentals=0),
        name="second_product",
    )(narrow, *[tile for tile, _, _ in tiles])


def merge_kernel(own, mine_ref, other_ref, *out_refs):
    for m, out_ref in enumerate(out_refs):
        here = slice(m * own, (m + 1) * own)
        out_ref[...] = mine_ref[:, here] + other_ref[:, here]


def merge(mine, other, own):
    return pl.pallas_call(
        functools.partial(merge_kernel, own),
        out_shape=[jax.ShapeDtypeStruct((mine.shape[0], own), jnp.float32)] * len(SQUARE),
        compiler_params=pltpu.CompilerParams(vmem_limit_bytes=4 << 20),
        name="merge",
    )(mine, other)


def sums_kernel(side_ref, rho_ref, *refs):
    shares, (image_ref, sums_ref) = refs[: len(SQUARE)], refs[len(SQUARE) :]
    side, rho = side_ref[...], rho_ref[...]
    image = noise_level * rho
    for share in shares:
        image = image + share[...]
    image_ref[...] = image
    total = lambda a, b: jnp.sum(a * b, axis=1, keepdims=True)
    lane = lax.broadcasted_iota(jnp.int32, (side.shape[0], LANES), 1)
    sums = 0.0
    for k, one in enumerate((total(side, side), total(side, rho), total(rho, rho), total(rho, image))):
        sums = jnp.where(lane == k, one, sums)
    sums = sums.T
    sums_ref[...] = jnp.concatenate([sums[k : k + 1] for k in range(LANES // sums.shape[1])], axis=1)


def local_sums(side, rho, shares):
    return pl.pallas_call(
        sums_kernel,
        out_shape=[
            jax.ShapeDtypeStruct(side.shape, jnp.float32),
            jax.ShapeDtypeStruct((1, LANES), jnp.float32),
        ],
        compiler_params=pltpu.CompilerParams(vmem_limit_bytes=4 << 20),
        name="local_sums",
    )(side, rho, *shares)


def finish_kernel(side_ref, rho_ref, image_ref, sums_ref, field_ref, residual_ref):
    side, rho, image = side_ref[...], rho_ref[...], image_ref[...]
    probes = side.shape[0]
    sums = jnp.sum(sums_ref[...], axis=0, keepdims=True)
    sums = jnp.concatenate([sums[:, k * probes : (k + 1) * probes] for k in range(4)] * 2, axis=0).T
    rr, side_rho, rho_rho, rho_image = (sums[:, k : k + 1] for k in range(4))
    curve = (rr - side_rho) / STEP
    alpha = rr / curve
    turn = alpha / STEP
    rest = 1.0 - turn
    rr_next = rest * rest * rr + 2.0 * rest * turn * side_rho + turn * turn * rho_rho
    gain = rest + rr_next / rr
    cross = (side_rho - rho_rho) / STEP
    curve = gain * gain * curve + 2.0 * gain * turn * cross + turn * turn * rho_image
    alpha_next = rr_next / curve
    direction = gain * side + turn * rho
    field_ref[...] = alpha * side + alpha_next * direction
    residual_ref[...] = rest * side + turn * rho - alpha_next * (gain / STEP * (side - rho) + turn * image)


def finish(side, rho, image, sums):
    return pl.pallas_call(
        finish_kernel,
        out_shape=[jax.ShapeDtypeStruct(side.shape, jnp.float32)] * 2,
        compiler_params=pltpu.CompilerParams(vmem_limit_bytes=4 << 20),
        name="finish",
    )(side, rho, image, sums)


def on_device(states, offsets, right_side):
    own, probes = right_side.shape
    side = right_side.T
    points = lax.dynamic_slice_in_dim(states, offsets[0], own, 0)
    with jax.named_scope("fetch_points"):
        message = pack(points, side.astype(jnp.bfloat16))
        rows = [points] + [swap(points, offset) for offset in ROWS[1:3]]
        cols = [message] + [swap(message, offset) for offset in SQUARE[1:3]]
        first = [message, swap_core(message)]
        tile_a, image_a, half_a = build([points], first, own, probes, side=side)
        tile_b, image_b, half_b = build(rows[1:3], first, own, probes)
        (rows[1], rows[2], cols[1], cols[2]), image_a, image_b = lax.optimization_barrier(
            ((rows[1], rows[2], cols[1], cols[2]), image_a, image_b)
        )
        cols.append(hand_on(cols[1], cols[2], SQUARE[3]))
        rows.append(hand_on(rows[1], rows[2], ROWS[3]))

    with jax.named_scope("build_tiles"):
        half = [half_a, half_b]
        others = [swap_core(cols[1]), swap_core(cols[2])]
        tile_d, image = build(rows[:3], cols[1:3], own, probes, half, [image_a, image_b])
        tile_e, image = build(rows[:3], others, own, probes, half, [image])
        rows[3], image = lax.optimization_barrier((rows[3], image))
        tile_f, image_far, half_far = build([rows[3]], first + cols[1:3] + others, own, probes)
        cols[3], image_far = lax.optimization_barrier((cols[3], image_far))
        last = swap_core(cols[3])
        half.append(half_far)
        tile_g, image = build(rows, [cols[3]], own, probes, half, [image, image_far])
        tile_h, image = build(rows, [last], own, probes, half, [image])
        tiles = [
            (tile_a, 0, 0),
            (tile_b, own, 0),
            (tile_d, 0, 2 * own),
            (tile_e, 0, 4 * own),
            (tile_f, 3 * own, 0),
            (tile_g, 0, 6 * own),
            (tile_h, 0, 7 * own),
        ]

    with jax.named_scope("sum_over_rows"):
        parts = [image] + swap_each(share(image, own), ROWS[1:])

    rho, narrow = sum_rows(parts, own)
    other = second_product(tiles, narrow, own, 1)
    narrow, other = lax.optimization_barrier((narrow, other))
    mine = second_product(tiles, narrow, own, 0)

    with jax.named_scope("sum_over_columns"):
        blocks = merge(mine, swap_core(other), own)
        shares = [blocks[0]] + swap_each(blocks[1:], SQUARE[1:])

    with jax.named_scope("final_sums"):
        image, sums = local_sums(side, rho, shares)
        sums = jnp.broadcast_to(sums, (NY * NZ * NC, LANES))
        sums = lax.all_to_all(sums, ("y", "z", "c"), 0, 0, tiled=True)

    field, residual = finish(side, rho, image, sums)
    return field.T, residual.T


def solution(mesh):
    fine = Mesh(mesh.devices.reshape(NY, NZ, NC, NX), ("y", "z", "c", "x"))
    rows = ("y", "z", "c")
    in_specs = (P(rows, None), P(rows), P(rows, "x"))
    out_specs = (P(rows, "x"), P(rows, "x"))
    return jax.shard_map(on_device, mesh=fine, in_specs=in_specs, out_specs=out_specs, check_vma=False)
```

```python
import functools

import jax
import jax.numpy as jnp
from jax import lax
from jax.experimental import pallas as pl
from jax.experimental.pallas import tpu as pltpu
from jax.sharding import Mesh
from jax.sharding import PartitionSpec as P

NY, NZ, NC, NX = 4, 4, 2, 4
LANES = 128
CHUNK = 256
HERE = (0, 0)
ROWS = (HERE, (1, 0), (0, 1), (1, 1))
SQUARE = (HERE, (3, 0), (0, 3), (3, 3))
COLS = ((0, 0), (1, 0), (0, 1), (0, 2), (1, 1), (1, 2), (0, 3), (1, 3))

noise_level = 1.0
kernel_rate = 0.5
STEP = 1.0 / (1.0 + noise_level)


def swap(value, offset):
    pairs = []
    for y in range(NY):
        for z in range(NZ):
            pairs.append((y * NZ + z, (y ^ offset[0]) * NZ + (z ^ offset[1])))
    return lax.ppermute(value, ("y", "z"), pairs)


def swap_each(values, offsets):
    received = [swap(value, offset) for value, offset in reversed(list(zip(values, offsets)))]
    return received[::-1]


def hand_on(along_y, along_z, offset):
    value = jnp.where(lax.axis_index("c") == 0, along_z, along_y)
    pairs = []
    for y in range(NY):
        for z in range(NZ):
            here = (y * NZ + z) * NC
            pairs += [(here, ((y ^ offset[0]) * NZ + z) * NC), (here + 1, (y * NZ + (z ^ offset[1])) * NC + 1)]
    return lax.ppermute(value, ("y", "z", "c"), pairs)


def swap_core(value):
    return lax.ppermute(value, "c", [(0, 1), (1, 0)])


def split(value):
    high = value.astype(jnp.bfloat16)
    rest = value - high.astype(jnp.float32)
    middle = rest.astype(jnp.bfloat16)
    return high, middle, (rest - middle.astype(jnp.float32)).astype(jnp.bfloat16)


def pack_kernel(points_ref, side_ref, out_ref):
    own, width = points_ref.shape
    probes = side_ref.shape[0]
    out_ref[:own, :] = points_ref[...]
    high, middle, _ = split(points_ref[...].astype(jnp.float32) ** 2)
    ones = jnp.ones((probes, width), jnp.bfloat16)
    norms = 0.0
    for term in (high, middle):
        norms = norms + lax.dot_general(ones, term, (((1,), (1,)), ((), ())), preferred_element_type=jnp.float32)
    high, middle, low = split(norms)
    row = lax.broadcasted_iota(jnp.int32, norms.shape, 0)
    norms = jnp.where(row == 0, high.astype(jnp.float32), jnp.where(row == 1, middle.astype(jnp.float32), low.astype(jnp.float32)))
    at = own
    for part in (side_ref[...], norms.astype(jnp.bfloat16)):
        for j in range(own // width):
            out_ref[at : at + probes, :] = part[:, j * width : (j + 1) * width]
            at += probes


def pack(points, side):
    own, width = points.shape
    extra = side.shape[0] * 2 * own // width
    return pl.pallas_call(
        pack_kernel,
        out_shape=jax.ShapeDtypeStruct((own + extra, width), jnp.bfloat16),
        compiler_params=pltpu.CompilerParams(vmem_limit_bytes=8 << 20),
        name="pack",
    )(points, side)


def unpack_rows(message, probes, own, term):
    width = message.shape[1]
    count = own // width
    at = own + term * count * probes
    return jnp.concatenate([message[at + j * probes : at + (j + 1) * probes] for j in range(count)], axis=1)


def tile_kernel(counts, probes, *refs):
    rows_count, cols_count, known_halves, prior_count, has_side = counts
    refs = list(refs)
    row_refs = [refs.pop(0) for _ in range(rows_count)]
    col_refs = [refs.pop(0) for _ in range(cols_count)]
    half_refs = [refs.pop(0) for _ in range(known_halves)]
    prior_refs = [refs.pop(0) for _ in range(prior_count)]
    side_ref = refs.pop(0) if has_side else None
    tile_ref, image_ref = refs.pop(0), refs.pop(0)
    own = tile_ref.shape[0] // rows_count
    if known_halves:
        pieces = []
        for half_ref in half_refs:
            pieces += [half_ref[j * own : (j + 1) * own, :] for j in range(half_ref.shape[0] // own)]
        halves = pieces
    else:
        new_ref = refs.pop(0)
        halves = []
        for i, row_ref in enumerate(row_refs):
            squares = row_ref[:own, :].astype(jnp.float32) ** 2
            halves.append(-kernel_rate * jnp.sum(squares, axis=1, keepdims=True))
            new_ref[i * own : (i + 1) * own, :] = halves[-1]
    if prior_count:
        at = 0
        for prior_ref in prior_refs:
            image_ref[:, at : at + prior_ref.shape[1]] = prior_ref[...]
            at += prior_ref.shape[1]
    else:
        image_ref[...] = jnp.zeros_like(image_ref)
        if has_side:
            image_ref[:, :own] = (noise_level - 1.0 / STEP) * side_ref[...]
    for j, col_ref in enumerate(col_refs):
        field = unpack_rows(col_ref, probes, own, 0)
        norms = unpack_rows(col_ref, probes, own, 1).astype(jnp.float32)
        col_half = -kernel_rate * (norms[0:1] + norms[1:2] + norms[2:3])
        for i, row_ref in enumerate(row_refs):
            for k in range(own // CHUNK):
                part = slice(k * CHUNK, (k + 1) * CHUNK)
                place = slice(i * own + k * CHUNK, i * own + (k + 1) * CHUNK)
                cross = lax.dot_general(
                    row_ref[part, :], col_ref[:own, :], (((1,), (1,)), ((), ())), preferred_element_type=jnp.float32
                )
                kern = jnp.exp(2.0 * kernel_rate * cross + halves[i][part, :] + col_half).astype(jnp.bfloat16)
                tile_ref[place, j * own : (j + 1) * own] = kern
                image_ref[:, place] += lax.dot_general(
                    field, kern, (((1,), (1,)), ((), ())), preferred_element_type=jnp.float32
                )


def build(rows, cols, own, probes, halves=(), prior=(), side=None):
    features = rows[0].shape[1]
    height, width = len(rows) * own, len(cols) * own
    counts = (len(rows), len(cols), len(halves), len(prior), side is not None)
    out_shape = [
        pltpu.VMEM((height, width), jnp.bfloat16),
        jax.ShapeDtypeStruct((probes, height), jnp.float32),
    ]
    if not halves:
        out_shape.append(jax.ShapeDtypeStruct((height, 1), jnp.float32))
    args = [*rows, *cols, *halves, *prior] + ([] if side is None else [side])
    return pl.pallas_call(
        functools.partial(tile_kernel, counts, probes),
        out_shape=out_shape,
        compiler_params=pltpu.CompilerParams(vmem_limit_bytes=8 << 20),
        cost_estimate=pl.CostEstimate(
            flops=height * width * features // 8, bytes_accessed=1 << 10, transcendentals=0
        ),
        name="build_tile",
    )(*args)


def share_kernel(own, image_ref, *out_refs):
    probes = image_ref.shape[0]
    for k, out_ref in enumerate(out_refs, 1):
        for i in range(len(ROWS)):
            high, middle, _ = split(image_ref[:, i * own : (i + 1) * own])
            out_ref[i * probes : (i + 1) * probes, :] = high
            if i == k:
                out_ref[len(ROWS) * probes :, :] = middle


def share(image, own):
    probes = image.shape[0]
    height = (len(ROWS) + 1) * probes
    return pl.pallas_call(
        functools.partial(share_kernel, own),
        out_shape=[jax.ShapeDtypeStruct((height, own), jnp.bfloat16)] * (len(ROWS) - 1),
        compiler_params=pltpu.CompilerParams(vmem_limit_bytes=4 << 20),
        name="share",
    )(image)


def rho_kernel(own, *refs):
    parts, (rho_ref, narrow_ref) = refs[: len(ROWS)], refs[len(ROWS) :]
    probes = rho_ref.shape[0]
    for j, p in enumerate(ROWS):
        at = j * own
        piece = parts[0][:, at : at + own]
        for s, part in zip(ROWS[1:], parts[1:]):
            at = ROWS.index((p[0] ^ s[0], p[1] ^ s[1])) * probes
            piece = piece + part[at : at + probes, :].astype(jnp.float32)
            if p == HERE:
                piece = piece + part[len(ROWS) * probes :, :].astype(jnp.float32)
        rho = -STEP * piece
        if p == HERE:
            rho_ref[...] = rho
        high, low, _ = split(rho)
        narrow_ref[:probes, j * own : (j + 1) * own] = high
        narrow_ref[probes:, j * own : (j + 1) * own] = low


def sum_rows(parts, own):
    probes, rows = parts[0].shape
    return pl.pallas_call(
        functools.partial(rho_kernel, own),
        out_shape=[
            jax.ShapeDtypeStruct((probes, own), jnp.float32),
            jax.ShapeDtypeStruct((2 * probes, rows), jnp.bfloat16),
        ],
        compiler_params=pltpu.CompilerParams(vmem_limit_bytes=4 << 20),
        name="sum_rows",
    )(*parts)


def second_kernel(own, half, places, narrow_ref, *refs):
    tiles, out_ref = refs[: len(places)], refs[len(places)]
    probes = out_ref.shape[0]
    for j, (h, m) in enumerate(COLS):
        if h != half:
            continue
        part = 0.0
        for tile_ref, (top, left) in zip(tiles, places):
            at = j * own - left
            if 0 <= at < tile_ref.shape[1]:
                part = part + jnp.dot(
                    narrow_ref[:, top : top + tile_ref.shape[0]],
                    tile_ref[:, at : at + own],
                    preferred_element_type=jnp.float32,
                )
        out_ref[:, m * own : (m + 1) * own] = part[:probes] + part[probes:]


def second_product(tiles, narrow, own, half):
    height, rows = narrow.shape
    cols = len(SQUARE) * own
    places = [(top, left) for _, top, left in tiles]
    return pl.pallas_call(
        functools.partial(second_kernel, own, half, places),
        in_specs=[pl.BlockSpec(memory_space=pltpu.VMEM)] * (1 + len(tiles)),
        out_shape=jax.ShapeDtypeStruct((height // 2, cols), jnp.float32),
        compiler_params=pltpu.CompilerParams(vmem_limit_bytes=8 << 20),
        cost_estimate=pl.CostEstimate(flops=rows * cols * 32, bytes_accessed=1 << 10, transcendentals=0),
        name="second_product",
    )(narrow, *[tile for tile, _, _ in tiles])


def merge_kernel(own, mine_ref, other_ref, *out_refs):
    for m, out_ref in enumerate(out_refs):
        here = slice(m * own, (m + 1) * own)
        out_ref[...] = mine_ref[:, here] + other_ref[:, here]


def merge(mine, other, own):
    return pl.pallas_call(
        functools.partial(merge_kernel, own),
        out_shape=[jax.ShapeDtypeStruct((mine.shape[0], own), jnp.float32)] * len(SQUARE),
        compiler_params=pltpu.CompilerParams(vmem_limit_bytes=4 << 20),
        name="merge",
    )(mine, other)


def sums_kernel(side_ref, rho_ref, *refs):
    shares, (image_ref, sums_ref) = refs[: len(SQUARE)], refs[len(SQUARE) :]
    side, rho = side_ref[...], rho_ref[...]
    image = noise_level * rho
    for share in shares:
        image = image + share[...]
    image_ref[...] = image
    total = lambda a, b: jnp.sum(a * b, axis=1, keepdims=True)
    lane = lax.broadcasted_iota(jnp.int32, (side.shape[0], LANES), 1)
    sums = 0.0
    for k, one in enumerate((total(side, side), total(side, rho), total(rho, rho), total(rho, image))):
        sums = jnp.where(lane == k, one, sums)
    sums = sums.T
    sums_ref[...] = jnp.concatenate([sums[k : k + 1] for k in range(LANES // sums.shape[1])], axis=1)


def local_sums(side, rho, shares):
    return pl.pallas_call(
        sums_kernel,
        out_shape=[
            jax.ShapeDtypeStruct(side.shape, jnp.float32),
            jax.ShapeDtypeStruct((1, LANES), jnp.float32),
        ],
        compiler_params=pltpu.CompilerParams(vmem_limit_bytes=4 << 20),
        name="local_sums",
    )(side, rho, *shares)


def finish_kernel(side_ref, rho_ref, image_ref, sums_ref, field_ref, residual_ref):
    side, rho, image = side_ref[...], rho_ref[...], image_ref[...]
    probes = side.shape[0]
    sums = jnp.sum(sums_ref[...], axis=0, keepdims=True)
    sums = jnp.concatenate([sums[:, k * probes : (k + 1) * probes] for k in range(4)] * 2, axis=0).T
    rr, side_rho, rho_rho, rho_image = (sums[:, k : k + 1] for k in range(4))
    curve = (rr - side_rho) / STEP
    alpha = rr / curve
    turn = alpha / STEP
    rest = 1.0 - turn
    rr_next = rest * rest * rr + 2.0 * rest * turn * side_rho + turn * turn * rho_rho
    gain = rest + rr_next / rr
    cross = (side_rho - rho_rho) / STEP
    curve = gain * gain * curve + 2.0 * gain * turn * cross + turn * turn * rho_image
    alpha_next = rr_next / curve
    direction = gain * side + turn * rho
    field_ref[...] = alpha * side + alpha_next * direction
    residual_ref[...] = rest * side + turn * rho - alpha_next * (gain / STEP * (side - rho) + turn * image)


def finish(side, rho, image, sums):
    return pl.pallas_call(
        finish_kernel,
        out_shape=[jax.ShapeDtypeStruct(side.shape, jnp.float32)] * 2,
        compiler_params=pltpu.CompilerParams(vmem_limit_bytes=4 << 20),
        name="finish",
    )(side, rho, image, sums)


def on_device(states, offsets, right_side):
    own, probes = right_side.shape
    side = right_side.T
    points = lax.dynamic_slice_in_dim(states, offsets[0], own, 0)
    with jax.named_scope("fetch_points"):
        message = pack(points, side.astype(jnp.bfloat16))
        rows = [points] + [swap(points, offset) for offset in ROWS[1:3]]
        cols = [message] + [swap(message, offset) for offset in SQUARE[1:3]]
        first = [message, swap_core(message)]
        tile_a, image_a, half_a = build([points], first, own, probes, side=side)
        tile_b, image_b, half_b = build(rows[1:3], first, own, probes)
        (rows[1], rows[2], cols[1], cols[2]), image_a, image_b = lax.optimization_barrier(
            ((rows[1], rows[2], cols[1], cols[2]), image_a, image_b)
        )
        cols.append(hand_on(cols[1], cols[2], SQUARE[3]))
        rows.append(hand_on(rows[1], rows[2], ROWS[3]))

    with jax.named_scope("build_tiles"):
        half = [half_a, half_b]
        tile_d, image = build(rows[:3], cols[1:3], own, probes, half, [image_a, image_b])
        (near_y, near_z), image = lax.optimization_barrier(((cols[1], cols[2]), image))
        others = [swap_core(near_y), swap_core(near_z)]
        tile_e, image = build(rows[:3], others, own, probes, half, [image])
        rows[3], image = lax.optimization_barrier((rows[3], image))
        tile_f, image_far, half_far = build([rows[3]], first + cols[1:3] + others, own, probes)
        cols[3], image_far = lax.optimization_barrier((cols[3], image_far))
        last = swap_core(cols[3])
        half.append(half_far)
        tile_g, image = build(rows, [cols[3]], own, probes, half, [image, image_far])
        tile_h, image = build(rows, [last], own, probes, half, [image])
        tiles = [
            (tile_a, 0, 0),
            (tile_b, own, 0),
            (tile_d, 0, 2 * own),
            (tile_e, 0, 4 * own),
            (tile_f, 3 * own, 0),
            (tile_g, 0, 6 * own),
            (tile_h, 0, 7 * own),
        ]

    with jax.named_scope("sum_over_rows"):
        parts = [image] + swap_each(share(image, own), ROWS[1:])

    rho, narrow = sum_rows(parts, own)
    other = second_product(tiles, narrow, own, 1)
    narrow, other = lax.optimization_barrier((narrow, other))
    mine = second_product(tiles, narrow, own, 0)

    with jax.named_scope("sum_over_columns"):
        blocks = merge(mine, swap_core(other), own)
        shares = [blocks[0]] + swap_each(blocks[1:], SQUARE[1:])

    with jax.named_scope("final_sums"):
        image, sums = local_sums(side, rho, shares)
        sums = jnp.broadcast_to(sums, (NY * NZ * NC, LANES))
        sums = lax.all_to_all(sums, ("y", "z", "c"), 0, 0, tiled=True)

    field, residual = finish(side, rho, image, sums)
    return field.T, residual.T


def solution(mesh):
    fine = Mesh(mesh.devices.reshape(NY, NZ, NC, NX), ("y", "z", "c", "x"))
    rows = ("y", "z", "c")
    in_specs = (P(rows, None), P(rows), P(rows, "x"))
    out_specs = (P(rows, "x"), P(rows, "x"))
    return jax.shard_map(on_device, mesh=fine, in_specs=in_specs, out_specs=out_specs, check_vma=False)
```

```python
import functools

import jax
import jax.numpy as jnp
from jax import lax
from jax.experimental import pallas as pl
from jax.experimental.pallas import tpu as pltpu
from jax.sharding import Mesh
from jax.sharding import PartitionSpec as P

NY, NZ, NC, NX = 4, 4, 2, 4
LANES = 128
CHUNK = 256
HERE = (0, 0)
ROWS = (HERE, (1, 0), (0, 3), (1, 3))
SQUARE = (HERE, (3, 0), (0, 1), (3, 1))
COLS = ((0, 0), (1, 0), (0, 1), (0, 2), (1, 1), (1, 2), (0, 3), (1, 3))

noise_level = 1.0
kernel_rate = 0.5
STEP = 1.0 / (1.0 + noise_level)


def swap(value, offset):
    pairs = []
    for y in range(NY):
        for z in range(NZ):
            pairs.append((y * NZ + z, (y ^ offset[0]) * NZ + (z ^ offset[1])))
    return lax.ppermute(value, ("y", "z"), pairs)


def swap_each(values, offsets):
    received = [swap(value, offset) for value, offset in reversed(list(zip(values, offsets)))]
    return received[::-1]


def hand_on(along_y, along_z, offset):
    value = jnp.where(lax.axis_index("c") == 0, along_z, along_y)
    pairs = []
    for y in range(NY):
        for z in range(NZ):
            here = (y * NZ + z) * NC
            pairs += [(here, ((y ^ offset[0]) * NZ + z) * NC), (here + 1, (y * NZ + (z ^ offset[1])) * NC + 1)]
    return lax.ppermute(value, ("y", "z", "c"), pairs)


def swap_core(value):
    return lax.ppermute(value, "c", [(0, 1), (1, 0)])


def split(value):
    high = value.astype(jnp.bfloat16)
    rest = value - high.astype(jnp.float32)
    middle = rest.astype(jnp.bfloat16)
    return high, middle, (rest - middle.astype(jnp.float32)).astype(jnp.bfloat16)


def pack_kernel(points_ref, side_ref, out_ref):
    own, width = points_ref.shape
    probes = side_ref.shape[0]
    out_ref[:own, :] = points_ref[...]
    high, middle, _ = split(points_ref[...].astype(jnp.float32) ** 2)
    ones = jnp.ones((probes, width), jnp.bfloat16)
    norms = 0.0
    for term in (high, middle):
        norms = norms + lax.dot_general(ones, term, (((1,), (1,)), ((), ())), preferred_element_type=jnp.float32)
    high, middle, low = split(norms)
    row = lax.broadcasted_iota(jnp.int32, norms.shape, 0)
    norms = jnp.where(row == 0, high.astype(jnp.float32), jnp.where(row == 1, middle.astype(jnp.float32), low.astype(jnp.float32)))
    at = own
    for part in (side_ref[...], norms.astype(jnp.bfloat16)):
        for j in range(own // width):
            out_ref[at : at + probes, :] = part[:, j * width : (j + 1) * width]
            at += probes


def pack(points, side):
    own, width = points.shape
    extra = side.shape[0] * 2 * own // width
    return pl.pallas_call(
        pack_kernel,
        out_shape=jax.ShapeDtypeStruct((own + extra, width), jnp.bfloat16),
        compiler_params=pltpu.CompilerParams(vmem_limit_bytes=8 << 20),
        name="pack",
    )(points, side)


def unpack_rows(message, probes, own, term):
    width = message.shape[1]
    count = own // width
    at = own + term * count * probes
    return jnp.concatenate([message[at + j * probes : at + (j + 1) * probes] for j in range(count)], axis=1)


def tile_kernel(counts, probes, *refs):
    rows_count, cols_count, known_halves, prior_count, has_side = counts
    refs = list(refs)
    row_refs = [refs.pop(0) for _ in range(rows_count)]
    col_refs = [refs.pop(0) for _ in range(cols_count)]
    half_refs = [refs.pop(0) for _ in range(known_halves)]
    prior_refs = [refs.pop(0) for _ in range(prior_count)]
    side_ref = refs.pop(0) if has_side else None
    tile_ref, image_ref = refs.pop(0), refs.pop(0)
    own = tile_ref.shape[0] // rows_count
    if known_halves:
        pieces = []
        for half_ref in half_refs:
            pieces += [half_ref[j * own : (j + 1) * own, :] for j in range(half_ref.shape[0] // own)]
        halves = pieces
    else:
        new_ref = refs.pop(0)
        halves = []
        for i, row_ref in enumerate(row_refs):
            squares = row_ref[:own, :].astype(jnp.float32) ** 2
            halves.append(-kernel_rate * jnp.sum(squares, axis=1, keepdims=True))
            new_ref[i * own : (i + 1) * own, :] = halves[-1]
    if prior_count:
        at = 0
        for prior_ref in prior_refs:
            image_ref[:, at : at + prior_ref.shape[1]] = prior_ref[...]
            at += prior_ref.shape[1]
    else:
        image_ref[...] = jnp.zeros_like(image_ref)
        if has_side:
            image_ref[:, :own] = (noise_level - 1.0 / STEP) * side_ref[...]
    for j, col_ref in enumerate(col_refs):
        field = unpack_rows(col_ref, probes, own, 0)
        norms = unpack_rows(col_ref, probes, own, 1).astype(jnp.float32)
        col_half = -kernel_rate * (norms[0:1] + norms[1:2] + norms[2:3])
        for i, row_ref in enumerate(row_refs):
            for k in range(own // CHUNK):
                part = slice(k * CHUNK, (k + 1) * CHUNK)
                place = slice(i * own + k * CHUNK, i * own + (k + 1) * CHUNK)
                cross = lax.dot_general(
                    row_ref[part, :], col_ref[:own, :], (((1,), (1,)), ((), ())), preferred_element_type=jnp.float32
                )
                kern = jnp.exp(2.0 * kernel_rate * cross + halves[i][part, :] + col_half).astype(jnp.bfloat16)
                tile_ref[place, j * own : (j + 1) * own] = kern
                image_ref[:, place] += lax.dot_general(
                    field, kern, (((1,), (1,)), ((), ())), preferred_element_type=jnp.float32
                )


def build(rows, cols, own, probes, halves=(), prior=(), side=None):
    features = rows[0].shape[1]
    height, width = len(rows) * own, len(cols) * own
    counts = (len(rows), len(cols), len(halves), len(prior), side is not None)
    out_shape = [
        pltpu.VMEM((height, width), jnp.bfloat16),
        jax.ShapeDtypeStruct((probes, height), jnp.float32),
    ]
    if not halves:
        out_shape.append(jax.ShapeDtypeStruct((height, 1), jnp.float32))
    args = [*rows, *cols, *halves, *prior] + ([] if side is None else [side])
    return pl.pallas_call(
        functools.partial(tile_kernel, counts, probes),
        out_shape=out_shape,
        compiler_params=pltpu.CompilerParams(vmem_limit_bytes=8 << 20),
        cost_estimate=pl.CostEstimate(
            flops=height * width * features // 8, bytes_accessed=1 << 10, transcendentals=0
        ),
        name="build_tile",
    )(*args)


def share_kernel(own, image_ref, *out_refs):
    probes = image_ref.shape[0]
    for k, out_ref in enumerate(out_refs, 1):
        for i in range(len(ROWS)):
            high, middle, _ = split(image_ref[:, i * own : (i + 1) * own])
            out_ref[i * probes : (i + 1) * probes, :] = high
            if i == k:
                out_ref[len(ROWS) * probes :, :] = middle


def share(image, own):
    probes = image.shape[0]
    height = (len(ROWS) + 1) * probes
    return pl.pallas_call(
        functools.partial(share_kernel, own),
        out_shape=[jax.ShapeDtypeStruct((height, own), jnp.bfloat16)] * (len(ROWS) - 1),
        compiler_params=pltpu.CompilerParams(vmem_limit_bytes=4 << 20),
        name="share",
    )(image)


def rho_kernel(own, *refs):
    parts, (rho_ref, narrow_ref) = refs[: len(ROWS)], refs[len(ROWS) :]
    probes = rho_ref.shape[0]
    for j, p in enumerate(ROWS):
        at = j * own
        piece = parts[0][:, at : at + own]
        for s, part in zip(ROWS[1:], parts[1:]):
            at = ROWS.index((p[0] ^ s[0], p[1] ^ s[1])) * probes
            piece = piece + part[at : at + probes, :].astype(jnp.float32)
            if p == HERE:
                piece = piece + part[len(ROWS) * probes :, :].astype(jnp.float32)
        rho = -STEP * piece
        if p == HERE:
            rho_ref[...] = rho
        high, low, _ = split(rho)
        narrow_ref[:probes, j * own : (j + 1) * own] = high
        narrow_ref[probes:, j * own : (j + 1) * own] = low


def sum_rows(parts, own):
    probes, rows = parts[0].shape
    return pl.pallas_call(
        functools.partial(rho_kernel, own),
        out_shape=[
            jax.ShapeDtypeStruct((probes, own), jnp.float32),
            jax.ShapeDtypeStruct((2 * probes, rows), jnp.bfloat16),
        ],
        compiler_params=pltpu.CompilerParams(vmem_limit_bytes=4 << 20),
        name="sum_rows",
    )(*parts)


def second_kernel(own, half, places, narrow_ref, *refs):
    tiles, out_ref = refs[: len(places)], refs[len(places)]
    probes = out_ref.shape[0]
    for j, (h, m) in enumerate(COLS):
        if h != half:
            continue
        part = 0.0
        for tile_ref, (top, left) in zip(tiles, places):
            at = j * own - left
            if 0 <= at < tile_ref.shape[1]:
                part = part + jnp.dot(
                    narrow_ref[:, top : top + tile_ref.shape[0]],
                    tile_ref[:, at : at + own],
                    preferred_element_type=jnp.float32,
                )
        out_ref[:, m * own : (m + 1) * own] = part[:probes] + part[probes:]


def second_product(tiles, narrow, own, half):
    height, rows = narrow.shape
    cols = len(SQUARE) * own
    places = [(top, left) for _, top, left in tiles]
    return pl.pallas_call(
        functools.partial(second_kernel, own, half, places),
        in_specs=[pl.BlockSpec(memory_space=pltpu.VMEM)] * (1 + len(tiles)),
        out_shape=jax.ShapeDtypeStruct((height // 2, cols), jnp.float32),
        compiler_params=pltpu.CompilerParams(vmem_limit_bytes=8 << 20),
        cost_estimate=pl.CostEstimate(flops=rows * cols * 32, bytes_accessed=1 << 10, transcendentals=0),
        name="second_product",
    )(narrow, *[tile for tile, _, _ in tiles])


def merge_kernel(own, mine_ref, other_ref, *out_refs):
    for m, out_ref in enumerate(out_refs):
        here = slice(m * own, (m + 1) * own)
        out_ref[...] = mine_ref[:, here] + other_ref[:, here]


def merge(mine, other, own):
    return pl.pallas_call(
        functools.partial(merge_kernel, own),
        out_shape=[jax.ShapeDtypeStruct((mine.shape[0], own), jnp.float32)] * len(SQUARE),
        compiler_params=pltpu.CompilerParams(vmem_limit_bytes=4 << 20),
        name="merge",
    )(mine, other)


def sums_kernel(side_ref, rho_ref, *refs):
    shares, (image_ref, sums_ref) = refs[: len(SQUARE)], refs[len(SQUARE) :]
    side, rho = side_ref[...], rho_ref[...]
    image = noise_level * rho
    for share in shares:
        image = image + share[...]
    image_ref[...] = image
    total = lambda a, b: jnp.sum(a * b, axis=1, keepdims=True)
    lane = lax.broadcasted_iota(jnp.int32, (side.shape[0], LANES), 1)
    sums = 0.0
    for k, one in enumerate((total(side, side), total(side, rho), total(rho, rho), total(rho, image))):
        sums = jnp.where(lane == k, one, sums)
    sums = sums.T
    sums_ref[...] = jnp.concatenate([sums[k : k + 1] for k in range(LANES // sums.shape[1])], axis=1)


def local_sums(side, rho, shares):
    return pl.pallas_call(
        sums_kernel,
        out_shape=[
            jax.ShapeDtypeStruct(side.shape, jnp.float32),
            jax.ShapeDtypeStruct((1, LANES), jnp.float32),
        ],
        compiler_params=pltpu.CompilerParams(vmem_limit_bytes=4 << 20),
        name="local_sums",
    )(side, rho, *shares)


def finish_kernel(side_ref, rho_ref, image_ref, sums_ref, field_ref, residual_ref):
    side, rho, image = side_ref[...], rho_ref[...], image_ref[...]
    probes = side.shape[0]
    sums = jnp.sum(sums_ref[...], axis=0, keepdims=True)
    sums = jnp.concatenate([sums[:, k * probes : (k + 1) * probes] for k in range(4)] * 2, axis=0).T
    rr, side_rho, rho_rho, rho_image = (sums[:, k : k + 1] for k in range(4))
    curve = (rr - side_rho) / STEP
    alpha = rr / curve
    turn = alpha / STEP
    rest = 1.0 - turn
    rr_next = rest * rest * rr + 2.0 * rest * turn * side_rho + turn * turn * rho_rho
    gain = rest + rr_next / rr
    cross = (side_rho - rho_rho) / STEP
    curve = gain * gain * curve + 2.0 * gain * turn * cross + turn * turn * rho_image
    alpha_next = rr_next / curve
    direction = gain * side + turn * rho
    field_ref[...] = alpha * side + alpha_next * direction
    residual_ref[...] = rest * side + turn * rho - alpha_next * (gain / STEP * (side - rho) + turn * image)


def finish(side, rho, image, sums):
    return pl.pallas_call(
        finish_kernel,
        out_shape=[jax.ShapeDtypeStruct(side.shape, jnp.float32)] * 2,
        compiler_params=pltpu.CompilerParams(vmem_limit_bytes=4 << 20),
        name="finish",
    )(side, rho, image, sums)


def on_device(states, offsets, right_side):
    own, probes = right_side.shape
    side = right_side.T
    points = lax.dynamic_slice_in_dim(states, offsets[0], own, 0)
    with jax.named_scope("fetch_points"):
        message = pack(points, side.astype(jnp.bfloat16))
        rows = [points] + [swap(points, offset) for offset in ROWS[1:3]]
        cols = [message] + [swap(message, offset) for offset in SQUARE[1:3]]
        first = [message, swap_core(message)]
        tile_a, image_a, half_a = build([points], first, own, probes, side=side)
        tile_b, image_b, half_b = build(rows[1:3], first, own, probes)
        (rows[1], rows[2], cols[1], cols[2]), image_a, image_b = lax.optimization_barrier(
            ((rows[1], rows[2], cols[1], cols[2]), image_a, image_b)
        )
        cols.append(hand_on(cols[1], cols[2], SQUARE[3]))
        rows.append(hand_on(rows[1], rows[2], ROWS[3]))

    with jax.named_scope("build_tiles"):
        half = [half_a, half_b]
        others = [swap_core(cols[1]), swap_core(cols[2])]
        tile_d, image = build(rows[:3], cols[1:3], own, probes, half, [image_a, image_b])
        tile_e, image = build(rows[:3], others, own, probes, half, [image])
        rows[3], image = lax.optimization_barrier((rows[3], image))
        tile_f, image_far, half_far = build([rows[3]], first + cols[1:3] + others, own, probes)
        cols[3], image_far = lax.optimization_barrier((cols[3], image_far))
        last = swap_core(cols[3])
        half.append(half_far)
        tile_g, image = build(rows, [cols[3]], own, probes, half, [image, image_far])
        tile_h, image = build(rows, [last], own, probes, half, [image])
        tiles = [
            (tile_a, 0, 0),
            (tile_b, own, 0),
            (tile_d, 0, 2 * own),
            (tile_e, 0, 4 * own),
            (tile_f, 3 * own, 0),
            (tile_g, 0, 6 * own),
            (tile_h, 0, 7 * own),
        ]

    with jax.named_scope("sum_over_rows"):
        parts = [image] + swap_each(share(image, own), ROWS[1:])

    rho, narrow = sum_rows(parts, own)
    other = second_product(tiles, narrow, own, 1)
    narrow, other = lax.optimization_barrier((narrow, other))
    mine = second_product(tiles, narrow, own, 0)

    with jax.named_scope("sum_over_columns"):
        blocks = merge(mine, swap_core(other), own)
        shares = [blocks[0]] + swap_each(blocks[1:], SQUARE[1:])

    with jax.named_scope("final_sums"):
        image, sums = local_sums(side, rho, shares)
        sums = jnp.broadcast_to(sums, (NY * NZ * NC, LANES))
        sums = lax.all_to_all(sums, ("y", "z", "c"), 0, 0, tiled=True)

    field, residual = finish(side, rho, image, sums)
    return field.T, residual.T


def solution(mesh):
    fine = Mesh(mesh.devices.reshape(NY, NZ, NC, NX), ("y", "z", "c", "x"))
    rows = ("y", "z", "c")
    in_specs = (P(rows, None), P(rows), P(rows, "x"))
    out_specs = (P(rows, "x"), P(rows, "x"))
    return jax.shard_map(on_device, mesh=fine, in_specs=in_specs, out_specs=out_specs, check_vma=False)
```

```python
import functools

import jax
import jax.numpy as jnp
from jax import lax
from jax.experimental import pallas as pl
from jax.experimental.pallas import tpu as pltpu
from jax.sharding import Mesh
from jax.sharding import PartitionSpec as P

NY, NZ, NC, NX = 4, 4, 2, 4
LANES = 128
CHUNK = 256
HERE = (0, 0)
ROWS = (HERE, (1, 0), (0, 1), (1, 1))
SQUARE = (HERE, (3, 0), (0, 3), (3, 3))
COLS = ((0, 0), (1, 0), (0, 1), (0, 2), (1, 1), (1, 2), (0, 3), (1, 3))

noise_level = 1.0
kernel_rate = 0.5
STEP = 1.0 / (1.0 + noise_level)


def swap(value, offset):
    pairs = []
    for y in range(NY):
        for z in range(NZ):
            pairs.append((y * NZ + z, (y ^ offset[0]) * NZ + (z ^ offset[1])))
    return lax.ppermute(value, ("y", "z"), pairs)


def swap_each(values, offsets):
    received = [swap(value, offset) for value, offset in reversed(list(zip(values, offsets)))]
    return received[::-1]


def hand_on(along_y, along_z, offset):
    value = jnp.where(lax.axis_index("c") == 0, along_z, along_y)
    pairs = []
    for y in range(NY):
        for z in range(NZ):
            here = (y * NZ + z) * NC
            pairs += [(here, ((y ^ offset[0]) * NZ + z) * NC), (here + 1, (y * NZ + (z ^ offset[1])) * NC + 1)]
    return lax.ppermute(value, ("y", "z", "c"), pairs)


def swap_core(value):
    return lax.ppermute(value, "c", [(0, 1), (1, 0)])


def split(value):
    high = value.astype(jnp.bfloat16)
    rest = value - high.astype(jnp.float32)
    middle = rest.astype(jnp.bfloat16)
    return high, middle, (rest - middle.astype(jnp.float32)).astype(jnp.bfloat16)


def pack_kernel(points_ref, side_ref, out_ref):
    own, width = points_ref.shape
    probes = side_ref.shape[0]
    out_ref[:own, :] = points_ref[...]
    high, middle, _ = split(points_ref[...].astype(jnp.float32) ** 2)
    ones = jnp.ones((probes, width), jnp.bfloat16)
    norms = 0.0
    for term in (high, middle):
        norms = norms + lax.dot_general(ones, term, (((1,), (1,)), ((), ())), preferred_element_type=jnp.float32)
    high, middle, low = split(norms)
    row = lax.broadcasted_iota(jnp.int32, norms.shape, 0)
    norms = jnp.where(row == 0, high.astype(jnp.float32), jnp.where(row == 1, middle.astype(jnp.float32), low.astype(jnp.float32)))
    at = own
    for part in (side_ref[...], norms.astype(jnp.bfloat16)):
        for j in range(own // width):
            out_ref[at : at + probes, :] = part[:, j * width : (j + 1) * width]
            at += probes


def pack(points, side):
    own, width = points.shape
    extra = side.shape[0] * 2 * own // width
    return pl.pallas_call(
        pack_kernel,
        out_shape=jax.ShapeDtypeStruct((own + extra, width), jnp.bfloat16),
        compiler_params=pltpu.CompilerParams(vmem_limit_bytes=8 << 20),
        name="pack",
    )(points, side)


def unpack_rows(message, probes, own, term):
    width = message.shape[1]
    count = own // width
    at = own + term * count * probes
    return jnp.concatenate([message[at + j * probes : at + (j + 1) * probes] for j in range(count)], axis=1)


def tile_kernel(counts, probes, *refs):
    rows_count, cols_count, known_halves, prior_count, has_side = counts
    refs = list(refs)
    row_refs = [refs.pop(0) for _ in range(rows_count)]
    col_refs = [refs.pop(0) for _ in range(cols_count)]
    half_refs = [refs.pop(0) for _ in range(known_halves)]
    prior_refs = [refs.pop(0) for _ in range(prior_count)]
    side_ref = refs.pop(0) if has_side else None
    tile_ref, image_ref = refs.pop(0), refs.pop(0)
    own = tile_ref.shape[0] // rows_count
    if known_halves:
        pieces = []
        for half_ref in half_refs:
            pieces += [half_ref[j * own : (j + 1) * own, :] for j in range(half_ref.shape[0] // own)]
        halves = pieces
    else:
        new_ref = refs.pop(0)
        halves = []
        for i, row_ref in enumerate(row_refs):
            squares = row_ref[:own, :].astype(jnp.float32) ** 2
            halves.append(-kernel_rate * jnp.sum(squares, axis=1, keepdims=True))
            new_ref[i * own : (i + 1) * own, :] = halves[-1]
    if prior_count:
        at = 0
        for prior_ref in prior_refs:
            image_ref[:, at : at + prior_ref.shape[1]] = prior_ref[...]
            at += prior_ref.shape[1]
    else:
        image_ref[...] = jnp.zeros_like(image_ref)
        if has_side:
            image_ref[:, :own] = (noise_level - 1.0 / STEP) * side_ref[...]
    for j, col_ref in enumerate(col_refs):
        field = unpack_rows(col_ref, probes, own, 0)
        norms = unpack_rows(col_ref, probes, own, 1).astype(jnp.float32)
        col_half = -kernel_rate * (norms[0:1] + norms[1:2] + norms[2:3])
        for i, row_ref in enumerate(row_refs):
            for k in range(own // CHUNK):
                part = slice(k * CHUNK, (k + 1) * CHUNK)
                place = slice(i * own + k * CHUNK, i * own + (k + 1) * CHUNK)
                cross = lax.dot_general(
                    row_ref[part, :], col_ref[:own, :], (((1,), (1,)), ((), ())), preferred_element_type=jnp.float32
                )
                kern = jnp.exp(2.0 * kernel_rate * cross + halves[i][part, :] + col_half).astype(jnp.bfloat16)
                tile_ref[place, j * own : (j + 1) * own] = kern
                image_ref[:, place] += lax.dot_general(
                    field, kern, (((1,), (1,)), ((), ())), preferred_element_type=jnp.float32
                )


def build(rows, cols, own, probes, halves=(), prior=(), side=None):
    features = rows[0].shape[1]
    height, width = len(rows) * own, len(cols) * own
    counts = (len(rows), len(cols), len(halves), len(prior), side is not None)
    out_shape = [
        pltpu.VMEM((height, width), jnp.bfloat16),
        jax.ShapeDtypeStruct((probes, height), jnp.float32),
    ]
    if not halves:
        out_shape.append(jax.ShapeDtypeStruct((height, 1), jnp.float32))
    args = [*rows, *cols, *halves, *prior] + ([] if side is None else [side])
    return pl.pallas_call(
        functools.partial(tile_kernel, counts, probes),
        out_shape=out_shape,
        compiler_params=pltpu.CompilerParams(vmem_limit_bytes=8 << 20),
        cost_estimate=pl.CostEstimate(
            flops=height * width * features * 8, bytes_accessed=1 << 10, transcendentals=0
        ),
        name="build_tile",
    )(*args)


def share_kernel(own, image_ref, *out_refs):
    probes = image_ref.shape[0]
    for k, out_ref in enumerate(out_refs, 1):
        for i in range(len(ROWS)):
            high, middle, _ = split(image_ref[:, i * own : (i + 1) * own])
            out_ref[i * probes : (i + 1) * probes, :] = high
            if i == k:
                out_ref[len(ROWS) * probes :, :] = middle


def share(image, own):
    probes = image.shape[0]
    height = (len(ROWS) + 1) * probes
    return pl.pallas_call(
        functools.partial(share_kernel, own),
        out_shape=[jax.ShapeDtypeStruct((height, own), jnp.bfloat16)] * (len(ROWS) - 1),
        compiler_params=pltpu.CompilerParams(vmem_limit_bytes=4 << 20),
        name="share",
    )(image)


def rho_kernel(own, *refs):
    parts, (rho_ref, narrow_ref) = refs[: len(ROWS)], refs[len(ROWS) :]
    probes = rho_ref.shape[0]
    for j, p in enumerate(ROWS):
        at = j * own
        piece = parts[0][:, at : at + own]
        for s, part in zip(ROWS[1:], parts[1:]):
            at = ROWS.index((p[0] ^ s[0], p[1] ^ s[1])) * probes
            piece = piece + part[at : at + probes, :].astype(jnp.float32)
            if p == HERE:
                piece = piece + part[len(ROWS) * probes :, :].astype(jnp.float32)
        rho = -STEP * piece
        if p == HERE:
            rho_ref[...] = rho
        high, low, _ = split(rho)
        narrow_ref[:probes, j * own : (j + 1) * own] = high
        narrow_ref[probes:, j * own : (j + 1) * own] = low


def sum_rows(parts, own):
    probes, rows = parts[0].shape
    return pl.pallas_call(
        functools.partial(rho_kernel, own),
        out_shape=[
            jax.ShapeDtypeStruct((probes, own), jnp.float32),
            jax.ShapeDtypeStruct((2 * probes, rows), jnp.bfloat16),
        ],
        compiler_params=pltpu.CompilerParams(vmem_limit_bytes=4 << 20),
        name="sum_rows",
    )(*parts)


def second_kernel(own, half, places, narrow_ref, *refs):
    tiles, out_ref = refs[: len(places)], refs[len(places)]
    probes = out_ref.shape[0]
    for j, (h, m) in enumerate(COLS):
        if h != half:
            continue
        part = 0.0
        for tile_ref, (top, left) in zip(tiles, places):
            at = j * own - left
            if 0 <= at < tile_ref.shape[1]:
                part = part + jnp.dot(
                    narrow_ref[:, top : top + tile_ref.shape[0]],
                    tile_ref[:, at : at + own],
                    preferred_element_type=jnp.float32,
                )
        out_ref[:, m * own : (m + 1) * own] = part[:probes] + part[probes:]


def second_product(tiles, narrow, own, half):
    height, rows = narrow.shape
    cols = len(SQUARE) * own
    places = [(top, left) for _, top, left in tiles]
    return pl.pallas_call(
        functools.partial(second_kernel, own, half, places),
        in_specs=[pl.BlockSpec(memory_space=pltpu.VMEM)] * (1 + len(tiles)),
        out_shape=jax.ShapeDtypeStruct((height // 2, cols), jnp.float32),
        compiler_params=pltpu.CompilerParams(vmem_limit_bytes=8 << 20),
        cost_estimate=pl.CostEstimate(flops=rows * cols * 32, bytes_accessed=1 << 10, transcendentals=0),
        name="second_product",
    )(narrow, *[tile for tile, _, _ in tiles])


def merge_kernel(own, mine_ref, other_ref, *out_refs):
    for m, out_ref in enumerate(out_refs):
        here = slice(m * own, (m + 1) * own)
        out_ref[...] = mine_ref[:, here] + other_ref[:, here]


def merge(mine, other, own):
    return pl.pallas_call(
        functools.partial(merge_kernel, own),
        out_shape=[jax.ShapeDtypeStruct((mine.shape[0], own), jnp.float32)] * len(SQUARE),
        compiler_params=pltpu.CompilerParams(vmem_limit_bytes=4 << 20),
        name="merge",
    )(mine, other)


def sums_kernel(side_ref, rho_ref, *refs):
    shares, (image_ref, sums_ref) = refs[: len(SQUARE)], refs[len(SQUARE) :]
    side, rho = side_ref[...], rho_ref[...]
    image = noise_level * rho
    for share in shares:
        image = image + share[...]
    image_ref[...] = image
    total = lambda a, b: jnp.sum(a * b, axis=1, keepdims=True)
    lane = lax.broadcasted_iota(jnp.int32, (side.shape[0], LANES), 1)
    sums = 0.0
    for k, one in enumerate((total(side, side), total(side, rho), total(rho, rho), total(rho, image))):
        sums = jnp.where(lane == k, one, sums)
    sums = sums.T
    sums_ref[...] = jnp.concatenate([sums[k : k + 1] for k in range(LANES // sums.shape[1])], axis=1)


def local_sums(side, rho, shares):
    return pl.pallas_call(
        sums_kernel,
        out_shape=[
            jax.ShapeDtypeStruct(side.shape, jnp.float32),
            jax.ShapeDtypeStruct((1, LANES), jnp.float32),
        ],
        compiler_params=pltpu.CompilerParams(vmem_limit_bytes=4 << 20),
        name="local_sums",
    )(side, rho, *shares)


def finish_kernel(side_ref, rho_ref, image_ref, sums_ref, field_ref, residual_ref):
    side, rho, image = side_ref[...], rho_ref[...], image_ref[...]
    probes = side.shape[0]
    sums = jnp.sum(sums_ref[...], axis=0, keepdims=True)
    sums = jnp.concatenate([sums[:, k * probes : (k + 1) * probes] for k in range(4)] * 2, axis=0).T
    rr, side_rho, rho_rho, rho_image = (sums[:, k : k + 1] for k in range(4))
    curve = (rr - side_rho) / STEP
    alpha = rr / curve
    turn = alpha / STEP
    rest = 1.0 - turn
    rr_next = rest * rest * rr + 2.0 * rest * turn * side_rho + turn * turn * rho_rho
    gain = rest + rr_next / rr
    cross = (side_rho - rho_rho) / STEP
    curve = gain * gain * curve + 2.0 * gain * turn * cross + turn * turn * rho_image
    alpha_next = rr_next / curve
    direction = gain * side + turn * rho
    field_ref[...] = alpha * side + alpha_next * direction
    residual_ref[...] = rest * side + turn * rho - alpha_next * (gain / STEP * (side - rho) + turn * image)


def finish(side, rho, image, sums):
    return pl.pallas_call(
        finish_kernel,
        out_shape=[jax.ShapeDtypeStruct(side.shape, jnp.float32)] * 2,
        compiler_params=pltpu.CompilerParams(vmem_limit_bytes=4 << 20),
        name="finish",
    )(side, rho, image, sums)


def on_device(states, offsets, right_side):
    own, probes = right_side.shape
    side = right_side.T
    points = lax.dynamic_slice_in_dim(states, offsets[0], own, 0)
    with jax.named_scope("fetch_points"):
        message = pack(points, side.astype(jnp.bfloat16))
        rows = [points] + [swap(points, offset) for offset in ROWS[1:]]
        cols = [message] + [swap(message, offset) for offset in SQUARE[1:3]]
        first = [message, swap_core(message)]
        tile_a, image_a, half_a = build([points], first, own, probes, side=side)
        tile_b, image_b, half_b = build(rows[1:3], first, own, probes)
        (rows[1], rows[2], cols[1], cols[2]), image_a, image_b = lax.optimization_barrier(
            ((rows[1], rows[2], cols[1], cols[2]), image_a, image_b)
        )
        cols.append(hand_on(cols[1], cols[2], SQUARE[3]))

    with jax.named_scope("build_tiles"):
        half = [half_a, half_b]
        others = [swap_core(cols[1]), swap_core(cols[2])]
        tile_d, image = build(rows[:3], cols[1:3], own, probes, half, [image_a, image_b])
        tile_e, image = build(rows[:3], others, own, probes, half, [image])
        rows[3], image = lax.optimization_barrier((rows[3], image))
        tile_f, image_far, half_far = build([rows[3]], first + cols[1:3] + others, own, probes)
        cols[3], image_far = lax.optimization_barrier((cols[3], image_far))
        last = swap_core(cols[3])
        half.append(half_far)
        tile_g, image = build(rows, [cols[3]], own, probes, half, [image, image_far])
        tile_h, image = build(rows, [last], own, probes, half, [image])
        tiles = [
            (tile_a, 0, 0),
            (tile_b, own, 0),
            (tile_d, 0, 2 * own),
            (tile_e, 0, 4 * own),
            (tile_f, 3 * own, 0),
            (tile_g, 0, 6 * own),
            (tile_h, 0, 7 * own),
        ]

    with jax.named_scope("sum_over_rows"):
        parts = [image] + swap_each(share(image, own), ROWS[1:])

    rho, narrow = sum_rows(parts, own)
    other = second_product(tiles, narrow, own, 1)
    narrow, other = lax.optimization_barrier((narrow, other))
    mine = second_product(tiles, narrow, own, 0)

    with jax.named_scope("sum_over_columns"):
        blocks = merge(mine, swap_core(other), own)
        shares = [blocks[0]] + swap_each(blocks[1:], SQUARE[1:])

    with jax.named_scope("final_sums"):
        image, sums = local_sums(side, rho, shares)
        sums = jnp.broadcast_to(sums, (NY * NZ * NC, LANES))
        sums = lax.all_to_all(sums, ("y", "z", "c"), 0, 0, tiled=True)

    field, residual = finish(side, rho, image, sums)
    return field.T, residual.T


def solution(mesh):
    fine = Mesh(mesh.devices.reshape(NY, NZ, NC, NX), ("y", "z", "c", "x"))
    rows = ("y", "z", "c")
    in_specs = (P(rows, None), P(rows), P(rows, "x"))
    out_specs = (P(rows, "x"), P(rows, "x"))
    return jax.shard_map(on_device, mesh=fine, in_specs=in_specs, out_specs=out_specs, check_vma=False)
```

```python
import functools

import jax
import jax.numpy as jnp
from jax import lax
from jax.experimental import pallas as pl
from jax.experimental.pallas import tpu as pltpu
from jax.sharding import Mesh
from jax.sharding import PartitionSpec as P

NY, NZ, NC, NX = 4, 4, 2, 4
LANES = 128
CHUNK = 256
HERE = (0, 0)
ROWS = (HERE, (1, 0), (0, 1), (1, 1))
SQUARE = (HERE, (3, 0), (0, 3), (3, 3))
COLS = ((0, 0), (1, 0), (0, 1), (0, 2), (1, 1), (1, 2), (0, 3), (1, 3))

noise_level = 1.0
kernel_rate = 0.5
STEP = 1.0 / (1.0 + noise_level)


def swap(value, offset):
    pairs = []
    for y in range(NY):
        for z in range(NZ):
            pairs.append((y * NZ + z, (y ^ offset[0]) * NZ + (z ^ offset[1])))
    return lax.ppermute(value, ("y", "z"), pairs)


def swap_each(values, offsets):
    received = [swap(value, offset) for value, offset in reversed(list(zip(values, offsets)))]
    return received[::-1]


def swap_core(value):
    return lax.ppermute(value, "c", [(0, 1), (1, 0)])


def split(value):
    high = value.astype(jnp.bfloat16)
    rest = value - high.astype(jnp.float32)
    middle = rest.astype(jnp.bfloat16)
    return high, middle, (rest - middle.astype(jnp.float32)).astype(jnp.bfloat16)


def pack_kernel(points_ref, side_ref, out_ref):
    own, width = points_ref.shape
    probes = side_ref.shape[0]
    out_ref[:own, :] = points_ref[...]
    high, middle, _ = split(points_ref[...].astype(jnp.float32) ** 2)
    ones = jnp.ones((probes, width), jnp.bfloat16)
    norms = 0.0
    for term in (high, middle):
        norms = norms + lax.dot_general(ones, term, (((1,), (1,)), ((), ())), preferred_element_type=jnp.float32)
    high, middle, low = split(norms)
    row = lax.broadcasted_iota(jnp.int32, norms.shape, 0)
    norms = jnp.where(row == 0, high.astype(jnp.float32), jnp.where(row == 1, middle.astype(jnp.float32), low.astype(jnp.float32)))
    at = own
    for part in (side_ref[...], norms.astype(jnp.bfloat16)):
        for j in range(own // width):
            out_ref[at : at + probes, :] = part[:, j * width : (j + 1) * width]
            at += probes


def pack(points, side):
    own, width = points.shape
    extra = side.shape[0] * 2 * own // width
    return pl.pallas_call(
        pack_kernel,
        out_shape=jax.ShapeDtypeStruct((own + extra, width), jnp.bfloat16),
        compiler_params=pltpu.CompilerParams(vmem_limit_bytes=8 << 20),
        name="pack",
    )(points, side)


def unpack_rows(message, probes, own, term):
    width = message.shape[1]
    count = own // width
    at = own + term * count * probes
    return jnp.concatenate([message[at + j * probes : at + (j + 1) * probes] for j in range(count)], axis=1)


def tile_kernel(counts, probes, *refs):
    rows_count, cols_count, known_halves, prior_count, has_side = counts
    refs = list(refs)
    row_refs = [refs.pop(0) for _ in range(rows_count)]
    col_refs = [refs.pop(0) for _ in range(cols_count)]
    half_refs = [refs.pop(0) for _ in range(known_halves)]
    prior_refs = [refs.pop(0) for _ in range(prior_count)]
    side_ref = refs.pop(0) if has_side else None
    tile_ref, image_ref = refs.pop(0), refs.pop(0)
    own = tile_ref.shape[0] // rows_count
    if known_halves:
        pieces = []
        for half_ref in half_refs:
            pieces += [half_ref[j * own : (j + 1) * own, :] for j in range(half_ref.shape[0] // own)]
        halves = pieces
    else:
        new_ref = refs.pop(0)
        halves = []
        for i, row_ref in enumerate(row_refs):
            squares = row_ref[:own, :].astype(jnp.float32) ** 2
            halves.append(-kernel_rate * jnp.sum(squares, axis=1, keepdims=True))
            new_ref[i * own : (i + 1) * own, :] = halves[-1]
    if prior_count:
        at = 0
        for prior_ref in prior_refs:
            image_ref[:, at : at + prior_ref.shape[1]] = prior_ref[...]
            at += prior_ref.shape[1]
    else:
        image_ref[...] = jnp.zeros_like(image_ref)
        if has_side:
            image_ref[:, :own] = (noise_level - 1.0 / STEP) * side_ref[...]
    for j, col_ref in enumerate(col_refs):
        field = unpack_rows(col_ref, probes, own, 0)
        norms = unpack_rows(col_ref, probes, own, 1).astype(jnp.float32)
        col_half = -kernel_rate * (norms[0:1] + norms[1:2] + norms[2:3])
        for i, row_ref in enumerate(row_refs):
            for k in range(own // CHUNK):
                part = slice(k * CHUNK, (k + 1) * CHUNK)
                place = slice(i * own + k * CHUNK, i * own + (k + 1) * CHUNK)
                cross = lax.dot_general(
                    row_ref[part, :], col_ref[:own, :], (((1,), (1,)), ((), ())), preferred_element_type=jnp.float32
                )
                kern = jnp.exp(2.0 * kernel_rate * cross + halves[i][part, :] + col_half).astype(jnp.bfloat16)
                tile_ref[place, j * own : (j + 1) * own] = kern
                image_ref[:, place] += lax.dot_general(
                    field, kern, (((1,), (1,)), ((), ())), preferred_element_type=jnp.float32
                )


def build(rows, cols, own, probes, halves=(), prior=(), side=None):
    features = rows[0].shape[1]
    height, width = len(rows) * own, len(cols) * own
    counts = (len(rows), len(cols), len(halves), len(prior), side is not None)
    out_shape = [
        pltpu.VMEM((height, width), jnp.bfloat16),
        jax.ShapeDtypeStruct((probes, height), jnp.float32),
    ]
    if not halves:
        out_shape.append(jax.ShapeDtypeStruct((height, 1), jnp.float32))
    args = [*rows, *cols, *halves, *prior] + ([] if side is None else [side])
    return pl.pallas_call(
        functools.partial(tile_kernel, counts, probes),
        out_shape=out_shape,
        compiler_params=pltpu.CompilerParams(vmem_limit_bytes=8 << 20),
        cost_estimate=pl.CostEstimate(
            flops=height * width * features * 8, bytes_accessed=1 << 10, transcendentals=0
        ),
        name="build_tile",
    )(*args)


def share_kernel(own, image_ref, *out_refs):
    probes = image_ref.shape[0]
    for k, out_ref in enumerate(out_refs, 1):
        for i in range(len(ROWS)):
            high, middle, _ = split(image_ref[:, i * own : (i + 1) * own])
            out_ref[i * probes : (i + 1) * probes, :] = high
            if i == k:
                out_ref[len(ROWS) * probes :, :] = middle


def share(image, own):
    probes = image.shape[0]
    height = (len(ROWS) + 1) * probes
    return pl.pallas_call(
        functools.partial(share_kernel, own),
        out_shape=[jax.ShapeDtypeStruct((height, own), jnp.bfloat16)] * (len(ROWS) - 1),
        compiler_params=pltpu.CompilerParams(vmem_limit_bytes=4 << 20),
        name="share",
    )(image)


def rho_kernel(own, *refs):
    parts, (rho_ref, narrow_ref) = refs[: len(ROWS)], refs[len(ROWS) :]
    probes = rho_ref.shape[0]
    for j, p in enumerate(ROWS):
        at = j * own
        piece = parts[0][:, at : at + own]
        for s, part in zip(ROWS[1:], parts[1:]):
            at = ROWS.index((p[0] ^ s[0], p[1] ^ s[1])) * probes
            piece = piece + part[at : at + probes, :].astype(jnp.float32)
            if p == HERE:
                piece = piece + part[len(ROWS) * probes :, :].astype(jnp.float32)
        rho = -STEP * piece
        if p == HERE:
            rho_ref[...] = rho
        high, low, _ = split(rho)
        narrow_ref[:probes, j * own : (j + 1) * own] = high
        narrow_ref[probes:, j * own : (j + 1) * own] = low


def sum_rows(parts, own):
    probes, rows = parts[0].shape
    return pl.pallas_call(
        functools.partial(rho_kernel, own),
        out_shape=[
            jax.ShapeDtypeStruct((probes, own), jnp.float32),
            jax.ShapeDtypeStruct((2 * probes, rows), jnp.bfloat16),
        ],
        compiler_params=pltpu.CompilerParams(vmem_limit_bytes=4 << 20),
        name="sum_rows",
    )(*parts)


def second_kernel(own, half, places, narrow_ref, *refs):
    tiles, out_ref = refs[: len(places)], refs[len(places)]
    probes = out_ref.shape[0]
    for j, (h, m) in enumerate(COLS):
        if h != half:
            continue
        part = 0.0
        for tile_ref, (top, left) in zip(tiles, places):
            at = j * own - left
            if 0 <= at < tile_ref.shape[1]:
                part = part + jnp.dot(
                    narrow_ref[:, top : top + tile_ref.shape[0]],
                    tile_ref[:, at : at + own],
                    preferred_element_type=jnp.float32,
                )
        out_ref[:, m * own : (m + 1) * own] = part[:probes] + part[probes:]


def second_product(tiles, narrow, own, half):
    height, rows = narrow.shape
    cols = len(SQUARE) * own
    places = [(top, left) for _, top, left in tiles]
    return pl.pallas_call(
        functools.partial(second_kernel, own, half, places),
        in_specs=[pl.BlockSpec(memory_space=pltpu.VMEM)] * (1 + len(tiles)),
        out_shape=jax.ShapeDtypeStruct((height // 2, cols), jnp.float32),
        compiler_params=pltpu.CompilerParams(vmem_limit_bytes=8 << 20),
        cost_estimate=pl.CostEstimate(flops=rows * cols * 32, bytes_accessed=1 << 10, transcendentals=0),
        name="second_product",
    )(narrow, *[tile for tile, _, _ in tiles])


def merge_kernel(own, mine_ref, other_ref, *out_refs):
    for m, out_ref in enumerate(out_refs):
        here = slice(m * own, (m + 1) * own)
        out_ref[...] = mine_ref[:, here] + other_ref[:, here]


def merge(mine, other, own):
    return pl.pallas_call(
        functools.partial(merge_kernel, own),
        out_shape=[jax.ShapeDtypeStruct((mine.shape[0], own), jnp.float32)] * len(SQUARE),
        compiler_params=pltpu.CompilerParams(vmem_limit_bytes=4 << 20),
        name="merge",
    )(mine, other)


def sums_kernel(side_ref, rho_ref, *refs):
    shares, (image_ref, sums_ref) = refs[: len(SQUARE)], refs[len(SQUARE) :]
    side, rho = side_ref[...], rho_ref[...]
    image = noise_level * rho
    for share in shares:
        image = image + share[...]
    image_ref[...] = image
    total = lambda a, b: jnp.sum(a * b, axis=1, keepdims=True)
    lane = lax.broadcasted_iota(jnp.int32, (side.shape[0], LANES), 1)
    sums = 0.0
    for k, one in enumerate((total(side, side), total(side, rho), total(rho, rho), total(rho, image))):
        sums = jnp.where(lane == k, one, sums)
    sums = sums.T
    sums_ref[...] = jnp.concatenate([sums[k : k + 1] for k in range(LANES // sums.shape[1])], axis=1)


def local_sums(side, rho, shares):
    return pl.pallas_call(
        sums_kernel,
        out_shape=[
            jax.ShapeDtypeStruct(side.shape, jnp.float32),
            jax.ShapeDtypeStruct((1, LANES), jnp.float32),
        ],
        compiler_params=pltpu.CompilerParams(vmem_limit_bytes=4 << 20),
        name="local_sums",
    )(side, rho, *shares)


def finish_kernel(side_ref, rho_ref, image_ref, sums_ref, field_ref, residual_ref):
    side, rho, image = side_ref[...], rho_ref[...], image_ref[...]
    probes = side.shape[0]
    sums = jnp.sum(sums_ref[...], axis=0, keepdims=True)
    sums = jnp.concatenate([sums[:, k * probes : (k + 1) * probes] for k in range(4)] * 2, axis=0).T
    rr, side_rho, rho_rho, rho_image = (sums[:, k : k + 1] for k in range(4))
    curve = (rr - side_rho) / STEP
    alpha = rr / curve
    turn = alpha / STEP
    rest = 1.0 - turn
    rr_next = rest * rest * rr + 2.0 * rest * turn * side_rho + turn * turn * rho_rho
    gain = rest + rr_next / rr
    cross = (side_rho - rho_rho) / STEP
    curve = gain * gain * curve + 2.0 * gain * turn * cross + turn * turn * rho_image
    alpha_next = rr_next / curve
    direction = gain * side + turn * rho
    field_ref[...] = alpha * side + alpha_next * direction
    residual_ref[...] = rest * side + turn * rho - alpha_next * (gain / STEP * (side - rho) + turn * image)


def finish(side, rho, image, sums):
    return pl.pallas_call(
        finish_kernel,
        out_shape=[jax.ShapeDtypeStruct(side.shape, jnp.float32)] * 2,
        compiler_params=pltpu.CompilerParams(vmem_limit_bytes=4 << 20),
        name="finish",
    )(side, rho, image, sums)


def on_device(states, offsets, right_side):
    own, probes = right_side.shape
    side = right_side.T
    points = lax.dynamic_slice_in_dim(states, offsets[0], own, 0)
    with jax.named_scope("fetch_points"):
        message = pack(points, side.astype(jnp.bfloat16))
        rows = [points] + [swap(points, offset) for offset in ROWS[1:]]
        cols = [message] + [swap(message, offset) for offset in SQUARE[1:]]
        first = [message, swap_core(message)]
        tile_a, image_a, half_a = build([points], first, own, probes, side=side)
        tile_b, image_b, half_b = build(rows[1:3], first, own, probes)
        (rows[1], rows[2], cols[1], cols[2]), image_a, image_b = lax.optimization_barrier(
            ((rows[1], rows[2], cols[1], cols[2]), image_a, image_b)
        )

    with jax.named_scope("build_tiles"):
        half = [half_a, half_b]
        others = [swap_core(cols[1]), swap_core(cols[2])]
        tile_d, image = build(rows[:3], cols[1:3], own, probes, half, [image_a, image_b])
        tile_e, image = build(rows[:3], others, own, probes, half, [image])
        rows[3], image = lax.optimization_barrier((rows[3], image))
        tile_f, image_far, half_far = build([rows[3]], first + cols[1:3] + others, own, probes)
        cols[3], image_far = lax.optimization_barrier((cols[3], image_far))
        last = swap_core(cols[3])
        half.append(half_far)
        tile_g, image = build(rows, [cols[3]], own, probes, half, [image, image_far])
        tile_h, image = build(rows, [last], own, probes, half, [image])
        tiles = [
            (tile_a, 0, 0),
            (tile_b, own, 0),
            (tile_d, 0, 2 * own),
            (tile_e, 0, 4 * own),
            (tile_f, 3 * own, 0),
            (tile_g, 0, 6 * own),
            (tile_h, 0, 7 * own),
        ]

    with jax.named_scope("sum_over_rows"):
        parts = [image] + swap_each(share(image, own), ROWS[1:])

    rho, narrow = sum_rows(parts, own)
    other = second_product(tiles, narrow, own, 1)
    narrow, other = lax.optimization_barrier((narrow, other))
    mine = second_product(tiles, narrow, own, 0)

    with jax.named_scope("sum_over_columns"):
        blocks = merge(mine, swap_core(other), own)
        shares = [blocks[0]] + swap_each(blocks[1:], SQUARE[1:])

    with jax.named_scope("final_sums"):
        image, sums = local_sums(side, rho, shares)
        sums = jnp.broadcast_to(sums, (NY * NZ * NC, LANES))
        sums = lax.all_to_all(sums, ("y", "z", "c"), 0, 0, tiled=True)

    field, residual = finish(side, rho, image, sums)
    return field.T, residual.T


def solution(mesh):
    fine = Mesh(mesh.devices.reshape(NY, NZ, NC, NX), ("y", "z", "c", "x"))
    rows = ("y", "z", "c")
    in_specs = (P(rows, None), P(rows), P(rows, "x"))
    out_specs = (P(rows, "x"), P(rows, "x"))
    return jax.shard_map(on_device, mesh=fine, in_specs=in_specs, out_specs=out_specs, check_vma=False)
```

```python
import functools

import jax
import jax.numpy as jnp
from jax import lax
from jax.experimental import pallas as pl
from jax.experimental.pallas import tpu as pltpu
from jax.sharding import Mesh
from jax.sharding import PartitionSpec as P

NY, NZ, NC, NX = 4, 4, 2, 4
LANES = 128
CHUNK = 256
HERE = (0, 0)
ROWS = (HERE, (1, 0), (0, 1), (1, 1))
SQUARE = (HERE, (3, 0), (0, 3), (3, 3))
COLS = ((0, 0), (1, 0), (0, 1), (0, 2), (1, 1), (1, 2), (0, 3), (1, 3))

noise_level = 1.0
kernel_rate = 0.5
STEP = 1.0 / (1.0 + noise_level)


def swap(value, offset):
    pairs = []
    for y in range(NY):
        for z in range(NZ):
            pairs.append((y * NZ + z, (y ^ offset[0]) * NZ + (z ^ offset[1])))
    return lax.ppermute(value, ("y", "z"), pairs)


def swap_each(values, offsets):
    received = [swap(value, offset) for value, offset in reversed(list(zip(values, offsets)))]
    return received[::-1]


def swap_core(value):
    return lax.ppermute(value, "c", [(0, 1), (1, 0)])


def split(value):
    high = value.astype(jnp.bfloat16)
    rest = value - high.astype(jnp.float32)
    middle = rest.astype(jnp.bfloat16)
    return high, middle, (rest - middle.astype(jnp.float32)).astype(jnp.bfloat16)


def pack_kernel(points_ref, side_ref, out_ref):
    own, width = points_ref.shape
    probes = side_ref.shape[0]
    out_ref[:own, :] = points_ref[...]
    high, middle, _ = split(points_ref[...].astype(jnp.float32) ** 2)
    ones = jnp.ones((probes, width), jnp.bfloat16)
    norms = 0.0
    for term in (high, middle):
        norms = norms + lax.dot_general(ones, term, (((1,), (1,)), ((), ())), preferred_element_type=jnp.float32)
    high, middle, low = split(norms)
    row = lax.broadcasted_iota(jnp.int32, norms.shape, 0)
    norms = jnp.where(row == 0, high.astype(jnp.float32), jnp.where(row == 1, middle.astype(jnp.float32), low.astype(jnp.float32)))
    at = own
    for part in (side_ref[...], norms.astype(jnp.bfloat16)):
        for j in range(own // width):
            out_ref[at : at + probes, :] = part[:, j * width : (j + 1) * width]
            at += probes


def pack(points, side):
    own, width = points.shape
    extra = side.shape[0] * 2 * own // width
    return pl.pallas_call(
        pack_kernel,
        out_shape=jax.ShapeDtypeStruct((own + extra, width), jnp.bfloat16),
        compiler_params=pltpu.CompilerParams(vmem_limit_bytes=8 << 20),
        name="pack",
    )(points, side)


def unpack_rows(message, probes, own, term):
    width = message.shape[1]
    count = own // width
    at = own + term * count * probes
    return jnp.concatenate([message[at + j * probes : at + (j + 1) * probes] for j in range(count)], axis=1)


def tile_kernel(counts, probes, *refs):
    rows_count, cols_count, known_halves, prior_count, has_side = counts
    refs = list(refs)
    row_refs = [refs.pop(0) for _ in range(rows_count)]
    col_refs = [refs.pop(0) for _ in range(cols_count)]
    half_refs = [refs.pop(0) for _ in range(known_halves)]
    prior_refs = [refs.pop(0) for _ in range(prior_count)]
    side_ref = refs.pop(0) if has_side else None
    tile_ref, image_ref = refs.pop(0), refs.pop(0)
    own = tile_ref.shape[0] // rows_count
    if known_halves:
        pieces = []
        for half_ref in half_refs:
            pieces += [half_ref[j * own : (j + 1) * own, :] for j in range(half_ref.shape[0] // own)]
        halves = pieces
    else:
        new_ref = refs.pop(0)
        halves = []
        for i, row_ref in enumerate(row_refs):
            squares = row_ref[:own, :].astype(jnp.float32) ** 2
            halves.append(-kernel_rate * jnp.sum(squares, axis=1, keepdims=True))
            new_ref[i * own : (i + 1) * own, :] = halves[-1]
    if prior_count:
        at = 0
        for prior_ref in prior_refs:
            image_ref[:, at : at + prior_ref.shape[1]] = prior_ref[...]
            at += prior_ref.shape[1]
    else:
        image_ref[...] = jnp.zeros_like(image_ref)
        if has_side:
            image_ref[:, :own] = (noise_level - 1.0 / STEP) * side_ref[...]
    for j, col_ref in enumerate(col_refs):
        field = unpack_rows(col_ref, probes, own, 0)
        norms = unpack_rows(col_ref, probes, own, 1).astype(jnp.float32)
        col_half = -kernel_rate * (norms[0:1] + norms[1:2] + norms[2:3])
        for i, row_ref in enumerate(row_refs):
            for k in range(own // CHUNK):
                part = slice(k * CHUNK, (k + 1) * CHUNK)
                place = slice(i * own + k * CHUNK, i * own + (k + 1) * CHUNK)
                cross = lax.dot_general(
                    row_ref[part, :], col_ref[:own, :], (((1,), (1,)), ((), ())), preferred_element_type=jnp.float32
                )
                kern = jnp.exp(2.0 * kernel_rate * cross + halves[i][part, :] + col_half).astype(jnp.bfloat16)
                tile_ref[place, j * own : (j + 1) * own] = kern
                image_ref[:, place] += lax.dot_general(
                    field, kern, (((1,), (1,)), ((), ())), preferred_element_type=jnp.float32
                )


def build(rows, cols, own, probes, halves=(), prior=(), side=None, weight=64):
    features = rows[0].shape[1]
    height, width = len(rows) * own, len(cols) * own
    counts = (len(rows), len(cols), len(halves), len(prior), side is not None)
    out_shape = [
        pltpu.VMEM((height, width), jnp.bfloat16),
        jax.ShapeDtypeStruct((probes, height), jnp.float32),
    ]
    if not halves:
        out_shape.append(jax.ShapeDtypeStruct((height, 1), jnp.float32))
    args = [*rows, *cols, *halves, *prior] + ([] if side is None else [side])
    return pl.pallas_call(
        functools.partial(tile_kernel, counts, probes),
        out_shape=out_shape,
        compiler_params=pltpu.CompilerParams(vmem_limit_bytes=8 << 20),
        cost_estimate=pl.CostEstimate(
            flops=height * width * features * weight // 8, bytes_accessed=1 << 10, transcendentals=0
        ),
        name="build_tile",
    )(*args)


def share_kernel(own, image_ref, *out_refs):
    probes = image_ref.shape[0]
    for k, out_ref in enumerate(out_refs, 1):
        for i in range(len(ROWS)):
            high, middle, _ = split(image_ref[:, i * own : (i + 1) * own])
            out_ref[i * probes : (i + 1) * probes, :] = high
            if i == k:
                out_ref[len(ROWS) * probes :, :] = middle


def share(image, own):
    probes = image.shape[0]
    height = (len(ROWS) + 1) * probes
    return pl.pallas_call(
        functools.partial(share_kernel, own),
        out_shape=[jax.ShapeDtypeStruct((height, own), jnp.bfloat16)] * (len(ROWS) - 1),
        compiler_params=pltpu.CompilerParams(vmem_limit_bytes=4 << 20),
        name="share",
    )(image)


def rho_kernel(own, *refs):
    parts, (rho_ref, narrow_ref) = refs[: len(ROWS)], refs[len(ROWS) :]
    probes = rho_ref.shape[0]
    for j, p in enumerate(ROWS):
        at = j * own
        piece = parts[0][:, at : at + own]
        for s, part in zip(ROWS[1:], parts[1:]):
            at = ROWS.index((p[0] ^ s[0], p[1] ^ s[1])) * probes
            piece = piece + part[at : at + probes, :].astype(jnp.float32)
            if p == HERE:
                piece = piece + part[len(ROWS) * probes :, :].astype(jnp.float32)
        rho = -STEP * piece
        if p == HERE:
            rho_ref[...] = rho
        high, low, _ = split(rho)
        narrow_ref[:probes, j * own : (j + 1) * own] = high
        narrow_ref[probes:, j * own : (j + 1) * own] = low


def sum_rows(parts, own):
    probes, rows = parts[0].shape
    return pl.pallas_call(
        functools.partial(rho_kernel, own),
        out_shape=[
            jax.ShapeDtypeStruct((probes, own), jnp.float32),
            jax.ShapeDtypeStruct((2 * probes, rows), jnp.bfloat16),
        ],
        compiler_params=pltpu.CompilerParams(vmem_limit_bytes=4 << 20),
        name="sum_rows",
    )(*parts)


def second_kernel(own, half, places, narrow_ref, *refs):
    tiles, out_ref = refs[: len(places)], refs[len(places)]
    probes = out_ref.shape[0]
    for j, (h, m) in enumerate(COLS):
        if h != half:
            continue
        part = 0.0
        for tile_ref, (top, left) in zip(tiles, places):
            at = j * own - left
            if 0 <= at < tile_ref.shape[1]:
                part = part + jnp.dot(
                    narrow_ref[:, top : top + tile_ref.shape[0]],
                    tile_ref[:, at : at + own],
                    preferred_element_type=jnp.float32,
                )
        out_ref[:, m * own : (m + 1) * own] = part[:probes] + part[probes:]


def second_product(tiles, narrow, own, half):
    height, rows = narrow.shape
    cols = len(SQUARE) * own
    places = [(top, left) for _, top, left in tiles]
    return pl.pallas_call(
        functools.partial(second_kernel, own, half, places),
        in_specs=[pl.BlockSpec(memory_space=pltpu.VMEM)] * (1 + len(tiles)),
        out_shape=jax.ShapeDtypeStruct((height // 2, cols), jnp.float32),
        compiler_params=pltpu.CompilerParams(vmem_limit_bytes=8 << 20),
        cost_estimate=pl.CostEstimate(flops=rows * cols * 32, bytes_accessed=1 << 10, transcendentals=0),
        name="second_product",
    )(narrow, *[tile for tile, _, _ in tiles])


def merge_kernel(own, mine_ref, other_ref, *out_refs):
    for m, out_ref in enumerate(out_refs):
        here = slice(m * own, (m + 1) * own)
        out_ref[...] = mine_ref[:, here] + other_ref[:, here]


def merge(mine, other, own):
    return pl.pallas_call(
        functools.partial(merge_kernel, own),
        out_shape=[jax.ShapeDtypeStruct((mine.shape[0], own), jnp.float32)] * len(SQUARE),
        compiler_params=pltpu.CompilerParams(vmem_limit_bytes=4 << 20),
        name="merge",
    )(mine, other)


def sums_kernel(side_ref, rho_ref, *refs):
    shares, (image_ref, sums_ref) = refs[: len(SQUARE)], refs[len(SQUARE) :]
    side, rho = side_ref[...], rho_ref[...]
    image = noise_level * rho
    for share in shares:
        image = image + share[...]
    image_ref[...] = image
    total = lambda a, b: jnp.sum(a * b, axis=1, keepdims=True)
    lane = lax.broadcasted_iota(jnp.int32, (side.shape[0], LANES), 1)
    sums = 0.0
    for k, one in enumerate((total(side, side), total(side, rho), total(rho, rho), total(rho, image))):
        sums = jnp.where(lane == k, one, sums)
    sums = sums.T
    sums_ref[...] = jnp.concatenate([sums[k : k + 1] for k in range(LANES // sums.shape[1])], axis=1)


def local_sums(side, rho, shares):
    return pl.pallas_call(
        sums_kernel,
        out_shape=[
            jax.ShapeDtypeStruct(side.shape, jnp.float32),
            jax.ShapeDtypeStruct((1, LANES), jnp.float32),
        ],
        compiler_params=pltpu.CompilerParams(vmem_limit_bytes=4 << 20),
        name="local_sums",
    )(side, rho, *shares)


def finish_kernel(side_ref, rho_ref, image_ref, sums_ref, field_ref, residual_ref):
    side, rho, image = side_ref[...], rho_ref[...], image_ref[...]
    probes = side.shape[0]
    sums = jnp.sum(sums_ref[...], axis=0, keepdims=True)
    sums = jnp.concatenate([sums[:, k * probes : (k + 1) * probes] for k in range(4)] * 2, axis=0).T
    rr, side_rho, rho_rho, rho_image = (sums[:, k : k + 1] for k in range(4))
    curve = (rr - side_rho) / STEP
    alpha = rr / curve
    turn = alpha / STEP
    rest = 1.0 - turn
    rr_next = rest * rest * rr + 2.0 * rest * turn * side_rho + turn * turn * rho_rho
    gain = rest + rr_next / rr
    cross = (side_rho - rho_rho) / STEP
    curve = gain * gain * curve + 2.0 * gain * turn * cross + turn * turn * rho_image
    alpha_next = rr_next / curve
    direction = gain * side + turn * rho
    field_ref[...] = alpha * side + alpha_next * direction
    residual_ref[...] = rest * side + turn * rho - alpha_next * (gain / STEP * (side - rho) + turn * image)


def finish(side, rho, image, sums):
    return pl.pallas_call(
        finish_kernel,
        out_shape=[jax.ShapeDtypeStruct(side.shape, jnp.float32)] * 2,
        compiler_params=pltpu.CompilerParams(vmem_limit_bytes=4 << 20),
        name="finish",
    )(side, rho, image, sums)


def on_device(states, offsets, right_side):
    own, probes = right_side.shape
    side = right_side.T
    points = lax.dynamic_slice_in_dim(states, offsets[0], own, 0)
    with jax.named_scope("fetch_points"):
        message = pack(points, side.astype(jnp.bfloat16))
        rows = [points] + [swap(points, offset) for offset in ROWS[1:]]
        cols = [message] + [swap(message, offset) for offset in SQUARE[1:]]
        first = [message, swap_core(message)]
        tile_a, image_a, half_a = build([points], first, own, probes, side=side, weight=1)
        tile_b, image_b, half_b = build(rows[1:3], first, own, probes, weight=1)
        (rows[1], rows[2], cols[1], cols[2]), image_a, image_b = lax.optimization_barrier(
            ((rows[1], rows[2], cols[1], cols[2]), image_a, image_b)
        )

    with jax.named_scope("build_tiles"):
        half = [half_a, half_b]
        others = [swap_core(cols[1]), swap_core(cols[2])]
        tile_d, image = build(rows[:3], cols[1:3], own, probes, half, [image_a, image_b])
        tile_e, image = build(rows[:3], others, own, probes, half, [image])
        rows[3], image = lax.optimization_barrier((rows[3], image))
        tile_f, image_far, half_far = build([rows[3]], first + cols[1:3] + others, own, probes)
        cols[3], image_far = lax.optimization_barrier((cols[3], image_far))
        last = swap_core(cols[3])
        half.append(half_far)
        tile_g, image = build(rows, [cols[3]], own, probes, half, [image, image_far])
        tile_h, image = build(rows, [last], own, probes, half, [image])
        tiles = [
            (tile_a, 0, 0),
            (tile_b, own, 0),
            (tile_d, 0, 2 * own),
            (tile_e, 0, 4 * own),
            (tile_f, 3 * own, 0),
            (tile_g, 0, 6 * own),
            (tile_h, 0, 7 * own),
        ]

    with jax.named_scope("sum_over_rows"):
        parts = [image] + swap_each(share(image, own), ROWS[1:])

    rho, narrow = sum_rows(parts, own)
    other = second_product(tiles, narrow, own, 1)
    narrow, other = lax.optimization_barrier((narrow, other))
    mine = second_product(tiles, narrow, own, 0)

    with jax.named_scope("sum_over_columns"):
        blocks = merge(mine, swap_core(other), own)
        shares = [blocks[0]] + swap_each(blocks[1:], SQUARE[1:])

    with jax.named_scope("final_sums"):
        image, sums = local_sums(side, rho, shares)
        sums = jnp.broadcast_to(sums, (NY * NZ * NC, LANES))
        sums = lax.all_to_all(sums, ("y", "z", "c"), 0, 0, tiled=True)

    field, residual = finish(side, rho, image, sums)
    return field.T, residual.T


def solution(mesh):
    fine = Mesh(mesh.devices.reshape(NY, NZ, NC, NX), ("y", "z", "c", "x"))
    rows = ("y", "z", "c")
    in_specs = (P(rows, None), P(rows), P(rows, "x"))
    out_specs = (P(rows, "x"), P(rows, "x"))
    return jax.shard_map(on_device, mesh=fine, in_specs=in_specs, out_specs=out_specs, check_vma=False)
```

```python
import functools

import jax
import jax.numpy as jnp
from jax import lax
from jax.experimental import pallas as pl
from jax.experimental.pallas import tpu as pltpu
from jax.sharding import Mesh
from jax.sharding import PartitionSpec as P

NY, NZ, NC, NX = 4, 4, 2, 4
LANES = 128
CHUNK = 256
HERE = (0, 0)
ROWS = (HERE, (1, 0), (0, 1), (1, 1))
SQUARE = (HERE, (3, 0), (0, 3), (3, 3))
COLS = ((0, 0), (1, 0), (0, 1), (0, 2), (1, 1), (1, 2), (0, 3), (1, 3))

noise_level = 1.0
kernel_rate = 0.5
STEP = 1.0 / (1.0 + noise_level)


def swap(value, offset):
    pairs = []
    for y in range(NY):
        for z in range(NZ):
            pairs.append((y * NZ + z, (y ^ offset[0]) * NZ + (z ^ offset[1])))
    return lax.ppermute(value, ("y", "z"), pairs)


def swap_each(values, offsets):
    received = [swap(value, offset) for value, offset in reversed(list(zip(values, offsets)))]
    return received[::-1]


def swap_core(value):
    return lax.ppermute(value, "c", [(0, 1), (1, 0)])


def split(value):
    high = value.astype(jnp.bfloat16)
    rest = value - high.astype(jnp.float32)
    middle = rest.astype(jnp.bfloat16)
    return high, middle, (rest - middle.astype(jnp.float32)).astype(jnp.bfloat16)


def pack_kernel(points_ref, side_ref, out_ref):
    own, width = points_ref.shape
    probes = side_ref.shape[0]
    out_ref[:own, :] = points_ref[...]
    high, middle, _ = split(points_ref[...].astype(jnp.float32) ** 2)
    ones = jnp.ones((probes, width), jnp.bfloat16)
    norms = 0.0
    for term in (high, middle):
        norms = norms + lax.dot_general(ones, term, (((1,), (1,)), ((), ())), preferred_element_type=jnp.float32)
    high, middle, low = split(norms)
    row = lax.broadcasted_iota(jnp.int32, norms.shape, 0)
    norms = jnp.where(row == 0, high.astype(jnp.float32), jnp.where(row == 1, middle.astype(jnp.float32), low.astype(jnp.float32)))
    at = own
    for part in (side_ref[...], norms.astype(jnp.bfloat16)):
        for j in range(own // width):
            out_ref[at : at + probes, :] = part[:, j * width : (j + 1) * width]
            at += probes


def pack(points, side):
    own, width = points.shape
    extra = side.shape[0] * 2 * own // width
    return pl.pallas_call(
        pack_kernel,
        out_shape=jax.ShapeDtypeStruct((own + extra, width), jnp.bfloat16),
        compiler_params=pltpu.CompilerParams(vmem_limit_bytes=8 << 20),
        name="pack",
    )(points, side)


def unpack_rows(message, probes, own, term):
    width = message.shape[1]
    count = own // width
    at = own + term * count * probes
    return jnp.concatenate([message[at + j * probes : at + (j + 1) * probes] for j in range(count)], axis=1)


def tile_kernel(counts, probes, *refs):
    rows_count, cols_count, known_halves, prior_count, has_side = counts
    refs = list(refs)
    row_refs = [refs.pop(0) for _ in range(rows_count)]
    col_refs = [refs.pop(0) for _ in range(cols_count)]
    half_refs = [refs.pop(0) for _ in range(known_halves)]
    prior_refs = [refs.pop(0) for _ in range(prior_count)]
    side_ref = refs.pop(0) if has_side else None
    tile_ref, image_ref = refs.pop(0), refs.pop(0)
    own = tile_ref.shape[0] // rows_count
    if known_halves:
        pieces = []
        for half_ref in half_refs:
            pieces += [half_ref[j * own : (j + 1) * own, :] for j in range(half_ref.shape[0] // own)]
        halves = pieces
    else:
        new_ref = refs.pop(0)
        halves = []
        for i, row_ref in enumerate(row_refs):
            squares = row_ref[:own, :].astype(jnp.float32) ** 2
            halves.append(-kernel_rate * jnp.sum(squares, axis=1, keepdims=True))
            new_ref[i * own : (i + 1) * own, :] = halves[-1]
    if prior_count:
        at = 0
        for prior_ref in prior_refs:
            image_ref[:, at : at + prior_ref.shape[1]] = prior_ref[...]
            at += prior_ref.shape[1]
    else:
        image_ref[...] = jnp.zeros_like(image_ref)
        if has_side:
            image_ref[:, :own] = (noise_level - 1.0 / STEP) * side_ref[...]
    for j, col_ref in enumerate(col_refs):
        field = unpack_rows(col_ref, probes, own, 0)
        norms = unpack_rows(col_ref, probes, own, 1).astype(jnp.float32)
        col_half = -kernel_rate * (norms[0:1] + norms[1:2] + norms[2:3])
        for i, row_ref in enumerate(row_refs):
            for k in range(own // CHUNK):
                part = slice(k * CHUNK, (k + 1) * CHUNK)
                place = slice(i * own + k * CHUNK, i * own + (k + 1) * CHUNK)
                cross = lax.dot_general(
                    row_ref[part, :], col_ref[:own, :], (((1,), (1,)), ((), ())), preferred_element_type=jnp.float32
                )
                kern = jnp.exp(2.0 * kernel_rate * cross + halves[i][part, :] + col_half).astype(jnp.bfloat16)
                tile_ref[place, j * own : (j + 1) * own] = kern
                image_ref[:, place] += lax.dot_general(
                    field, kern, (((1,), (1,)), ((), ())), preferred_element_type=jnp.float32
                )


def build(rows, cols, own, probes, halves=(), prior=(), side=None, weight=64):
    features = rows[0].shape[1]
    height, width = len(rows) * own, len(cols) * own
    counts = (len(rows), len(cols), len(halves), len(prior), side is not None)
    out_shape = [
        pltpu.VMEM((height, width), jnp.bfloat16),
        jax.ShapeDtypeStruct((probes, height), jnp.float32),
    ]
    if not halves:
        out_shape.append(jax.ShapeDtypeStruct((height, 1), jnp.float32))
    args = [*rows, *cols, *halves, *prior] + ([] if side is None else [side])
    return pl.pallas_call(
        functools.partial(tile_kernel, counts, probes),
        out_shape=out_shape,
        compiler_params=pltpu.CompilerParams(vmem_limit_bytes=8 << 20),
        cost_estimate=pl.CostEstimate(
            flops=height * width * features * weight // 8, bytes_accessed=1 << 10, transcendentals=0
        ),
        name="build_tile",
    )(*args)


def share_kernel(own, image_ref, *out_refs):
    probes = image_ref.shape[0]
    for k, out_ref in enumerate(out_refs, 1):
        for i in range(len(ROWS)):
            high, middle, _ = split(image_ref[:, i * own : (i + 1) * own])
            out_ref[i * probes : (i + 1) * probes, :] = high
            if i == k:
                out_ref[len(ROWS) * probes :, :] = middle


def share(image, own):
    probes = image.shape[0]
    height = (len(ROWS) + 1) * probes
    return pl.pallas_call(
        functools.partial(share_kernel, own),
        out_shape=[jax.ShapeDtypeStruct((height, own), jnp.bfloat16)] * (len(ROWS) - 1),
        compiler_params=pltpu.CompilerParams(vmem_limit_bytes=4 << 20),
        name="share",
    )(image)


def rho_kernel(own, *refs):
    parts, (rho_ref, narrow_ref) = refs[: len(ROWS)], refs[len(ROWS) :]
    probes = rho_ref.shape[0]
    for j, p in enumerate(ROWS):
        at = j * own
        piece = parts[0][:, at : at + own]
        for s, part in zip(ROWS[1:], parts[1:]):
            at = ROWS.index((p[0] ^ s[0], p[1] ^ s[1])) * probes
            piece = piece + part[at : at + probes, :].astype(jnp.float32)
            if p == HERE:
                piece = piece + part[len(ROWS) * probes :, :].astype(jnp.float32)
        rho = -STEP * piece
        if p == HERE:
            rho_ref[...] = rho
        high, low, _ = split(rho)
        narrow_ref[:probes, j * own : (j + 1) * own] = high
        narrow_ref[probes:, j * own : (j + 1) * own] = low


def sum_rows(parts, own):
    probes, rows = parts[0].shape
    return pl.pallas_call(
        functools.partial(rho_kernel, own),
        out_shape=[
            jax.ShapeDtypeStruct((probes, own), jnp.float32),
            jax.ShapeDtypeStruct((2 * probes, rows), jnp.bfloat16),
        ],
        compiler_params=pltpu.CompilerParams(vmem_limit_bytes=4 << 20),
        name="sum_rows",
    )(*parts)


def second_kernel(own, half, places, narrow_ref, *refs):
    tiles, out_ref = refs[: len(places)], refs[len(places)]
    probes = out_ref.shape[0]
    for j, (h, m) in enumerate(COLS):
        if h != half:
            continue
        part = 0.0
        for tile_ref, (top, left) in zip(tiles, places):
            at = j * own - left
            if 0 <= at < tile_ref.shape[1]:
                part = part + jnp.dot(
                    narrow_ref[:, top : top + tile_ref.shape[0]],
                    tile_ref[:, at : at + own],
                    preferred_element_type=jnp.float32,
                )
        out_ref[:, m * own : (m + 1) * own] = part[:probes] + part[probes:]


def second_product(tiles, narrow, own, half):
    height, rows = narrow.shape
    cols = len(SQUARE) * own
    places = [(top, left) for _, top, left in tiles]
    return pl.pallas_call(
        functools.partial(second_kernel, own, half, places),
        in_specs=[pl.BlockSpec(memory_space=pltpu.VMEM)] * (1 + len(tiles)),
        out_shape=jax.ShapeDtypeStruct((height // 2, cols), jnp.float32),
        compiler_params=pltpu.CompilerParams(vmem_limit_bytes=8 << 20),
        cost_estimate=pl.CostEstimate(flops=rows * cols * 32, bytes_accessed=1 << 10, transcendentals=0),
        name="second_product",
    )(narrow, *[tile for tile, _, _ in tiles])


def merge_kernel(own, mine_ref, other_ref, *out_refs):
    for m, out_ref in enumerate(out_refs):
        here = slice(m * own, (m + 1) * own)
        out_ref[...] = mine_ref[:, here] + other_ref[:, here]


def merge(mine, other, own):
    return pl.pallas_call(
        functools.partial(merge_kernel, own),
        out_shape=[jax.ShapeDtypeStruct((mine.shape[0], own), jnp.float32)] * len(SQUARE),
        compiler_params=pltpu.CompilerParams(vmem_limit_bytes=4 << 20),
        name="merge",
    )(mine, other)


def sums_kernel(side_ref, rho_ref, *refs):
    shares, (image_ref, sums_ref) = refs[: len(SQUARE)], refs[len(SQUARE) :]
    side, rho = side_ref[...], rho_ref[...]
    image = noise_level * rho
    for share in shares:
        image = image + share[...]
    image_ref[...] = image
    total = lambda a, b: jnp.sum(a * b, axis=1, keepdims=True)
    lane = lax.broadcasted_iota(jnp.int32, (side.shape[0], LANES), 1)
    sums = 0.0
    for k, one in enumerate((total(side, side), total(side, rho), total(rho, rho), total(rho, image))):
        sums = jnp.where(lane == k, one, sums)
    sums = sums.T
    sums_ref[...] = jnp.concatenate([sums[k : k + 1] for k in range(LANES // sums.shape[1])], axis=1)


def local_sums(side, rho, shares):
    return pl.pallas_call(
        sums_kernel,
        out_shape=[
            jax.ShapeDtypeStruct(side.shape, jnp.float32),
            jax.ShapeDtypeStruct((1, LANES), jnp.float32),
        ],
        compiler_params=pltpu.CompilerParams(vmem_limit_bytes=4 << 20),
        name="local_sums",
    )(side, rho, *shares)


def finish_kernel(side_ref, rho_ref, image_ref, sums_ref, field_ref, residual_ref):
    side, rho, image = side_ref[...], rho_ref[...], image_ref[...]
    probes = side.shape[0]
    sums = jnp.sum(sums_ref[...], axis=0, keepdims=True)
    sums = jnp.concatenate([sums[:, k * probes : (k + 1) * probes] for k in range(4)] * 2, axis=0).T
    rr, side_rho, rho_rho, rho_image = (sums[:, k : k + 1] for k in range(4))
    curve = (rr - side_rho) / STEP
    alpha = rr / curve
    turn = alpha / STEP
    rest = 1.0 - turn
    rr_next = rest * rest * rr + 2.0 * rest * turn * side_rho + turn * turn * rho_rho
    gain = rest + rr_next / rr
    cross = (side_rho - rho_rho) / STEP
    curve = gain * gain * curve + 2.0 * gain * turn * cross + turn * turn * rho_image
    alpha_next = rr_next / curve
    direction = gain * side + turn * rho
    field_ref[...] = alpha * side + alpha_next * direction
    residual_ref[...] = rest * side + turn * rho - alpha_next * (gain / STEP * (side - rho) + turn * image)


def finish(side, rho, image, sums):
    return pl.pallas_call(
        finish_kernel,
        out_shape=[jax.ShapeDtypeStruct(side.shape, jnp.float32)] * 2,
        compiler_params=pltpu.CompilerParams(vmem_limit_bytes=4 << 20),
        name="finish",
    )(side, rho, image, sums)


def on_device(states, offsets, right_side):
    own, probes = right_side.shape
    side = right_side.T
    points = lax.dynamic_slice_in_dim(states, offsets[0], own, 0)
    with jax.named_scope("fetch_points"):
        message = pack(points, side.astype(jnp.bfloat16))
        rows = [points] + [swap(points, offset) for offset in ROWS[1:]]
        cols = [message] + [swap(message, offset) for offset in SQUARE[1:3]]
        first = [message, swap_core(message)]
        tile_a, image_a, half_a = build([points], first, own, probes, side=side, weight=1)
        (rows[1], rows[2]), image_a = lax.optimization_barrier(((rows[1], rows[2]), image_a))
        tile_b, image_b, half_b = build(rows[1:3], first, own, probes, weight=1)
        half = [half_a, half_b]
        again, image_b = lax.optimization_barrier((message, image_b))
        cols.append(swap(again, SQUARE[3]))

    with jax.named_scope("build_tiles"):
        cols[2], image_b = lax.optimization_barrier((cols[2], image_b))
        tile_c, image = build(rows[:3], cols[2:3], own, probes, half, [image_a, image_b])
        other_z = swap_core(cols[2])
        cols[1], image = lax.optimization_barrier((cols[1], image))
        tile_d, image = build(rows[:3], cols[1:2], own, probes, half, [image])
        other_y = swap_core(cols[1])
        others = [other_y, other_z]
        tile_e, image = build(rows[:3], [other_z], own, probes, half, [image])
        other_y, image = lax.optimization_barrier((other_y, image))
        tile_i, image = build(rows[:3], [other_y], own, probes, half, [image])
        rows[3], image = lax.optimization_barrier((rows[3], image))
        tile_f, image_far, half_far = build([rows[3]], first + cols[1:3] + others, own, probes)
        cols[3], image_far = lax.optimization_barrier((cols[3], image_far))
        last = swap_core(cols[3])
        half.append(half_far)
        tile_g, image = build(rows, [cols[3]], own, probes, half, [image, image_far])
        tile_h, image = build(rows, [last], own, probes, half, [image])
        tiles = [
            (tile_a, 0, 0),
            (tile_b, own, 0),
            (tile_d, 0, 2 * own),
            (tile_c, 0, 3 * own),
            (tile_i, 0, 4 * own),
            (tile_e, 0, 5 * own),
            (tile_f, 3 * own, 0),
            (tile_g, 0, 6 * own),
            (tile_h, 0, 7 * own),
        ]

    with jax.named_scope("sum_over_rows"):
        parts = [image] + swap_each(share(image, own), ROWS[1:])

    rho, narrow = sum_rows(parts, own)
    other = second_product(tiles, narrow, own, 1)
    narrow, other = lax.optimization_barrier((narrow, other))
    mine = second_product(tiles, narrow, own, 0)

    with jax.named_scope("sum_over_columns"):
        blocks = merge(mine, swap_core(other), own)
        shares = [blocks[0]] + swap_each(blocks[1:], SQUARE[1:])

    with jax.named_scope("final_sums"):
        image, sums = local_sums(side, rho, shares)
        sums = jnp.broadcast_to(sums, (NY * NZ * NC, LANES))
        sums = lax.all_to_all(sums, ("y", "z", "c"), 0, 0, tiled=True)

    field, residual = finish(side, rho, image, sums)
    return field.T, residual.T


def solution(mesh):
    fine = Mesh(mesh.devices.reshape(NY, NZ, NC, NX), ("y", "z", "c", "x"))
    rows = ("y", "z", "c")
    in_specs = (P(rows, None), P(rows), P(rows, "x"))
    out_specs = (P(rows, "x"), P(rows, "x"))
    return jax.shard_map(on_device, mesh=fine, in_specs=in_specs, out_specs=out_specs, check_vma=False)
```

```python
import functools

import jax
import jax.numpy as jnp
from jax import lax
from jax.experimental import pallas as pl
from jax.experimental.pallas import tpu as pltpu
from jax.sharding import Mesh
from jax.sharding import PartitionSpec as P

NY, NZ, NC, NX = 4, 4, 2, 4
LANES = 128
CHUNK = 256
HERE = (0, 0)
ROWS = (HERE, (1, 0), (0, 1), (1, 1))
SQUARE = (HERE, (3, 0), (0, 3), (3, 3))
COLS = ((0, 0), (1, 0), (0, 1), (0, 2), (1, 1), (1, 2), (0, 3), (1, 3))

noise_level = 1.0
kernel_rate = 0.5
STEP = 1.0 / (1.0 + noise_level)


def swap(value, offset):
    pairs = []
    for y in range(NY):
        for z in range(NZ):
            pairs.append((y * NZ + z, (y ^ offset[0]) * NZ + (z ^ offset[1])))
    return lax.ppermute(value, ("y", "z"), pairs)


def swap_each(values, offsets):
    received = [swap(value, offset) for value, offset in reversed(list(zip(values, offsets)))]
    return received[::-1]


def swap_core(value):
    return lax.ppermute(value, "c", [(0, 1), (1, 0)])


def split(value):
    high = value.astype(jnp.bfloat16)
    rest = value - high.astype(jnp.float32)
    middle = rest.astype(jnp.bfloat16)
    return high, middle, (rest - middle.astype(jnp.float32)).astype(jnp.bfloat16)


def pack_kernel(points_ref, side_ref, out_ref):
    own, width = points_ref.shape
    probes = side_ref.shape[0]
    out_ref[:own, :] = points_ref[...]
    high, middle, _ = split(points_ref[...].astype(jnp.float32) ** 2)
    ones = jnp.ones((probes, width), jnp.bfloat16)
    norms = 0.0
    for term in (high, middle):
        norms = norms + lax.dot_general(ones, term, (((1,), (1,)), ((), ())), preferred_element_type=jnp.float32)
    high, middle, low = split(norms)
    row = lax.broadcasted_iota(jnp.int32, norms.shape, 0)
    norms = jnp.where(row == 0, high.astype(jnp.float32), jnp.where(row == 1, middle.astype(jnp.float32), low.astype(jnp.float32)))
    at = own
    for part in (side_ref[...], norms.astype(jnp.bfloat16)):
        for j in range(own // width):
            out_ref[at : at + probes, :] = part[:, j * width : (j + 1) * width]
            at += probes


def pack(points, side):
    own, width = points.shape
    extra = side.shape[0] * 2 * own // width
    return pl.pallas_call(
        pack_kernel,
        out_shape=jax.ShapeDtypeStruct((own + extra, width), jnp.bfloat16),
        compiler_params=pltpu.CompilerParams(vmem_limit_bytes=8 << 20),
        name="pack",
    )(points, side)


def unpack_rows(message, probes, own, term):
    width = message.shape[1]
    count = own // width
    at = own + term * count * probes
    return jnp.concatenate([message[at + j * probes : at + (j + 1) * probes] for j in range(count)], axis=1)


def tile_kernel(counts, probes, *refs):
    rows_count, cols_count, known_halves, prior_count, has_side = counts
    refs = list(refs)
    row_refs = [refs.pop(0) for _ in range(rows_count)]
    col_refs = [refs.pop(0) for _ in range(cols_count)]
    half_refs = [refs.pop(0) for _ in range(known_halves)]
    prior_refs = [refs.pop(0) for _ in range(prior_count)]
    side_ref = refs.pop(0) if has_side else None
    tile_ref, image_ref = refs.pop(0), refs.pop(0)
    own = tile_ref.shape[0] // rows_count
    if known_halves:
        pieces = []
        for half_ref in half_refs:
            pieces += [half_ref[j * own : (j + 1) * own, :] for j in range(half_ref.shape[0] // own)]
        halves = pieces
    else:
        new_ref = refs.pop(0)
        halves = []
        for i, row_ref in enumerate(row_refs):
            squares = row_ref[:own, :].astype(jnp.float32) ** 2
            halves.append(-kernel_rate * jnp.sum(squares, axis=1, keepdims=True))
            new_ref[i * own : (i + 1) * own, :] = halves[-1]
    if prior_count:
        at = 0
        for prior_ref in prior_refs:
            image_ref[:, at : at + prior_ref.shape[1]] = prior_ref[...]
            at += prior_ref.shape[1]
    else:
        image_ref[...] = jnp.zeros_like(image_ref)
        if has_side:
            image_ref[:, :own] = (noise_level - 1.0 / STEP) * side_ref[...]
    for j, col_ref in enumerate(col_refs):
        field = unpack_rows(col_ref, probes, own, 0)
        norms = unpack_rows(col_ref, probes, own, 1).astype(jnp.float32)
        col_half = -kernel_rate * (norms[0:1] + norms[1:2] + norms[2:3])
        for i, row_ref in enumerate(row_refs):
            for k in range(own // CHUNK):
                part = slice(k * CHUNK, (k + 1) * CHUNK)
                place = slice(i * own + k * CHUNK, i * own + (k + 1) * CHUNK)
                cross = lax.dot_general(
                    row_ref[part, :], col_ref[:own, :], (((1,), (1,)), ((), ())), preferred_element_type=jnp.float32
                )
                kern = jnp.exp(2.0 * kernel_rate * cross + halves[i][part, :] + col_half).astype(jnp.bfloat16)
                tile_ref[place, j * own : (j + 1) * own] = kern
                image_ref[:, place] += lax.dot_general(
                    field, kern, (((1,), (1,)), ((), ())), preferred_element_type=jnp.float32
                )


def build(rows, cols, own, probes, halves=(), prior=(), side=None, weight=64):
    features = rows[0].shape[1]
    height, width = len(rows) * own, len(cols) * own
    counts = (len(rows), len(cols), len(halves), len(prior), side is not None)
    out_shape = [
        pltpu.VMEM((height, width), jnp.bfloat16),
        jax.ShapeDtypeStruct((probes, height), jnp.float32),
    ]
    if not halves:
        out_shape.append(jax.ShapeDtypeStruct((height, 1), jnp.float32))
    args = [*rows, *cols, *halves, *prior] + ([] if side is None else [side])
    return pl.pallas_call(
        functools.partial(tile_kernel, counts, probes),
        out_shape=out_shape,
        compiler_params=pltpu.CompilerParams(vmem_limit_bytes=8 << 20),
        cost_estimate=pl.CostEstimate(
            flops=height * width * features * weight // 8, bytes_accessed=1 << 10, transcendentals=0
        ),
        name="build_tile",
    )(*args)


def share_kernel(own, image_ref, *out_refs):
    probes = image_ref.shape[0]
    for k, out_ref in enumerate(out_refs, 1):
        for i in range(len(ROWS)):
            high, middle, _ = split(image_ref[:, i * own : (i + 1) * own])
            out_ref[i * probes : (i + 1) * probes, :] = high
            if i == k:
                out_ref[len(ROWS) * probes :, :] = middle


def share(image, own):
    probes = image.shape[0]
    height = (len(ROWS) + 1) * probes
    return pl.pallas_call(
        functools.partial(share_kernel, own),
        out_shape=[jax.ShapeDtypeStruct((height, own), jnp.bfloat16)] * (len(ROWS) - 1),
        compiler_params=pltpu.CompilerParams(vmem_limit_bytes=4 << 20),
        name="share",
    )(image)


def rho_kernel(own, *refs):
    parts, (rho_ref, narrow_ref) = refs[: len(ROWS)], refs[len(ROWS) :]
    probes = rho_ref.shape[0]
    for j, p in enumerate(ROWS):
        at = j * own
        piece = parts[0][:, at : at + own]
        for s, part in zip(ROWS[1:], parts[1:]):
            at = ROWS.index((p[0] ^ s[0], p[1] ^ s[1])) * probes
            piece = piece + part[at : at + probes, :].astype(jnp.float32)
            if p == HERE:
                piece = piece + part[len(ROWS) * probes :, :].astype(jnp.float32)
        rho = -STEP * piece
        if p == HERE:
            rho_ref[...] = rho
        high, low, _ = split(rho)
        narrow_ref[:probes, j * own : (j + 1) * own] = high
        narrow_ref[probes:, j * own : (j + 1) * own] = low


def sum_rows(parts, own):
    probes, rows = parts[0].shape
    return pl.pallas_call(
        functools.partial(rho_kernel, own),
        out_shape=[
            jax.ShapeDtypeStruct((probes, own), jnp.float32),
            jax.ShapeDtypeStruct((2 * probes, rows), jnp.bfloat16),
        ],
        compiler_params=pltpu.CompilerParams(vmem_limit_bytes=4 << 20),
        name="sum_rows",
    )(*parts)


def second_kernel(own, half, places, narrow_ref, *refs):
    tiles, out_ref = refs[: len(places)], refs[len(places)]
    probes = out_ref.shape[0]
    for j, (h, m) in enumerate(COLS):
        if h != half:
            continue
        part = 0.0
        for tile_ref, (top, left) in zip(tiles, places):
            at = j * own - left
            if 0 <= at < tile_ref.shape[1]:
                part = part + jnp.dot(
                    narrow_ref[:, top : top + tile_ref.shape[0]],
                    tile_ref[:, at : at + own],
                    preferred_element_type=jnp.float32,
                )
        out_ref[:, m * own : (m + 1) * own] = part[:probes] + part[probes:]


def second_product(tiles, narrow, own, half):
    height, rows = narrow.shape
    cols = len(SQUARE) * own
    places = [(top, left) for _, top, left in tiles]
    return pl.pallas_call(
        functools.partial(second_kernel, own, half, places),
        in_specs=[pl.BlockSpec(memory_space=pltpu.VMEM)] * (1 + len(tiles)),
        out_shape=jax.ShapeDtypeStruct((height // 2, cols), jnp.float32),
        compiler_params=pltpu.CompilerParams(vmem_limit_bytes=8 << 20),
        cost_estimate=pl.CostEstimate(flops=rows * cols * 32, bytes_accessed=1 << 10, transcendentals=0),
        name="second_product",
    )(narrow, *[tile for tile, _, _ in tiles])


def merge_kernel(own, mine_ref, other_ref, *out_refs):
    for m, out_ref in enumerate(out_refs):
        here = slice(m * own, (m + 1) * own)
        out_ref[...] = mine_ref[:, here] + other_ref[:, here]


def merge(mine, other, own):
    return pl.pallas_call(
        functools.partial(merge_kernel, own),
        out_shape=[jax.ShapeDtypeStruct((mine.shape[0], own), jnp.float32)] * len(SQUARE),
        compiler_params=pltpu.CompilerParams(vmem_limit_bytes=4 << 20),
        name="merge",
    )(mine, other)


def sums_kernel(side_ref, rho_ref, *refs):
    shares, (image_ref, sums_ref) = refs[: len(SQUARE)], refs[len(SQUARE) :]
    side, rho = side_ref[...], rho_ref[...]
    image = noise_level * rho
    for share in shares:
        image = image + share[...]
    image_ref[...] = image
    total = lambda a, b: jnp.sum(a * b, axis=1, keepdims=True)
    lane = lax.broadcasted_iota(jnp.int32, (side.shape[0], LANES), 1)
    sums = 0.0
    for k, one in enumerate((total(side, side), total(side, rho), total(rho, rho), total(rho, image))):
        sums = jnp.where(lane == k, one, sums)
    sums = sums.T
    sums_ref[...] = jnp.concatenate([sums[k : k + 1] for k in range(LANES // sums.shape[1])], axis=1)


def local_sums(side, rho, shares):
    return pl.pallas_call(
        sums_kernel,
        out_shape=[
            jax.ShapeDtypeStruct(side.shape, jnp.float32),
            jax.ShapeDtypeStruct((1, LANES), jnp.float32),
        ],
        compiler_params=pltpu.CompilerParams(vmem_limit_bytes=4 << 20),
        name="local_sums",
    )(side, rho, *shares)


def finish_kernel(side_ref, rho_ref, image_ref, sums_ref, field_ref, residual_ref):
    side, rho, image = side_ref[...], rho_ref[...], image_ref[...]
    probes = side.shape[0]
    sums = jnp.sum(sums_ref[...], axis=0, keepdims=True)
    sums = jnp.concatenate([sums[:, k * probes : (k + 1) * probes] for k in range(4)] * 2, axis=0).T
    rr, side_rho, rho_rho, rho_image = (sums[:, k : k + 1] for k in range(4))
    curve = (rr - side_rho) / STEP
    alpha = rr / curve
    turn = alpha / STEP
    rest = 1.0 - turn
    rr_next = rest * rest * rr + 2.0 * rest * turn * side_rho + turn * turn * rho_rho
    gain = rest + rr_next / rr
    cross = (side_rho - rho_rho) / STEP
    curve = gain * gain * curve + 2.0 * gain * turn * cross + turn * turn * rho_image
    alpha_next = rr_next / curve
    direction = gain * side + turn * rho
    field_ref[...] = alpha * side + alpha_next * direction
    residual_ref[...] = rest * side + turn * rho - alpha_next * (gain / STEP * (side - rho) + turn * image)


def finish(side, rho, image, sums):
    return pl.pallas_call(
        finish_kernel,
        out_shape=[jax.ShapeDtypeStruct(side.shape, jnp.float32)] * 2,
        compiler_params=pltpu.CompilerParams(vmem_limit_bytes=4 << 20),
        name="finish",
    )(side, rho, image, sums)


def on_device(states, offsets, right_side):
    own, probes = right_side.shape
    side = right_side.T
    points = lax.dynamic_slice_in_dim(states, offsets[0], own, 0)
    with jax.named_scope("fetch_points"):
        message = pack(points, side.astype(jnp.bfloat16))
        rows = [points] + [swap(points, offset) for offset in ROWS[1:3]]
        cols = [message] + [swap(message, offset) for offset in SQUARE[1:]]
        first = [message, swap_core(message)]
        tile_a, image_a, half_a = build([points], first, own, probes, side=side, weight=1)
        (rows[1], rows[2], again), image_a = lax.optimization_barrier(((rows[1], rows[2], points), image_a))
        rows.append(swap(again, ROWS[3]))
        tile_b, image_b, half_b = build(rows[1:3], first, own, probes, weight=1)
        half = [half_a, half_b]

    with jax.named_scope("build_tiles"):
        cols[2], image_b = lax.optimization_barrier((cols[2], image_b))
        tile_c, image = build(rows[:3], cols[2:3], own, probes, half, [image_a, image_b])
        other_z = swap_core(cols[2])
        cols[1], image = lax.optimization_barrier((cols[1], image))
        tile_d, image = build(rows[:3], cols[1:2], own, probes, half, [image])
        other_y = swap_core(cols[1])
        others = [other_y, other_z]
        tile_e, image = build(rows[:3], [other_z], own, probes, half, [image])
        other_y, image = lax.optimization_barrier((other_y, image))
        tile_i, image = build(rows[:3], [other_y], own, probes, half, [image])
        rows[3], image = lax.optimization_barrier((rows[3], image))
        tile_f, image_far, half_far = build([rows[3]], first + cols[1:3] + others, own, probes)
        cols[3], image_far = lax.optimization_barrier((cols[3], image_far))
        last = swap_core(cols[3])
        half.append(half_far)
        tile_g, image = build(rows, [cols[3]], own, probes, half, [image, image_far])
        tile_h, image = build(rows, [last], own, probes, half, [image])
        tiles = [
            (tile_a, 0, 0),
            (tile_b, own, 0),
            (tile_d, 0, 2 * own),
            (tile_c, 0, 3 * own),
            (tile_i, 0, 4 * own),
            (tile_e, 0, 5 * own),
            (tile_f, 3 * own, 0),
            (tile_g, 0, 6 * own),
            (tile_h, 0, 7 * own),
        ]

    with jax.named_scope("sum_over_rows"):
        parts = [image] + swap_each(share(image, own), ROWS[1:])

    rho, narrow = sum_rows(parts, own)
    other = second_product(tiles, narrow, own, 1)
    narrow, other = lax.optimization_barrier((narrow, other))
    mine = second_product(tiles, narrow, own, 0)

    with jax.named_scope("sum_over_columns"):
        blocks = merge(mine, swap_core(other), own)
        shares = [blocks[0]] + swap_each(blocks[1:], SQUARE[1:])

    with jax.named_scope("final_sums"):
        image, sums = local_sums(side, rho, shares)
        sums = jnp.broadcast_to(sums, (NY * NZ * NC, LANES))
        sums = lax.all_to_all(sums, ("y", "z", "c"), 0, 0, tiled=True)

    field, residual = finish(side, rho, image, sums)
    return field.T, residual.T


def solution(mesh):
    fine = Mesh(mesh.devices.reshape(NY, NZ, NC, NX), ("y", "z", "c", "x"))
    rows = ("y", "z", "c")
    in_specs = (P(rows, None), P(rows), P(rows, "x"))
    out_specs = (P(rows, "x"), P(rows, "x"))
    return jax.shard_map(on_device, mesh=fine, in_specs=in_specs, out_specs=out_specs, check_vma=False)
```

```python
import functools

import jax
import jax.numpy as jnp
from jax import lax
from jax.experimental import pallas as pl
from jax.experimental.pallas import tpu as pltpu
from jax.sharding import Mesh
from jax.sharding import PartitionSpec as P

NY, NZ, NC, NX = 4, 4, 2, 4
LANES = 128
CHUNK = 256
HERE = (0, 0)
ROWS = (HERE, (1, 0), (0, 1), (1, 1))
SQUARE = (HERE, (3, 0), (0, 3), (3, 3))
COLS = ((0, 0), (1, 0), (0, 1), (0, 2), (1, 1), (1, 2), (0, 3), (1, 3))

noise_level = 1.0
kernel_rate = 0.5
STEP = 1.0 / (1.0 + noise_level)


def swap(value, offset):
    pairs = []
    for y in range(NY):
        for z in range(NZ):
            pairs.append((y * NZ + z, (y ^ offset[0]) * NZ + (z ^ offset[1])))
    return lax.ppermute(value, ("y", "z"), pairs)


def swap_each(values, offsets):
    received = [swap(value, offset) for value, offset in reversed(list(zip(values, offsets)))]
    return received[::-1]


def swap_core(value):
    return lax.ppermute(value, "c", [(0, 1), (1, 0)])


def split(value):
    high = value.astype(jnp.bfloat16)
    rest = value - high.astype(jnp.float32)
    middle = rest.astype(jnp.bfloat16)
    return high, middle, (rest - middle.astype(jnp.float32)).astype(jnp.bfloat16)


def pack_kernel(points_ref, side_ref, out_ref):
    own, width = points_ref.shape
    probes = side_ref.shape[0]
    out_ref[:own, :] = points_ref[...]
    high, middle, _ = split(points_ref[...].astype(jnp.float32) ** 2)
    ones = jnp.ones((probes, width), jnp.bfloat16)
    norms = 0.0
    for term in (high, middle):
        norms = norms + lax.dot_general(ones, term, (((1,), (1,)), ((), ())), preferred_element_type=jnp.float32)
    high, middle, low = split(norms)
    row = lax.broadcasted_iota(jnp.int32, norms.shape, 0)
    norms = jnp.where(row == 0, high.astype(jnp.float32), jnp.where(row == 1, middle.astype(jnp.float32), low.astype(jnp.float32)))
    at = own
    for part in (side_ref[...], norms.astype(jnp.bfloat16)):
        for j in range(own // width):
            out_ref[at : at + probes, :] = part[:, j * width : (j + 1) * width]
            at += probes


def pack(points, side):
    own, width = points.shape
    extra = side.shape[0] * 2 * own // width
    return pl.pallas_call(
        pack_kernel,
        out_shape=jax.ShapeDtypeStruct((own + extra, width), jnp.bfloat16),
        compiler_params=pltpu.CompilerParams(vmem_limit_bytes=8 << 20),
        name="pack",
    )(points, side)


def unpack_rows(message, probes, own, term):
    width = message.shape[1]
    count = own // width
    at = own + term * count * probes
    return jnp.concatenate([message[at + j * probes : at + (j + 1) * probes] for j in range(count)], axis=1)


def tile_kernel(counts, probes, *refs):
    rows_count, cols_count, known_halves, prior_count, has_side = counts
    refs = list(refs)
    row_refs = [refs.pop(0) for _ in range(rows_count)]
    col_refs = [refs.pop(0) for _ in range(cols_count)]
    half_refs = [refs.pop(0) for _ in range(known_halves)]
    prior_refs = [refs.pop(0) for _ in range(prior_count)]
    side_ref = refs.pop(0) if has_side else None
    tile_ref, image_ref = refs.pop(0), refs.pop(0)
    own = tile_ref.shape[0] // rows_count
    if known_halves:
        pieces = []
        for half_ref in half_refs:
            pieces += [half_ref[j * own : (j + 1) * own, :] for j in range(half_ref.shape[0] // own)]
        halves = pieces
    else:
        new_ref = refs.pop(0)
        halves = []
        for i, row_ref in enumerate(row_refs):
            squares = row_ref[:own, :].astype(jnp.float32) ** 2
            halves.append(-kernel_rate * jnp.sum(squares, axis=1, keepdims=True))
            new_ref[i * own : (i + 1) * own, :] = halves[-1]
    if prior_count:
        at = 0
        for prior_ref in prior_refs:
            image_ref[:, at : at + prior_ref.shape[1]] = prior_ref[...]
            at += prior_ref.shape[1]
    else:
        image_ref[...] = jnp.zeros_like(image_ref)
        if has_side:
            image_ref[:, :own] = (noise_level - 1.0 / STEP) * side_ref[...]
    for j, col_ref in enumerate(col_refs):
        field = unpack_rows(col_ref, probes, own, 0)
        norms = unpack_rows(col_ref, probes, own, 1).astype(jnp.float32)
        col_half = -kernel_rate * (norms[0:1] + norms[1:2] + norms[2:3])
        for i, row_ref in enumerate(row_refs):
            for k in range(own // CHUNK):
                part = slice(k * CHUNK, (k + 1) * CHUNK)
                place = slice(i * own + k * CHUNK, i * own + (k + 1) * CHUNK)
                cross = lax.dot_general(
                    row_ref[part, :], col_ref[:own, :], (((1,), (1,)), ((), ())), preferred_element_type=jnp.float32
                )
                kern = jnp.exp(2.0 * kernel_rate * cross + halves[i][part, :] + col_half).astype(jnp.bfloat16)
                tile_ref[place, j * own : (j + 1) * own] = kern
                image_ref[:, place] += lax.dot_general(
                    field, kern, (((1,), (1,)), ((), ())), preferred_element_type=jnp.float32
                )


def build(rows, cols, own, probes, halves=(), prior=(), side=None, weight=64):
    features = rows[0].shape[1]
    height, width = len(rows) * own, len(cols) * own
    counts = (len(rows), len(cols), len(halves), len(prior), side is not None)
    out_shape = [
        pltpu.VMEM((height, width), jnp.bfloat16),
        jax.ShapeDtypeStruct((probes, height), jnp.float32),
    ]
    if not halves:
        out_shape.append(jax.ShapeDtypeStruct((height, 1), jnp.float32))
    args = [*rows, *cols, *halves, *prior] + ([] if side is None else [side])
    return pl.pallas_call(
        functools.partial(tile_kernel, counts, probes),
        out_shape=out_shape,
        compiler_params=pltpu.CompilerParams(vmem_limit_bytes=8 << 20),
        cost_estimate=pl.CostEstimate(
            flops=height * width * features * weight // 8, bytes_accessed=1 << 10, transcendentals=0
        ),
        name="build_tile",
    )(*args)


def share_kernel(own, image_ref, *out_refs):
    probes = image_ref.shape[0]
    for k, out_ref in enumerate(out_refs, 1):
        for i in range(len(ROWS)):
            high, middle, _ = split(image_ref[:, i * own : (i + 1) * own])
            out_ref[i * probes : (i + 1) * probes, :] = high
            if i == k:
                out_ref[len(ROWS) * probes :, :] = middle


def share(image, own):
    probes = image.shape[0]
    height = (len(ROWS) + 1) * probes
    return pl.pallas_call(
        functools.partial(share_kernel, own),
        out_shape=[jax.ShapeDtypeStruct((height, own), jnp.bfloat16)] * (len(ROWS) - 1),
        compiler_params=pltpu.CompilerParams(vmem_limit_bytes=4 << 20),
        name="share",
    )(image)


def rho_kernel(own, *refs):
    parts, (rho_ref, narrow_ref) = refs[: len(ROWS)], refs[len(ROWS) :]
    probes = rho_ref.shape[0]
    for j, p in enumerate(ROWS):
        at = j * own
        piece = parts[0][:, at : at + own]
        for s, part in zip(ROWS[1:], parts[1:]):
            at = ROWS.index((p[0] ^ s[0], p[1] ^ s[1])) * probes
            piece = piece + part[at : at + probes, :].astype(jnp.float32)
            if p == HERE:
                piece = piece + part[len(ROWS) * probes :, :].astype(jnp.float32)
        rho = -STEP * piece
        if p == HERE:
            rho_ref[...] = rho
        high, low, _ = split(rho)
        narrow_ref[:probes, j * own : (j + 1) * own] = high
        narrow_ref[probes:, j * own : (j + 1) * own] = low


def sum_rows(parts, own):
    probes, rows = parts[0].shape
    return pl.pallas_call(
        functools.partial(rho_kernel, own),
        out_shape=[
            jax.ShapeDtypeStruct((probes, own), jnp.float32),
            jax.ShapeDtypeStruct((2 * probes, rows), jnp.bfloat16),
        ],
        compiler_params=pltpu.CompilerParams(vmem_limit_bytes=4 << 20),
        name="sum_rows",
    )(*parts)


def second_kernel(own, half, places, narrow_ref, *refs):
    tiles, out_ref = refs[: len(places)], refs[len(places)]
    probes = out_ref.shape[0]
    for j, (h, m) in enumerate(COLS):
        if h != half:
            continue
        part = 0.0
        for tile_ref, (top, left) in zip(tiles, places):
            at = j * own - left
            if 0 <= at < tile_ref.shape[1]:
                part = part + jnp.dot(
                    narrow_ref[:, top : top + tile_ref.shape[0]],
                    tile_ref[:, at : at + own],
                    preferred_element_type=jnp.float32,
                )
        out_ref[:, m * own : (m + 1) * own] = part[:probes] + part[probes:]


def second_product(tiles, narrow, own, half):
    height, rows = narrow.shape
    cols = len(SQUARE) * own
    places = [(top, left) for _, top, left in tiles]
    return pl.pallas_call(
        functools.partial(second_kernel, own, half, places),
        in_specs=[pl.BlockSpec(memory_space=pltpu.VMEM)] * (1 + len(tiles)),
        out_shape=jax.ShapeDtypeStruct((height // 2, cols), jnp.float32),
        compiler_params=pltpu.CompilerParams(vmem_limit_bytes=8 << 20),
        cost_estimate=pl.CostEstimate(flops=rows * cols * 32, bytes_accessed=1 << 10, transcendentals=0),
        name="second_product",
    )(narrow, *[tile for tile, _, _ in tiles])


def merge_kernel(own, mine_ref, other_ref, *out_refs):
    for m, out_ref in enumerate(out_refs):
        here = slice(m * own, (m + 1) * own)
        out_ref[...] = mine_ref[:, here] + other_ref[:, here]


def merge(mine, other, own):
    return pl.pallas_call(
        functools.partial(merge_kernel, own),
        out_shape=[jax.ShapeDtypeStruct((mine.shape[0], own), jnp.float32)] * len(SQUARE),
        compiler_params=pltpu.CompilerParams(vmem_limit_bytes=4 << 20),
        name="merge",
    )(mine, other)


def sums_kernel(side_ref, rho_ref, *refs):
    shares, (image_ref, sums_ref) = refs[: len(SQUARE)], refs[len(SQUARE) :]
    side, rho = side_ref[...], rho_ref[...]
    image = noise_level * rho
    for share in shares:
        image = image + share[...]
    image_ref[...] = image
    total = lambda a, b: jnp.sum(a * b, axis=1, keepdims=True)
    lane = lax.broadcasted_iota(jnp.int32, (side.shape[0], LANES), 1)
    sums = 0.0
    for k, one in enumerate((total(side, side), total(side, rho), total(rho, rho), total(rho, image))):
        sums = jnp.where(lane == k, one, sums)
    sums = sums.T
    sums_ref[...] = jnp.concatenate([sums[k : k + 1] for k in range(LANES // sums.shape[1])], axis=1)


def local_sums(side, rho, shares):
    return pl.pallas_call(
        sums_kernel,
        out_shape=[
            jax.ShapeDtypeStruct(side.shape, jnp.float32),
            jax.ShapeDtypeStruct((1, LANES), jnp.float32),
        ],
        compiler_params=pltpu.CompilerParams(vmem_limit_bytes=4 << 20),
        name="local_sums",
    )(side, rho, *shares)


def finish_kernel(side_ref, rho_ref, image_ref, sums_ref, field_ref, residual_ref):
    side, rho, image = side_ref[...], rho_ref[...], image_ref[...]
    probes = side.shape[0]
    sums = jnp.sum(sums_ref[...], axis=0, keepdims=True)
    sums = jnp.concatenate([sums[:, k * probes : (k + 1) * probes] for k in range(4)] * 2, axis=0).T
    rr, side_rho, rho_rho, rho_image = (sums[:, k : k + 1] for k in range(4))
    curve = (rr - side_rho) / STEP
    alpha = rr / curve
    turn = alpha / STEP
    rest = 1.0 - turn
    rr_next = rest * rest * rr + 2.0 * rest * turn * side_rho + turn * turn * rho_rho
    gain = rest + rr_next / rr
    cross = (side_rho - rho_rho) / STEP
    curve = gain * gain * curve + 2.0 * gain * turn * cross + turn * turn * rho_image
    alpha_next = rr_next / curve
    direction = gain * side + turn * rho
    field_ref[...] = alpha * side + alpha_next * direction
    residual_ref[...] = rest * side + turn * rho - alpha_next * (gain / STEP * (side - rho) + turn * image)


def finish(side, rho, image, sums):
    return pl.pallas_call(
        finish_kernel,
        out_shape=[jax.ShapeDtypeStruct(side.shape, jnp.float32)] * 2,
        compiler_params=pltpu.CompilerParams(vmem_limit_bytes=4 << 20),
        name="finish",
    )(side, rho, image, sums)


def on_device(states, offsets, right_side):
    own, probes = right_side.shape
    side = right_side.T
    points = lax.dynamic_slice_in_dim(states, offsets[0], own, 0)
    with jax.named_scope("fetch_points"):
        message = pack(points, side.astype(jnp.bfloat16))
        rows = [points] + [swap(points, offset) for offset in ROWS[1:3]]
        cols = [message] + [swap(message, offset) for offset in SQUARE[1:]]
        first = [message, swap_core(message)]
        tile_a, image_a, half_a = build([points], first, own, probes, side=side, weight=1)
        (rows[1], rows[2]), image_a = lax.optimization_barrier(((rows[1], rows[2]), image_a))
        tile_b, image_b, half_b = build(rows[1:3], first, own, probes, weight=1)
        half = [half_a, half_b]
        again, image_b = lax.optimization_barrier((points, image_b))
        rows.append(swap(again, ROWS[3]))

    with jax.named_scope("build_tiles"):
        cols[2], image_b = lax.optimization_barrier((cols[2], image_b))
        tile_c, image = build(rows[:3], cols[2:3], own, probes, half, [image_a, image_b])
        other_z = swap_core(cols[2])
        cols[1], image = lax.optimization_barrier((cols[1], image))
        tile_d, image = build(rows[:3], cols[1:2], own, probes, half, [image])
        other_y = swap_core(cols[1])
        others = [other_y, other_z]
        tile_e, image = build(rows[:3], [other_z], own, probes, half, [image])
        other_y, image = lax.optimization_barrier((other_y, image))
        tile_i, image = build(rows[:3], [other_y], own, probes, half, [image])
        rows[3], image = lax.optimization_barrier((rows[3], image))
        tile_f, image_far, half_far = build([rows[3]], first + cols[1:3] + others, own, probes)
        cols[3], image_far = lax.optimization_barrier((cols[3], image_far))
        last = swap_core(cols[3])
        half.append(half_far)
        tile_g, image = build(rows, [cols[3]], own, probes, half, [image, image_far])
        tile_h, image = build(rows, [last], own, probes, half, [image])
        tiles = [
            (tile_a, 0, 0),
            (tile_b, own, 0),
            (tile_d, 0, 2 * own),
            (tile_c, 0, 3 * own),
            (tile_i, 0, 4 * own),
            (tile_e, 0, 5 * own),
            (tile_f, 3 * own, 0),
            (tile_g, 0, 6 * own),
            (tile_h, 0, 7 * own),
        ]

    with jax.named_scope("sum_over_rows"):
        parts = [image] + swap_each(share(image, own), ROWS[1:])

    rho, narrow = sum_rows(parts, own)
    other = second_product(tiles, narrow, own, 1)
    narrow, other = lax.optimization_barrier((narrow, other))
    mine = second_product(tiles, narrow, own, 0)

    with jax.named_scope("sum_over_columns"):
        blocks = merge(mine, swap_core(other), own)
        shares = [blocks[0]] + swap_each(blocks[1:], SQUARE[1:])

    with jax.named_scope("final_sums"):
        image, sums = local_sums(side, rho, shares)
        sums = jnp.broadcast_to(sums, (NY * NZ * NC, LANES))
        sums = lax.all_to_all(sums, ("y", "z", "c"), 0, 0, tiled=True)

    field, residual = finish(side, rho, image, sums)
    return field.T, residual.T


def solution(mesh):
    fine = Mesh(mesh.devices.reshape(NY, NZ, NC, NX), ("y", "z", "c", "x"))
    rows = ("y", "z", "c")
    in_specs = (P(rows, None), P(rows), P(rows, "x"))
    out_specs = (P(rows, "x"), P(rows, "x"))
    return jax.shard_map(on_device, mesh=fine, in_specs=in_specs, out_specs=out_specs, check_vma=False)
```

```python
import functools

import jax
import jax.numpy as jnp
from jax import lax
from jax.experimental import pallas as pl
from jax.experimental.pallas import tpu as pltpu
from jax.sharding import Mesh
from jax.sharding import PartitionSpec as P

NY, NZ, NC, NX = 4, 4, 2, 4
LANES = 128
CHUNK = 256
HERE = (0, 0)
ROWS = (HERE, (1, 0), (0, 3), (1, 3))
SQUARE = (HERE, (3, 0), (0, 1), (3, 1))
COLS = ((0, 0), (1, 0), (0, 1), (0, 2), (1, 1), (1, 2), (0, 3), (1, 3))

noise_level = 1.0
kernel_rate = 0.5
STEP = 1.0 / (1.0 + noise_level)


def swap(value, offset):
    pairs = []
    for y in range(NY):
        for z in range(NZ):
            pairs.append((y * NZ + z, (y ^ offset[0]) * NZ + (z ^ offset[1])))
    return lax.ppermute(value, ("y", "z"), pairs)


def swap_each(values, offsets):
    received = [swap(value, offset) for value, offset in reversed(list(zip(values, offsets)))]
    return received[::-1]


def swap_core(value):
    return lax.ppermute(value, "c", [(0, 1), (1, 0)])


def split(value):
    high = value.astype(jnp.bfloat16)
    rest = value - high.astype(jnp.float32)
    middle = rest.astype(jnp.bfloat16)
    return high, middle, (rest - middle.astype(jnp.float32)).astype(jnp.bfloat16)


def pack_kernel(points_ref, side_ref, out_ref):
    own, width = points_ref.shape
    probes = side_ref.shape[0]
    out_ref[:own, :] = points_ref[...]
    high, middle, _ = split(points_ref[...].astype(jnp.float32) ** 2)
    ones = jnp.ones((probes, width), jnp.bfloat16)
    norms = 0.0
    for term in (high, middle):
        norms = norms + lax.dot_general(ones, term, (((1,), (1,)), ((), ())), preferred_element_type=jnp.float32)
    high, middle, low = split(norms)
    row = lax.broadcasted_iota(jnp.int32, norms.shape, 0)
    norms = jnp.where(row == 0, high.astype(jnp.float32), jnp.where(row == 1, middle.astype(jnp.float32), low.astype(jnp.float32)))
    at = own
    for part in (side_ref[...], norms.astype(jnp.bfloat16)):
        for j in range(own // width):
            out_ref[at : at + probes, :] = part[:, j * width : (j + 1) * width]
            at += probes


def pack(points, side):
    own, width = points.shape
    extra = side.shape[0] * 2 * own // width
    return pl.pallas_call(
        pack_kernel,
        out_shape=jax.ShapeDtypeStruct((own + extra, width), jnp.bfloat16),
        compiler_params=pltpu.CompilerParams(vmem_limit_bytes=8 << 20),
        name="pack",
    )(points, side)


def unpack_rows(message, probes, own, term):
    width = message.shape[1]
    count = own // width
    at = own + term * count * probes
    return jnp.concatenate([message[at + j * probes : at + (j + 1) * probes] for j in range(count)], axis=1)


def tile_kernel(counts, probes, *refs):
    rows_count, cols_count, known_halves, prior_count, has_side = counts
    refs = list(refs)
    row_refs = [refs.pop(0) for _ in range(rows_count)]
    col_refs = [refs.pop(0) for _ in range(cols_count)]
    half_refs = [refs.pop(0) for _ in range(known_halves)]
    prior_refs = [refs.pop(0) for _ in range(prior_count)]
    side_ref = refs.pop(0) if has_side else None
    tile_ref, image_ref = refs.pop(0), refs.pop(0)
    own = tile_ref.shape[0] // rows_count
    if known_halves:
        pieces = []
        for half_ref in half_refs:
            pieces += [half_ref[j * own : (j + 1) * own, :] for j in range(half_ref.shape[0] // own)]
        halves = pieces
    else:
        new_ref = refs.pop(0)
        halves = []
        for i, row_ref in enumerate(row_refs):
            squares = row_ref[:own, :].astype(jnp.float32) ** 2
            halves.append(-kernel_rate * jnp.sum(squares, axis=1, keepdims=True))
            new_ref[i * own : (i + 1) * own, :] = halves[-1]
    if prior_count:
        at = 0
        for prior_ref in prior_refs:
            image_ref[:, at : at + prior_ref.shape[1]] = prior_ref[...]
            at += prior_ref.shape[1]
    else:
        image_ref[...] = jnp.zeros_like(image_ref)
        if has_side:
            image_ref[:, :own] = (noise_level - 1.0 / STEP) * side_ref[...]
    for j, col_ref in enumerate(col_refs):
        field = unpack_rows(col_ref, probes, own, 0)
        norms = unpack_rows(col_ref, probes, own, 1).astype(jnp.float32)
        col_half = -kernel_rate * (norms[0:1] + norms[1:2] + norms[2:3])
        for i, row_ref in enumerate(row_refs):
            for k in range(own // CHUNK):
                part = slice(k * CHUNK, (k + 1) * CHUNK)
                place = slice(i * own + k * CHUNK, i * own + (k + 1) * CHUNK)
                cross = lax.dot_general(
                    row_ref[part, :], col_ref[:own, :], (((1,), (1,)), ((), ())), preferred_element_type=jnp.float32
                )
                kern = jnp.exp(2.0 * kernel_rate * cross + halves[i][part, :] + col_half).astype(jnp.bfloat16)
                tile_ref[place, j * own : (j + 1) * own] = kern
                image_ref[:, place] += lax.dot_general(
                    field, kern, (((1,), (1,)), ((), ())), preferred_element_type=jnp.float32
                )


def build(rows, cols, own, probes, halves=(), prior=(), side=None, weight=64):
    features = rows[0].shape[1]
    height, width = len(rows) * own, len(cols) * own
    counts = (len(rows), len(cols), len(halves), len(prior), side is not None)
    out_shape = [
        pltpu.VMEM((height, width), jnp.bfloat16),
        jax.ShapeDtypeStruct((probes, height), jnp.float32),
    ]
    if not halves:
        out_shape.append(jax.ShapeDtypeStruct((height, 1), jnp.float32))
    args = [*rows, *cols, *halves, *prior] + ([] if side is None else [side])
    return pl.pallas_call(
        functools.partial(tile_kernel, counts, probes),
        out_shape=out_shape,
        compiler_params=pltpu.CompilerParams(vmem_limit_bytes=8 << 20),
        cost_estimate=pl.CostEstimate(
            flops=height * width * features * weight // 8, bytes_accessed=1 << 10, transcendentals=0
        ),
        name="build_tile",
    )(*args)


def share_kernel(own, image_ref, *out_refs):
    probes = image_ref.shape[0]
    for k, out_ref in enumerate(out_refs, 1):
        for i in range(len(ROWS)):
            high, middle, _ = split(image_ref[:, i * own : (i + 1) * own])
            out_ref[i * probes : (i + 1) * probes, :] = high
            if i == k:
                out_ref[len(ROWS) * probes :, :] = middle


def share(image, own):
    probes = image.shape[0]
    height = (len(ROWS) + 1) * probes
    return pl.pallas_call(
        functools.partial(share_kernel, own),
        out_shape=[jax.ShapeDtypeStruct((height, own), jnp.bfloat16)] * (len(ROWS) - 1),
        compiler_params=pltpu.CompilerParams(vmem_limit_bytes=4 << 20),
        name="share",
    )(image)


def rho_kernel(own, *refs):
    parts, (rho_ref, narrow_ref) = refs[: len(ROWS)], refs[len(ROWS) :]
    probes = rho_ref.shape[0]
    for j, p in enumerate(ROWS):
        at = j * own
        piece = parts[0][:, at : at + own]
        for s, part in zip(ROWS[1:], parts[1:]):
            at = ROWS.index((p[0] ^ s[0], p[1] ^ s[1])) * probes
            piece = piece + part[at : at + probes, :].astype(jnp.float32)
            if p == HERE:
                piece = piece + part[len(ROWS) * probes :, :].astype(jnp.float32)
        rho = -STEP * piece
        if p == HERE:
            rho_ref[...] = rho
        high, low, _ = split(rho)
        narrow_ref[:probes, j * own : (j + 1) * own] = high
        narrow_ref[probes:, j * own : (j + 1) * own] = low


def sum_rows(parts, own):
    probes, rows = parts[0].shape
    return pl.pallas_call(
        functools.partial(rho_kernel, own),
        out_shape=[
            jax.ShapeDtypeStruct((probes, own), jnp.float32),
            jax.ShapeDtypeStruct((2 * probes, rows), jnp.bfloat16),
        ],
        compiler_params=pltpu.CompilerParams(vmem_limit_bytes=4 << 20),
        name="sum_rows",
    )(*parts)


def second_kernel(own, half, places, narrow_ref, *refs):
    tiles, out_ref = refs[: len(places)], refs[len(places)]
    probes = out_ref.shape[0]
    for j, (h, m) in enumerate(COLS):
        if h != half:
            continue
        part = 0.0
        for tile_ref, (top, left) in zip(tiles, places):
            at = j * own - left
            if 0 <= at < tile_ref.shape[1]:
                part = part + jnp.dot(
                    narrow_ref[:, top : top + tile_ref.shape[0]],
                    tile_ref[:, at : at + own],
                    preferred_element_type=jnp.float32,
                )
        out_ref[:, m * own : (m + 1) * own] = part[:probes] + part[probes:]


def second_product(tiles, narrow, own, half):
    height, rows = narrow.shape
    cols = len(SQUARE) * own
    places = [(top, left) for _, top, left in tiles]
    return pl.pallas_call(
        functools.partial(second_kernel, own, half, places),
        in_specs=[pl.BlockSpec(memory_space=pltpu.VMEM)] * (1 + len(tiles)),
        out_shape=jax.ShapeDtypeStruct((height // 2, cols), jnp.float32),
        compiler_params=pltpu.CompilerParams(vmem_limit_bytes=8 << 20),
        cost_estimate=pl.CostEstimate(flops=rows * cols * 32, bytes_accessed=1 << 10, transcendentals=0),
        name="second_product",
    )(narrow, *[tile for tile, _, _ in tiles])


def merge_kernel(own, mine_ref, other_ref, *out_refs):
    for m, out_ref in enumerate(out_refs):
        here = slice(m * own, (m + 1) * own)
        out_ref[...] = mine_ref[:, here] + other_ref[:, here]


def merge(mine, other, own):
    return pl.pallas_call(
        functools.partial(merge_kernel, own),
        out_shape=[jax.ShapeDtypeStruct((mine.shape[0], own), jnp.float32)] * len(SQUARE),
        compiler_params=pltpu.CompilerParams(vmem_limit_bytes=4 << 20),
        name="merge",
    )(mine, other)


def sums_kernel(side_ref, rho_ref, *refs):
    shares, (image_ref, sums_ref) = refs[: len(SQUARE)], refs[len(SQUARE) :]
    side, rho = side_ref[...], rho_ref[...]
    image = noise_level * rho
    for share in shares:
        image = image + share[...]
    image_ref[...] = image
    total = lambda a, b: jnp.sum(a * b, axis=1, keepdims=True)
    lane = lax.broadcasted_iota(jnp.int32, (side.shape[0], LANES), 1)
    sums = 0.0
    for k, one in enumerate((total(side, side), total(side, rho), total(rho, rho), total(rho, image))):
        sums = jnp.where(lane == k, one, sums)
    sums = sums.T
    sums_ref[...] = jnp.concatenate([sums[k : k + 1] for k in range(LANES // sums.shape[1])], axis=1)


def local_sums(side, rho, shares):
    return pl.pallas_call(
        sums_kernel,
        out_shape=[
            jax.ShapeDtypeStruct(side.shape, jnp.float32),
            jax.ShapeDtypeStruct((1, LANES), jnp.float32),
        ],
        compiler_params=pltpu.CompilerParams(vmem_limit_bytes=4 << 20),
        name="local_sums",
    )(side, rho, *shares)


def finish_kernel(side_ref, rho_ref, image_ref, sums_ref, field_ref, residual_ref):
    side, rho, image = side_ref[...], rho_ref[...], image_ref[...]
    probes = side.shape[0]
    sums = jnp.sum(sums_ref[...], axis=0, keepdims=True)
    sums = jnp.concatenate([sums[:, k * probes : (k + 1) * probes] for k in range(4)] * 2, axis=0).T
    rr, side_rho, rho_rho, rho_image = (sums[:, k : k + 1] for k in range(4))
    curve = (rr - side_rho) / STEP
    alpha = rr / curve
    turn = alpha / STEP
    rest = 1.0 - turn
    rr_next = rest * rest * rr + 2.0 * rest * turn * side_rho + turn * turn * rho_rho
    gain = rest + rr_next / rr
    cross = (side_rho - rho_rho) / STEP
    curve = gain * gain * curve + 2.0 * gain * turn * cross + turn * turn * rho_image
    alpha_next = rr_next / curve
    direction = gain * side + turn * rho
    field_ref[...] = alpha * side + alpha_next * direction
    residual_ref[...] = rest * side + turn * rho - alpha_next * (gain / STEP * (side - rho) + turn * image)


def finish(side, rho, image, sums):
    return pl.pallas_call(
        finish_kernel,
        out_shape=[jax.ShapeDtypeStruct(side.shape, jnp.float32)] * 2,
        compiler_params=pltpu.CompilerParams(vmem_limit_bytes=4 << 20),
        name="finish",
    )(side, rho, image, sums)


def on_device(states, offsets, right_side):
    own, probes = right_side.shape
    side = right_side.T
    points = lax.dynamic_slice_in_dim(states, offsets[0], own, 0)
    with jax.named_scope("fetch_points"):
        message = pack(points, side.astype(jnp.bfloat16))
        rows = [points] + [swap(points, offset) for offset in ROWS[1:3]]
        cols = [message] + [swap(message, offset) for offset in SQUARE[1:]]
        first = [message, swap_core(message)]
        tile_a, image_a, half_a = build([points], first, own, probes, side=side, weight=1)
        (rows[1], rows[2], again), image_a = lax.optimization_barrier(((rows[1], rows[2], points), image_a))
        rows.append(swap(again, ROWS[3]))
        tile_b, image_b, half_b = build(rows[1:3], first, own, probes, weight=1)
        half = [half_a, half_b]

    with jax.named_scope("build_tiles"):
        cols[2], image_b = lax.optimization_barrier((cols[2], image_b))
        tile_c, image = build(rows[:3], cols[2:3], own, probes, half, [image_a, image_b])
        other_z = swap_core(cols[2])
        cols[1], image = lax.optimization_barrier((cols[1], image))
        tile_d, image = build(rows[:3], cols[1:2], own, probes, half, [image])
        other_y = swap_core(cols[1])
        others = [other_y, other_z]
        tile_e, image = build(rows[:3], [other_z], own, probes, half, [image])
        other_y, image = lax.optimization_barrier((other_y, image))
        tile_i, image = build(rows[:3], [other_y], own, probes, half, [image])
        rows[3], image = lax.optimization_barrier((rows[3], image))
        tile_f, image_far, half_far = build([rows[3]], first + cols[1:3] + others, own, probes)
        cols[3], image_far = lax.optimization_barrier((cols[3], image_far))
        last = swap_core(cols[3])
        half.append(half_far)
        tile_g, image = build(rows, [cols[3]], own, probes, half, [image, image_far])
        tile_h, image = build(rows, [last], own, probes, half, [image])
        tiles = [
            (tile_a, 0, 0),
            (tile_b, own, 0),
            (tile_d, 0, 2 * own),
            (tile_c, 0, 3 * own),
            (tile_i, 0, 4 * own),
            (tile_e, 0, 5 * own),
            (tile_f, 3 * own, 0),
            (tile_g, 0, 6 * own),
            (tile_h, 0, 7 * own),
        ]

    with jax.named_scope("sum_over_rows"):
        parts = [image] + swap_each(share(image, own), ROWS[1:])

    rho, narrow = sum_rows(parts, own)
    other = second_product(tiles, narrow, own, 1)
    narrow, other = lax.optimization_barrier((narrow, other))
    mine = second_product(tiles, narrow, own, 0)

    with jax.named_scope("sum_over_columns"):
        blocks = merge(mine, swap_core(other), own)
        shares = [blocks[0]] + swap_each(blocks[1:], SQUARE[1:])

    with jax.named_scope("final_sums"):
        image, sums = local_sums(side, rho, shares)
        sums = jnp.broadcast_to(sums, (NY * NZ * NC, LANES))
        sums = lax.all_to_all(sums, ("y", "z", "c"), 0, 0, tiled=True)

    field, residual = finish(side, rho, image, sums)
    return field.T, residual.T


def solution(mesh):
    fine = Mesh(mesh.devices.reshape(NY, NZ, NC, NX), ("y", "z", "c", "x"))
    rows = ("y", "z", "c")
    in_specs = (P(rows, None), P(rows), P(rows, "x"))
    out_specs = (P(rows, "x"), P(rows, "x"))
    return jax.shard_map(on_device, mesh=fine, in_specs=in_specs, out_specs=out_specs, check_vma=False)
```

```python
import functools

import jax
import jax.numpy as jnp
from jax import lax
from jax.experimental import pallas as pl
from jax.experimental.pallas import tpu as pltpu
from jax.sharding import Mesh
from jax.sharding import PartitionSpec as P

NY, NZ, NC, NX = 4, 4, 2, 4
LANES = 128
ALIGN = 16
CHUNK = 256
HERE = (0, 0)
ROWS = (HERE, (1, 0), (0, 1), (1, 1))
SQUARE = (HERE, (3, 0), (0, 3), (3, 3))
COLS = ((0, 0), (1, 0), (0, 1), (0, 2), (1, 1), (1, 2), (0, 3), (1, 3))

noise_level = 1.0
kernel_rate = 0.5
STEP = 1.0 / (1.0 + noise_level)


def swap(value, offset):
    pairs = []
    for y in range(NY):
        for z in range(NZ):
            pairs.append((y * NZ + z, (y ^ offset[0]) * NZ + (z ^ offset[1])))
    return lax.ppermute(value, ("y", "z"), pairs)


def swap_each(values, offsets):
    received = [swap(value, offset) for value, offset in reversed(list(zip(values, offsets)))]
    return received[::-1]


def swap_core(value):
    return lax.ppermute(value, "c", [(0, 1), (1, 0)])


def split(value):
    high = value.astype(jnp.bfloat16)
    rest = value - high.astype(jnp.float32)
    middle = rest.astype(jnp.bfloat16)
    return high, middle, (rest - middle.astype(jnp.float32)).astype(jnp.bfloat16)


def front_kernel(offset_ref, states_ref, side_from, points_ref, out_ref, window_ref, side_ref, sems):
    own, width = points_ref.shape
    probes = side_ref.shape[0]
    side_copy = pltpu.make_async_copy(side_from, side_ref, sems.at[0])
    side_copy.start()
    size = own + ALIGN
    offset = offset_ref[0]
    start = jnp.minimum(lax.div(offset, ALIGN) * ALIGN, states_ref.shape[0] - size)
    window_from = states_ref.at[pl.ds(pl.multiple_of(start, ALIGN), size), :]
    window_copy = pltpu.make_async_copy(window_from, window_ref, sems.at[1])
    window_copy.start()
    side_copy.wait()
    window_copy.wait()
    points = pltpu.roll(window_ref[...].astype(jnp.float32), lax.rem(size - (offset - start), size), 0)[:own]
    points_ref[...] = points.astype(jnp.bfloat16)
    out_ref[:own, :] = points.astype(jnp.bfloat16)
    high, middle, _ = split(points**2)
    ones = jnp.ones((probes, width), jnp.bfloat16)
    norms = 0.0
    for term in (high, middle):
        norms = norms + lax.dot_general(ones, term, (((1,), (1,)), ((), ())), preferred_element_type=jnp.float32)
    high, middle, low = split(norms)
    row = lax.broadcasted_iota(jnp.int32, norms.shape, 0)
    norms = jnp.where(row == 0, high.astype(jnp.float32), jnp.where(row == 1, middle.astype(jnp.float32), low.astype(jnp.float32)))
    at = own
    for part in (side_ref[...].astype(jnp.bfloat16), norms.astype(jnp.bfloat16)):
        for j in range(own // width):
            out_ref[at : at + probes, :] = part[:, j * width : (j + 1) * width]
            at += probes


def front(states, offsets, side):
    width = states.shape[1]
    probes, own = side.shape
    extra = probes * 2 * own // width
    return pl.pallas_call(
        front_kernel,
        in_specs=[
            pl.BlockSpec(memory_space=pltpu.SMEM),
            pl.BlockSpec(memory_space=pltpu.HBM),
            pl.BlockSpec(memory_space=pltpu.HBM),
        ],
        out_shape=[
            jax.ShapeDtypeStruct((own, width), jnp.bfloat16),
            jax.ShapeDtypeStruct((own + extra, width), jnp.bfloat16),
        ],
        scratch_shapes=[
            pltpu.VMEM((own + ALIGN, width), jnp.bfloat16),
            pltpu.VMEM((probes, own), jnp.float32),
            pltpu.SemaphoreType.DMA((2,)),
        ],
        compiler_params=pltpu.CompilerParams(vmem_limit_bytes=8 << 20),
        name="front",
    )(offsets, states, side)


def unpack_rows(message, probes, own, term):
    width = message.shape[1]
    count = own // width
    at = own + term * count * probes
    return jnp.concatenate([message[at + j * probes : at + (j + 1) * probes] for j in range(count)], axis=1)


def tile_kernel(counts, probes, *refs):
    rows_count, cols_count, known_halves, prior_count, has_side = counts
    refs = list(refs)
    row_refs = [refs.pop(0) for _ in range(rows_count)]
    col_refs = [refs.pop(0) for _ in range(cols_count)]
    half_refs = [refs.pop(0) for _ in range(known_halves)]
    prior_refs = [refs.pop(0) for _ in range(prior_count)]
    side_ref = refs.pop(0) if has_side else None
    tile_ref, image_ref = refs.pop(0), refs.pop(0)
    own = tile_ref.shape[0] // rows_count
    if known_halves:
        pieces = []
        for half_ref in half_refs:
            pieces += [half_ref[j * own : (j + 1) * own, :] for j in range(half_ref.shape[0] // own)]
        halves = pieces
    else:
        new_ref = refs.pop(0)
        halves = []
        for i, row_ref in enumerate(row_refs):
            squares = row_ref[:own, :].astype(jnp.float32) ** 2
            halves.append(-kernel_rate * jnp.sum(squares, axis=1, keepdims=True))
            new_ref[i * own : (i + 1) * own, :] = halves[-1]
    if prior_count:
        at = 0
        for prior_ref in prior_refs:
            image_ref[:, at : at + prior_ref.shape[1]] = prior_ref[...]
            at += prior_ref.shape[1]
    else:
        image_ref[...] = jnp.zeros_like(image_ref)
        if has_side:
            image_ref[:, :own] = (noise_level - 1.0 / STEP) * side_ref[...]
    for j, col_ref in enumerate(col_refs):
        field = unpack_rows(col_ref, probes, own, 0)
        norms = unpack_rows(col_ref, probes, own, 1).astype(jnp.float32)
        col_half = -kernel_rate * (norms[0:1] + norms[1:2] + norms[2:3])
        for i, row_ref in enumerate(row_refs):
            for k in range(own // CHUNK):
                part = slice(k * CHUNK, (k + 1) * CHUNK)
                place = slice(i * own + k * CHUNK, i * own + (k + 1) * CHUNK)
                cross = lax.dot_general(
                    row_ref[part, :], col_ref[:own, :], (((1,), (1,)), ((), ())), preferred_element_type=jnp.float32
                )
                kern = jnp.exp(2.0 * kernel_rate * cross + halves[i][part, :] + col_half).astype(jnp.bfloat16)
                tile_ref[place, j * own : (j + 1) * own] = kern
                image_ref[:, place] += lax.dot_general(
                    field, kern, (((1,), (1,)), ((), ())), preferred_element_type=jnp.float32
                )


def build(rows, cols, own, probes, halves=(), prior=(), side=None, weight=64):
    features = rows[0].shape[1]
    height, width = len(rows) * own, len(cols) * own
    counts = (len(rows), len(cols), len(halves), len(prior), side is not None)
    out_shape = [
        pltpu.VMEM((height, width), jnp.bfloat16),
        jax.ShapeDtypeStruct((probes, height), jnp.float32),
    ]
    if not halves:
        out_shape.append(jax.ShapeDtypeStruct((height, 1), jnp.float32))
    args = [*rows, *cols, *halves, *prior] + ([] if side is None else [side])
    return pl.pallas_call(
        functools.partial(tile_kernel, counts, probes),
        out_shape=out_shape,
        compiler_params=pltpu.CompilerParams(vmem_limit_bytes=8 << 20),
        cost_estimate=pl.CostEstimate(
            flops=height * width * features * weight // 8, bytes_accessed=1 << 10, transcendentals=0
        ),
        name="build_tile",
    )(*args)


def share_kernel(own, image_ref, *out_refs):
    probes = image_ref.shape[0]
    for k, out_ref in enumerate(out_refs, 1):
        for i in range(len(ROWS)):
            high, middle, _ = split(image_ref[:, i * own : (i + 1) * own])
            out_ref[i * probes : (i + 1) * probes, :] = high
            if i == k:
                out_ref[len(ROWS) * probes :, :] = middle


def share(image, own):
    probes = image.shape[0]
    height = (len(ROWS) + 1) * probes
    return pl.pallas_call(
        functools.partial(share_kernel, own),
        out_shape=[jax.ShapeDtypeStruct((height, own), jnp.bfloat16)] * (len(ROWS) - 1),
        compiler_params=pltpu.CompilerParams(vmem_limit_bytes=4 << 20),
        name="share",
    )(image)


def rho_kernel(own, *refs):
    parts, (rho_ref, narrow_ref) = refs[: len(ROWS)], refs[len(ROWS) :]
    probes = rho_ref.shape[0]
    for j, p in enumerate(ROWS):
        at = j * own
        piece = parts[0][:, at : at + own]
        for s, part in zip(ROWS[1:], parts[1:]):
            at = ROWS.index((p[0] ^ s[0], p[1] ^ s[1])) * probes
            piece = piece + part[at : at + probes, :].astype(jnp.float32)
            if p == HERE:
                piece = piece + part[len(ROWS) * probes :, :].astype(jnp.float32)
        rho = -STEP * piece
        if p == HERE:
            rho_ref[...] = rho
        high, low, _ = split(rho)
        narrow_ref[:probes, j * own : (j + 1) * own] = high
        narrow_ref[probes:, j * own : (j + 1) * own] = low


def sum_rows(parts, own):
    probes, rows = parts[0].shape
    return pl.pallas_call(
        functools.partial(rho_kernel, own),
        out_shape=[
            jax.ShapeDtypeStruct((probes, own), jnp.float32),
            jax.ShapeDtypeStruct((2 * probes, rows), jnp.bfloat16),
        ],
        compiler_params=pltpu.CompilerParams(vmem_limit_bytes=4 << 20),
        name="sum_rows",
    )(*parts)


def second_kernel(own, half, places, narrow_ref, *refs):
    tiles, out_ref = refs[: len(places)], refs[len(places)]
    probes = out_ref.shape[0]
    for j, (h, m) in enumerate(COLS):
        if h != half:
            continue
        part = 0.0
        for tile_ref, (top, left) in zip(tiles, places):
            at = j * own - left
            if 0 <= at < tile_ref.shape[1]:
                part = part + jnp.dot(
                    narrow_ref[:, top : top + tile_ref.shape[0]],
                    tile_ref[:, at : at + own],
                    preferred_element_type=jnp.float32,
                )
        out_ref[:, m * own : (m + 1) * own] = part[:probes] + part[probes:]


def second_product(tiles, narrow, own, half):
    height, rows = narrow.shape
    cols = len(SQUARE) * own
    places = [(top, left) for _, top, left in tiles]
    return pl.pallas_call(
        functools.partial(second_kernel, own, half, places),
        in_specs=[pl.BlockSpec(memory_space=pltpu.VMEM)] * (1 + len(tiles)),
        out_shape=jax.ShapeDtypeStruct((height // 2, cols), jnp.float32),
        compiler_params=pltpu.CompilerParams(vmem_limit_bytes=8 << 20),
        cost_estimate=pl.CostEstimate(flops=rows * cols * 32, bytes_accessed=1 << 10, transcendentals=0),
        name="second_product",
    )(narrow, *[tile for tile, _, _ in tiles])


def merge_kernel(own, mine_ref, other_ref, *out_refs):
    for m, out_ref in enumerate(out_refs):
        here = slice(m * own, (m + 1) * own)
        out_ref[...] = mine_ref[:, here] + other_ref[:, here]


def merge(mine, other, own):
    return pl.pallas_call(
        functools.partial(merge_kernel, own),
        out_shape=[jax.ShapeDtypeStruct((mine.shape[0], own), jnp.float32)] * len(SQUARE),
        compiler_params=pltpu.CompilerParams(vmem_limit_bytes=4 << 20),
        name="merge",
    )(mine, other)


def sums_kernel(side_ref, rho_ref, *refs):
    shares, (image_ref, sums_ref) = refs[: len(SQUARE)], refs[len(SQUARE) :]
    side, rho = side_ref[...], rho_ref[...]
    image = noise_level * rho
    for share in shares:
        image = image + share[...]
    image_ref[...] = image
    total = lambda a, b: jnp.sum(a * b, axis=1, keepdims=True)
    lane = lax.broadcasted_iota(jnp.int32, (side.shape[0], LANES), 1)
    sums = 0.0
    for k, one in enumerate((total(side, side), total(side, rho), total(rho, rho), total(rho, image))):
        sums = jnp.where(lane == k, one, sums)
    sums = sums.T
    sums_ref[...] = jnp.concatenate([sums[k : k + 1] for k in range(LANES // sums.shape[1])], axis=1)


def local_sums(side, rho, shares):
    return pl.pallas_call(
        sums_kernel,
        out_shape=[
            jax.ShapeDtypeStruct(side.shape, jnp.float32),
            jax.ShapeDtypeStruct((1, LANES), jnp.float32),
        ],
        compiler_params=pltpu.CompilerParams(vmem_limit_bytes=4 << 20),
        name="local_sums",
    )(side, rho, *shares)


def finish_kernel(side_ref, rho_ref, image_ref, sums_ref, field_ref, residual_ref):
    side, rho, image = side_ref[...], rho_ref[...], image_ref[...]
    probes = side.shape[0]
    sums = jnp.sum(sums_ref[...], axis=0, keepdims=True)
    sums = jnp.concatenate([sums[:, k * probes : (k + 1) * probes] for k in range(4)] * 2, axis=0).T
    rr, side_rho, rho_rho, rho_image = (sums[:, k : k + 1] for k in range(4))
    curve = (rr - side_rho) / STEP
    alpha = rr / curve
    turn = alpha / STEP
    rest = 1.0 - turn
    rr_next = rest * rest * rr + 2.0 * rest * turn * side_rho + turn * turn * rho_rho
    gain = rest + rr_next / rr
    cross = (side_rho - rho_rho) / STEP
    curve = gain * gain * curve + 2.0 * gain * turn * cross + turn * turn * rho_image
    alpha_next = rr_next / curve
    direction = gain * side + turn * rho
    field_ref[...] = alpha * side + alpha_next * direction
    residual_ref[...] = rest * side + turn * rho - alpha_next * (gain / STEP * (side - rho) + turn * image)


def finish(side, rho, image, sums):
    return pl.pallas_call(
        finish_kernel,
        out_shape=[jax.ShapeDtypeStruct(side.shape, jnp.float32)] * 2,
        compiler_params=pltpu.CompilerParams(vmem_limit_bytes=4 << 20),
        name="finish",
    )(side, rho, image, sums)


def on_device(states, offsets, right_side):
    own, probes = right_side.shape
    side = right_side.T
    points, message = front(states, offsets, side)
    with jax.named_scope("fetch_points"):
        rows = [points] + [swap(points, offset) for offset in ROWS[1:3]]
        cols = [message] + [swap(message, offset) for offset in SQUARE[1:]]
        first = [message, swap_core(message)]
        tile_a, image_a, half_a = build([points], first, own, probes, side=side, weight=1)
        (rows[1], rows[2], again), image_a = lax.optimization_barrier(((rows[1], rows[2], points), image_a))
        rows.append(swap(again, ROWS[3]))
        tile_b, image_b, half_b = build(rows[1:3], first, own, probes, weight=1)
        half = [half_a, half_b]

    with jax.named_scope("build_tiles"):
        cols[2], image_b = lax.optimization_barrier((cols[2], image_b))
        tile_c, image = build(rows[:3], cols[2:3], own, probes, half, [image_a, image_b])
        other_z = swap_core(cols[2])
        cols[1], image = lax.optimization_barrier((cols[1], image))
        tile_d, image = build(rows[:3], cols[1:2], own, probes, half, [image])
        other_y = swap_core(cols[1])
        others = [other_y, other_z]
        tile_e, image = build(rows[:3], [other_z], own, probes, half, [image])
        other_y, image = lax.optimization_barrier((other_y, image))
        tile_i, image = build(rows[:3], [other_y], own, probes, half, [image])
        rows[3], image = lax.optimization_barrier((rows[3], image))
        tile_f, image_far, half_far = build([rows[3]], first + cols[1:3] + others, own, probes)
        cols[3], image_far = lax.optimization_barrier((cols[3], image_far))
        last = swap_core(cols[3])
        half.append(half_far)
        tile_g, image = build(rows, [cols[3]], own, probes, half, [image, image_far])
        tile_h, image = build(rows, [last], own, probes, half, [image])
        tiles = [
            (tile_a, 0, 0),
            (tile_b, own, 0),
            (tile_d, 0, 2 * own),
            (tile_c, 0, 3 * own),
            (tile_i, 0, 4 * own),
            (tile_e, 0, 5 * own),
            (tile_f, 3 * own, 0),
            (tile_g, 0, 6 * own),
            (tile_h, 0, 7 * own),
        ]

    with jax.named_scope("sum_over_rows"):
        parts = [image] + swap_each(share(image, own), ROWS[1:])

    rho, narrow = sum_rows(parts, own)
    other = second_product(tiles, narrow, own, 1)
    narrow, other = lax.optimization_barrier((narrow, other))
    mine = second_product(tiles, narrow, own, 0)

    with jax.named_scope("sum_over_columns"):
        blocks = merge(mine, swap_core(other), own)
        shares = [blocks[0]] + swap_each(blocks[1:], SQUARE[1:])

    with jax.named_scope("final_sums"):
        image, sums = local_sums(side, rho, shares)
        sums = jnp.broadcast_to(sums, (NY * NZ * NC, LANES))
        sums = lax.all_to_all(sums, ("y", "z", "c"), 0, 0, tiled=True)

    field, residual = finish(side, rho, image, sums)
    return field.T, residual.T


def solution(mesh):
    fine = Mesh(mesh.devices.reshape(NY, NZ, NC, NX), ("y", "z", "c", "x"))
    rows = ("y", "z", "c")
    in_specs = (P(rows, None), P(rows), P(rows, "x"))
    out_specs = (P(rows, "x"), P(rows, "x"))
    return jax.shard_map(on_device, mesh=fine, in_specs=in_specs, out_specs=out_specs, check_vma=False)
```

```python
import functools

import jax
import jax.numpy as jnp
from jax import lax
from jax.experimental import pallas as pl
from jax.experimental.pallas import tpu as pltpu
from jax.sharding import Mesh
from jax.sharding import PartitionSpec as P

NY, NZ, NC, NX = 4, 4, 2, 4
LANES = 128
CHUNK = 256
HERE = (0, 0)
ROWS = (HERE, (1, 0), (0, 1), (1, 1))
SQUARE = (HERE, (3, 0), (0, 3), (3, 3))
COLS = ((0, 0), (1, 0), (0, 1), (0, 2), (1, 1), (1, 2), (0, 3), (1, 3))

noise_level = 1.0
kernel_rate = 0.5
STEP = 1.0 / (1.0 + noise_level)


def swap(value, offset):
    pairs = []
    for y in range(NY):
        for z in range(NZ):
            pairs.append((y * NZ + z, (y ^ offset[0]) * NZ + (z ^ offset[1])))
    return lax.ppermute(value, ("y", "z"), pairs)


def swap_each(values, offsets):
    received = [swap(value, offset) for value, offset in reversed(list(zip(values, offsets)))]
    return received[::-1]


def hand_on(along_y, along_z, offset):
    value = jnp.where(lax.axis_index("c") == 0, along_z, along_y)
    pairs = []
    for y in range(NY):
        for z in range(NZ):
            here = (y * NZ + z) * NC
            pairs += [(here, ((y ^ offset[0]) * NZ + z) * NC), (here + 1, (y * NZ + (z ^ offset[1])) * NC + 1)]
    return lax.ppermute(value, ("y", "z", "c"), pairs)


def swap_core(value):
    return lax.ppermute(value, "c", [(0, 1), (1, 0)])


def split(value):
    high = value.astype(jnp.bfloat16)
    rest = value - high.astype(jnp.float32)
    middle = rest.astype(jnp.bfloat16)
    return high, middle, (rest - middle.astype(jnp.float32)).astype(jnp.bfloat16)


def pack_kernel(points_ref, side_ref, out_ref):
    own, width = points_ref.shape
    probes = side_ref.shape[0]
    out_ref[:own, :] = points_ref[...]
    high, middle, _ = split(points_ref[...].astype(jnp.float32) ** 2)
    ones = jnp.ones((probes, width), jnp.bfloat16)
    norms = 0.0
    for term in (high, middle):
        norms = norms + lax.dot_general(ones, term, (((1,), (1,)), ((), ())), preferred_element_type=jnp.float32)
    high, middle, low = split(norms)
    row = lax.broadcasted_iota(jnp.int32, norms.shape, 0)
    norms = jnp.where(row == 0, high.astype(jnp.float32), jnp.where(row == 1, middle.astype(jnp.float32), low.astype(jnp.float32)))
    at = own
    for part in (side_ref[...], norms.astype(jnp.bfloat16)):
        for j in range(own // width):
            out_ref[at : at + probes, :] = part[:, j * width : (j + 1) * width]
            at += probes


def pack(points, side):
    own, width = points.shape
    extra = side.shape[0] * 2 * own // width
    return pl.pallas_call(
        pack_kernel,
        out_shape=jax.ShapeDtypeStruct((own + extra, width), jnp.bfloat16),
        compiler_params=pltpu.CompilerParams(vmem_limit_bytes=8 << 20),
        name="pack",
    )(points, side)


def unpack_rows(message, probes, own, term):
    width = message.shape[1]
    count = own // width
    at = own + term * count * probes
    return jnp.concatenate([message[at + j * probes : at + (j + 1) * probes] for j in range(count)], axis=1)


def tile_kernel(counts, probes, *refs):
    rows_count, cols_count, known_halves, prior_count, has_side = counts
    refs = list(refs)
    row_refs = [refs.pop(0) for _ in range(rows_count)]
    col_refs = [refs.pop(0) for _ in range(cols_count)]
    half_refs = [refs.pop(0) for _ in range(known_halves)]
    prior_refs = [refs.pop(0) for _ in range(prior_count)]
    side_ref = refs.pop(0) if has_side else None
    tile_ref, image_ref = refs.pop(0), refs.pop(0)
    own = tile_ref.shape[0] // rows_count
    if known_halves:
        pieces = []
        for half_ref in half_refs:
            pieces += [half_ref[j * own : (j + 1) * own, :] for j in range(half_ref.shape[0] // own)]
        halves = pieces
    else:
        new_ref = refs.pop(0)
        halves = []
        for i, row_ref in enumerate(row_refs):
            squares = row_ref[:own, :].astype(jnp.float32) ** 2
            halves.append(-kernel_rate * jnp.sum(squares, axis=1, keepdims=True))
            new_ref[i * own : (i + 1) * own, :] = halves[-1]
    if prior_count:
        at = 0
        for prior_ref in prior_refs:
            image_ref[:, at : at + prior_ref.shape[1]] = prior_ref[...]
            at += prior_ref.shape[1]
    else:
        image_ref[...] = jnp.zeros_like(image_ref)
        if has_side:
            image_ref[:, :own] = (noise_level - 1.0 / STEP) * side_ref[...]
    for j, col_ref in enumerate(col_refs):
        field = unpack_rows(col_ref, probes, own, 0)
        norms = unpack_rows(col_ref, probes, own, 1).astype(jnp.float32)
        col_half = -kernel_rate * (norms[0:1] + norms[1:2] + norms[2:3])
        for i, row_ref in enumerate(row_refs):
            for k in range(own // CHUNK):
                part = slice(k * CHUNK, (k + 1) * CHUNK)
                place = slice(i * own + k * CHUNK, i * own + (k + 1) * CHUNK)
                cross = lax.dot_general(
                    row_ref[part, :], col_ref[:own, :], (((1,), (1,)), ((), ())), preferred_element_type=jnp.float32
                )
                kern = jnp.exp(2.0 * kernel_rate * cross + halves[i][part, :] + col_half).astype(jnp.bfloat16)
                tile_ref[place, j * own : (j + 1) * own] = kern
                image_ref[:, place] += lax.dot_general(
                    field, kern, (((1,), (1,)), ((), ())), preferred_element_type=jnp.float32
                )


def build(rows, cols, own, probes, halves=(), prior=(), side=None, weight=64):
    features = rows[0].shape[1]
    height, width = len(rows) * own, len(cols) * own
    counts = (len(rows), len(cols), len(halves), len(prior), side is not None)
    out_shape = [
        pltpu.VMEM((height, width), jnp.bfloat16),
        jax.ShapeDtypeStruct((probes, height), jnp.float32),
    ]
    if not halves:
        out_shape.append(jax.ShapeDtypeStruct((height, 1), jnp.float32))
    args = [*rows, *cols, *halves, *prior] + ([] if side is None else [side])
    return pl.pallas_call(
        functools.partial(tile_kernel, counts, probes),
        out_shape=out_shape,
        compiler_params=pltpu.CompilerParams(vmem_limit_bytes=8 << 20),
        cost_estimate=pl.CostEstimate(
            flops=height * width * features * weight // 8, bytes_accessed=1 << 10, transcendentals=0
        ),
        name="build_tile",
    )(*args)


def share_kernel(own, image_ref, *out_refs):
    probes = image_ref.shape[0]
    for k, out_ref in enumerate(out_refs, 1):
        for i in range(len(ROWS)):
            high, middle, _ = split(image_ref[:, i * own : (i + 1) * own])
            out_ref[i * probes : (i + 1) * probes, :] = high
            if i == k:
                out_ref[len(ROWS) * probes :, :] = middle


def share(image, own):
    probes = image.shape[0]
    height = (len(ROWS) + 1) * probes
    return pl.pallas_call(
        functools.partial(share_kernel, own),
        out_shape=[jax.ShapeDtypeStruct((height, own), jnp.bfloat16)] * (len(ROWS) - 1),
        compiler_params=pltpu.CompilerParams(vmem_limit_bytes=4 << 20),
        name="share",
    )(image)


def rho_kernel(own, *refs):
    parts, (rho_ref, narrow_ref) = refs[: len(ROWS)], refs[len(ROWS) :]
    probes = rho_ref.shape[0]
    for j, p in enumerate(ROWS):
        at = j * own
        piece = parts[0][:, at : at + own]
        for s, part in zip(ROWS[1:], parts[1:]):
            at = ROWS.index((p[0] ^ s[0], p[1] ^ s[1])) * probes
            piece = piece + part[at : at + probes, :].astype(jnp.float32)
            if p == HERE:
                piece = piece + part[len(ROWS) * probes :, :].astype(jnp.float32)
        rho = -STEP * piece
        if p == HERE:
            rho_ref[...] = rho
        high, low, _ = split(rho)
        narrow_ref[:probes, j * own : (j + 1) * own] = high
        narrow_ref[probes:, j * own : (j + 1) * own] = low


def sum_rows(parts, own):
    probes, rows = parts[0].shape
    return pl.pallas_call(
        functools.partial(rho_kernel, own),
        out_shape=[
            jax.ShapeDtypeStruct((probes, own), jnp.float32),
            jax.ShapeDtypeStruct((2 * probes, rows), jnp.bfloat16),
        ],
        compiler_params=pltpu.CompilerParams(vmem_limit_bytes=4 << 20),
        name="sum_rows",
    )(*parts)


def second_kernel(own, half, places, narrow_ref, *refs):
    tiles, out_ref = refs[: len(places)], refs[len(places)]
    probes = out_ref.shape[0]
    for j, (h, m) in enumerate(COLS):
        if h != half:
            continue
        part = 0.0
        for tile_ref, (top, left) in zip(tiles, places):
            at = j * own - left
            if 0 <= at < tile_ref.shape[1]:
                part = part + jnp.dot(
                    narrow_ref[:, top : top + tile_ref.shape[0]],
                    tile_ref[:, at : at + own],
                    preferred_element_type=jnp.float32,
                )
        out_ref[:, m * own : (m + 1) * own] = part[:probes] + part[probes:]


def second_product(tiles, narrow, own, half):
    height, rows = narrow.shape
    cols = len(SQUARE) * own
    places = [(top, left) for _, top, left in tiles]
    return pl.pallas_call(
        functools.partial(second_kernel, own, half, places),
        in_specs=[pl.BlockSpec(memory_space=pltpu.VMEM)] * (1 + len(tiles)),
        out_shape=jax.ShapeDtypeStruct((height // 2, cols), jnp.float32),
        compiler_params=pltpu.CompilerParams(vmem_limit_bytes=8 << 20),
        cost_estimate=pl.CostEstimate(flops=rows * cols * 32, bytes_accessed=1 << 10, transcendentals=0),
        name="second_product",
    )(narrow, *[tile for tile, _, _ in tiles])


def merge_kernel(own, mine_ref, other_ref, *out_refs):
    for m, out_ref in enumerate(out_refs):
        here = slice(m * own, (m + 1) * own)
        out_ref[...] = mine_ref[:, here] + other_ref[:, here]


def merge(mine, other, own):
    return pl.pallas_call(
        functools.partial(merge_kernel, own),
        out_shape=[jax.ShapeDtypeStruct((mine.shape[0], own), jnp.float32)] * len(SQUARE),
        compiler_params=pltpu.CompilerParams(vmem_limit_bytes=4 << 20),
        name="merge",
    )(mine, other)


def sums_kernel(side_ref, rho_ref, *refs):
    shares, (image_ref, sums_ref) = refs[: len(SQUARE)], refs[len(SQUARE) :]
    side, rho = side_ref[...], rho_ref[...]
    image = noise_level * rho
    for share in shares:
        image = image + share[...]
    image_ref[...] = image
    total = lambda a, b: jnp.sum(a * b, axis=1, keepdims=True)
    lane = lax.broadcasted_iota(jnp.int32, (side.shape[0], LANES), 1)
    sums = 0.0
    for k, one in enumerate((total(side, side), total(side, rho), total(rho, rho), total(rho, image))):
        sums = jnp.where(lane == k, one, sums)
    sums = sums.T
    sums_ref[...] = jnp.concatenate([sums[k : k + 1] for k in range(LANES // sums.shape[1])], axis=1)


def local_sums(side, rho, shares):
    return pl.pallas_call(
        sums_kernel,
        out_shape=[
            jax.ShapeDtypeStruct(side.shape, jnp.float32),
            jax.ShapeDtypeStruct((1, LANES), jnp.float32),
        ],
        compiler_params=pltpu.CompilerParams(vmem_limit_bytes=4 << 20),
        name="local_sums",
    )(side, rho, *shares)


def finish_kernel(side_ref, rho_ref, image_ref, sums_ref, field_ref, residual_ref):
    side, rho, image = side_ref[...], rho_ref[...], image_ref[...]
    probes = side.shape[0]
    sums = jnp.sum(sums_ref[...], axis=0, keepdims=True)
    sums = jnp.concatenate([sums[:, k * probes : (k + 1) * probes] for k in range(4)] * 2, axis=0).T
    rr, side_rho, rho_rho, rho_image = (sums[:, k : k + 1] for k in range(4))
    curve = (rr - side_rho) / STEP
    alpha = rr / curve
    turn = alpha / STEP
    rest = 1.0 - turn
    rr_next = rest * rest * rr + 2.0 * rest * turn * side_rho + turn * turn * rho_rho
    gain = rest + rr_next / rr
    cross = (side_rho - rho_rho) / STEP
    curve = gain * gain * curve + 2.0 * gain * turn * cross + turn * turn * rho_image
    alpha_next = rr_next / curve
    direction = gain * side + turn * rho
    field_ref[...] = alpha * side + alpha_next * direction
    residual_ref[...] = rest * side + turn * rho - alpha_next * (gain / STEP * (side - rho) + turn * image)


def finish(side, rho, image, sums):
    return pl.pallas_call(
        finish_kernel,
        out_shape=[jax.ShapeDtypeStruct(side.shape, jnp.float32)] * 2,
        compiler_params=pltpu.CompilerParams(vmem_limit_bytes=4 << 20),
        name="finish",
    )(side, rho, image, sums)


def on_device(states, offsets, right_side):
    own, probes = right_side.shape
    side = right_side.T
    points = lax.dynamic_slice_in_dim(states, offsets[0], own, 0)
    with jax.named_scope("fetch_points"):
        message = pack(points, side.astype(jnp.bfloat16))
        rows = [points] + [swap(points, offset) for offset in ROWS[1:3]]
        cols = [message] + [swap(message, offset) for offset in SQUARE[1:]]
        first = [message, swap_core(message)]
        tile_a, image_a, half_a = build([points], first, own, probes, side=side, weight=1)
        (rows[1], rows[2]), image_a = lax.optimization_barrier(((rows[1], rows[2]), image_a))
        rows.append(hand_on(rows[1], rows[2], ROWS[3]))
        tile_b, image_b, half_b = build(rows[1:3], first, own, probes, weight=1)
        half = [half_a, half_b]

    with jax.named_scope("build_tiles"):
        cols[2], image_b = lax.optimization_barrier((cols[2], image_b))
        tile_c, image = build(rows[:3], cols[2:3], own, probes, half, [image_a, image_b])
        other_z = swap_core(cols[2])
        cols[1], image = lax.optimization_barrier((cols[1], image))
        tile_d, image = build(rows[:3], cols[1:2], own, probes, half, [image])
        other_y = swap_core(cols[1])
        others = [other_y, other_z]
        tile_e, image = build(rows[:3], [other_z], own, probes, half, [image])
        other_y, image = lax.optimization_barrier((other_y, image))
        tile_i, image = build(rows[:3], [other_y], own, probes, half, [image])
        rows[3], image = lax.optimization_barrier((rows[3], image))
        tile_f, image_far, half_far = build([rows[3]], first + cols[1:3] + others, own, probes)
        cols[3], image_far = lax.optimization_barrier((cols[3], image_far))
        last = swap_core(cols[3])
        half.append(half_far)
        tile_g, image = build(rows, [cols[3]], own, probes, half, [image, image_far])
        tile_h, image = build(rows, [last], own, probes, half, [image])
        tiles = [
            (tile_a, 0, 0),
            (tile_b, own, 0),
            (tile_d, 0, 2 * own),
            (tile_c, 0, 3 * own),
            (tile_i, 0, 4 * own),
            (tile_e, 0, 5 * own),
            (tile_f, 3 * own, 0),
            (tile_g, 0, 6 * own),
            (tile_h, 0, 7 * own),
        ]

    with jax.named_scope("sum_over_rows"):
        parts = [image] + swap_each(share(image, own), ROWS[1:])

    rho, narrow = sum_rows(parts, own)
    other = second_product(tiles, narrow, own, 1)
    narrow, other = lax.optimization_barrier((narrow, other))
    mine = second_product(tiles, narrow, own, 0)

    with jax.named_scope("sum_over_columns"):
        blocks = merge(mine, swap_core(other), own)
        shares = [blocks[0]] + swap_each(blocks[1:], SQUARE[1:])

    with jax.named_scope("final_sums"):
        image, sums = local_sums(side, rho, shares)
        sums = jnp.broadcast_to(sums, (NY * NZ * NC, LANES))
        sums = lax.all_to_all(sums, ("y", "z", "c"), 0, 0, tiled=True)

    field, residual = finish(side, rho, image, sums)
    return field.T, residual.T


def solution(mesh):
    fine = Mesh(mesh.devices.reshape(NY, NZ, NC, NX), ("y", "z", "c", "x"))
    rows = ("y", "z", "c")
    in_specs = (P(rows, None), P(rows), P(rows, "x"))
    out_specs = (P(rows, "x"), P(rows, "x"))
    return jax.shard_map(on_device, mesh=fine, in_specs=in_specs, out_specs=out_specs, check_vma=False)
```

```python
import functools

import jax
import jax.numpy as jnp
from jax import lax
from jax.experimental import pallas as pl
from jax.experimental.pallas import tpu as pltpu
from jax.sharding import Mesh
from jax.sharding import PartitionSpec as P

NY, NZ, NC, NX = 4, 4, 2, 4
LANES = 128
CHUNK = 256
HERE = (0, 0)
ROWS = (HERE, (1, 0), (0, 1), (1, 1))
SQUARE = (HERE, (3, 0), (0, 3), (3, 3))
COLS = ((0, 0), (1, 0), (0, 1), (0, 2), (1, 1), (1, 2), (0, 3), (1, 3))

noise_level = 1.0
kernel_rate = 0.5
STEP = 1.0 / (1.0 + noise_level)


def swap(value, offset):
    pairs = []
    for y in range(NY):
        for z in range(NZ):
            pairs.append((y * NZ + z, (y ^ offset[0]) * NZ + (z ^ offset[1])))
    return lax.ppermute(value, ("y", "z"), pairs)


def swap_each(values, offsets):
    received = [swap(value, offset) for value, offset in reversed(list(zip(values, offsets)))]
    return received[::-1]


def swap_core(value):
    return lax.ppermute(value, "c", [(0, 1), (1, 0)])


def split(value):
    high = value.astype(jnp.bfloat16)
    rest = value - high.astype(jnp.float32)
    middle = rest.astype(jnp.bfloat16)
    return high, middle, (rest - middle.astype(jnp.float32)).astype(jnp.bfloat16)


def pack_kernel(points_ref, side_ref, out_ref):
    own, width = points_ref.shape
    probes = side_ref.shape[0]
    out_ref[:own, :] = points_ref[...]
    high, middle, _ = split(points_ref[...].astype(jnp.float32) ** 2)
    ones = jnp.ones((probes, width), jnp.bfloat16)
    norms = 0.0
    for term in (high, middle):
        norms = norms + lax.dot_general(ones, term, (((1,), (1,)), ((), ())), preferred_element_type=jnp.float32)
    high, middle, low = split(norms)
    row = lax.broadcasted_iota(jnp.int32, norms.shape, 0)
    norms = jnp.where(row == 0, high.astype(jnp.float32), jnp.where(row == 1, middle.astype(jnp.float32), low.astype(jnp.float32)))
    at = own
    for part in (side_ref[...], norms.astype(jnp.bfloat16)):
        for j in range(own // width):
            out_ref[at : at + probes, :] = part[:, j * width : (j + 1) * width]
            at += probes


def pack(points, side):
    own, width = points.shape
    extra = side.shape[0] * 2 * own // width
    return pl.pallas_call(
        pack_kernel,
        out_shape=jax.ShapeDtypeStruct((own + extra, width), jnp.bfloat16),
        compiler_params=pltpu.CompilerParams(vmem_limit_bytes=8 << 20),
        name="pack",
    )(points, side)


def unpack_rows(message, probes, own, term):
    width = message.shape[1]
    count = own // width
    at = own + term * count * probes
    return jnp.concatenate([message[at + j * probes : at + (j + 1) * probes] for j in range(count)], axis=1)


def tile_kernel(counts, probes, *refs):
    rows_count, cols_count, known_halves, prior_count, has_side = counts
    refs = list(refs)
    row_refs = [refs.pop(0) for _ in range(rows_count)]
    col_refs = [refs.pop(0) for _ in range(cols_count)]
    half_refs = [refs.pop(0) for _ in range(known_halves)]
    prior_refs = [refs.pop(0) for _ in range(prior_count)]
    side_ref = refs.pop(0) if has_side else None
    tile_ref, image_ref = refs.pop(0), refs.pop(0)
    own = tile_ref.shape[0] // rows_count
    if known_halves:
        pieces = []
        for half_ref in half_refs:
            pieces += [half_ref[j * own : (j + 1) * own, :] for j in range(half_ref.shape[0] // own)]
        halves = pieces
    else:
        new_ref = refs.pop(0)
        halves = []
        for i, row_ref in enumerate(row_refs):
            squares = row_ref[:own, :].astype(jnp.float32) ** 2
            halves.append(-kernel_rate * jnp.sum(squares, axis=1, keepdims=True))
            new_ref[i * own : (i + 1) * own, :] = halves[-1]
    if prior_count:
        at = 0
        for prior_ref in prior_refs:
            image_ref[:, at : at + prior_ref.shape[1]] = prior_ref[...]
            at += prior_ref.shape[1]
    else:
        image_ref[...] = jnp.zeros_like(image_ref)
        if has_side:
            image_ref[:, :own] = (noise_level - 1.0 / STEP) * side_ref[...]
    for j, col_ref in enumerate(col_refs):
        field = unpack_rows(col_ref, probes, own, 0)
        norms = unpack_rows(col_ref, probes, own, 1).astype(jnp.float32)
        col_half = -kernel_rate * (norms[0:1] + norms[1:2] + norms[2:3])
        for i, row_ref in enumerate(row_refs):
            for k in range(own // CHUNK):
                part = slice(k * CHUNK, (k + 1) * CHUNK)
                place = slice(i * own + k * CHUNK, i * own + (k + 1) * CHUNK)
                cross = lax.dot_general(
                    row_ref[part, :], col_ref[:own, :], (((1,), (1,)), ((), ())), preferred_element_type=jnp.float32
                )
                kern = jnp.exp(2.0 * kernel_rate * cross + halves[i][part, :] + col_half).astype(jnp.bfloat16)
                tile_ref[place, j * own : (j + 1) * own] = kern
                image_ref[:, place] += lax.dot_general(
                    field, kern, (((1,), (1,)), ((), ())), preferred_element_type=jnp.float32
                )


def build(rows, cols, own, probes, halves=(), prior=(), side=None, weight=64):
    features = rows[0].shape[1]
    height, width = len(rows) * own, len(cols) * own
    counts = (len(rows), len(cols), len(halves), len(prior), side is not None)
    out_shape = [
        pltpu.VMEM((height, width), jnp.bfloat16),
        jax.ShapeDtypeStruct((probes, height), jnp.float32),
    ]
    if not halves:
        out_shape.append(jax.ShapeDtypeStruct((height, 1), jnp.float32))
    args = [*rows, *cols, *halves, *prior] + ([] if side is None else [side])
    return pl.pallas_call(
        functools.partial(tile_kernel, counts, probes),
        out_shape=out_shape,
        compiler_params=pltpu.CompilerParams(vmem_limit_bytes=8 << 20),
        cost_estimate=pl.CostEstimate(
            flops=height * width * features * weight // 8, bytes_accessed=1 << 10, transcendentals=0
        ),
        name="build_tile",
    )(*args)


def share_kernel(own, image_ref, *out_refs):
    probes = image_ref.shape[0]
    for k, out_ref in enumerate(out_refs, 1):
        for i in range(len(ROWS)):
            high, middle, _ = split(image_ref[:, i * own : (i + 1) * own])
            out_ref[i * probes : (i + 1) * probes, :] = high
            if i == k:
                out_ref[len(ROWS) * probes :, :] = middle


def share(image, own):
    probes = image.shape[0]
    height = (len(ROWS) + 1) * probes
    return pl.pallas_call(
        functools.partial(share_kernel, own),
        out_shape=[jax.ShapeDtypeStruct((height, own), jnp.bfloat16)] * (len(ROWS) - 1),
        compiler_params=pltpu.CompilerParams(vmem_limit_bytes=4 << 20),
        name="share",
    )(image)


def rho_kernel(own, *refs):
    parts, (rho_ref, narrow_ref) = refs[: len(ROWS)], refs[len(ROWS) :]
    probes = rho_ref.shape[0]
    for j, p in enumerate(ROWS):
        at = j * own
        piece = parts[0][:, at : at + own]
        for s, part in zip(ROWS[1:], parts[1:]):
            at = ROWS.index((p[0] ^ s[0], p[1] ^ s[1])) * probes
            piece = piece + part[at : at + probes, :].astype(jnp.float32)
            if p == HERE:
                piece = piece + part[len(ROWS) * probes :, :].astype(jnp.float32)
        rho = -STEP * piece
        if p == HERE:
            rho_ref[...] = rho
        high, low, _ = split(rho)
        narrow_ref[:probes, j * own : (j + 1) * own] = high
        narrow_ref[probes:, j * own : (j + 1) * own] = low


def sum_rows(parts, own):
    probes, rows = parts[0].shape
    return pl.pallas_call(
        functools.partial(rho_kernel, own),
        out_shape=[
            jax.ShapeDtypeStruct((probes, own), jnp.float32),
            jax.ShapeDtypeStruct((2 * probes, rows), jnp.bfloat16),
        ],
        compiler_params=pltpu.CompilerParams(vmem_limit_bytes=4 << 20),
        name="sum_rows",
    )(*parts)


def second_kernel(own, half, places, narrow_ref, *refs):
    tiles, out_ref = refs[: len(places)], refs[len(places)]
    probes = out_ref.shape[0]
    for j, (h, m) in enumerate(COLS):
        if h != half:
            continue
        part = 0.0
        for tile_ref, (top, left) in zip(tiles, places):
            at = j * own - left
            if 0 <= at < tile_ref.shape[1]:
                part = part + jnp.dot(
                    narrow_ref[:, top : top + tile_ref.shape[0]],
                    tile_ref[:, at : at + own],
                    preferred_element_type=jnp.float32,
                )
        out_ref[:, m * own : (m + 1) * own] = part[:probes] + part[probes:]


def second_product(tiles, narrow, own, half):
    height, rows = narrow.shape
    cols = len(SQUARE) * own
    places = [(top, left) for _, top, left in tiles]
    return pl.pallas_call(
        functools.partial(second_kernel, own, half, places),
        in_specs=[pl.BlockSpec(memory_space=pltpu.VMEM)] * (1 + len(tiles)),
        out_shape=jax.ShapeDtypeStruct((height // 2, cols), jnp.float32),
        compiler_params=pltpu.CompilerParams(vmem_limit_bytes=8 << 20),
        cost_estimate=pl.CostEstimate(flops=rows * cols * 32, bytes_accessed=1 << 10, transcendentals=0),
        name="second_product",
    )(narrow, *[tile for tile, _, _ in tiles])


def merge_kernel(own, mine_ref, other_ref, *out_refs):
    for m, out_ref in enumerate(out_refs):
        here = slice(m * own, (m + 1) * own)
        out_ref[...] = mine_ref[:, here] + other_ref[:, here]


def merge(mine, other, own):
    return pl.pallas_call(
        functools.partial(merge_kernel, own),
        out_shape=[jax.ShapeDtypeStruct((mine.shape[0], own), jnp.float32)] * len(SQUARE),
        compiler_params=pltpu.CompilerParams(vmem_limit_bytes=4 << 20),
        name="merge",
    )(mine, other)


def sums_kernel(side_ref, rho_ref, *refs):
    shares, (image_ref, sums_ref) = refs[: len(SQUARE)], refs[len(SQUARE) :]
    side, rho = side_ref[...], rho_ref[...]
    image = noise_level * rho
    for share in shares:
        image = image + share[...]
    image_ref[...] = image
    total = lambda a, b: jnp.sum(a * b, axis=1, keepdims=True)
    lane = lax.broadcasted_iota(jnp.int32, (side.shape[0], LANES), 1)
    sums = 0.0
    for k, one in enumerate((total(side, side), total(side, rho), total(rho, rho), total(rho, image))):
        sums = jnp.where(lane == k, one, sums)
    sums = sums.T
    sums_ref[...] = jnp.concatenate([sums[k : k + 1] for k in range(LANES // sums.shape[1])], axis=1)


def local_sums(side, rho, shares):
    return pl.pallas_call(
        sums_kernel,
        out_shape=[
            jax.ShapeDtypeStruct(side.shape, jnp.float32),
            jax.ShapeDtypeStruct((1, LANES), jnp.float32),
        ],
        compiler_params=pltpu.CompilerParams(vmem_limit_bytes=4 << 20),
        name="local_sums",
    )(side, rho, *shares)


def finish_kernel(side_ref, rho_ref, image_ref, sums_ref, field_ref, residual_ref):
    side, rho, image = side_ref[...], rho_ref[...], image_ref[...]
    probes = side.shape[0]
    sums = jnp.sum(sums_ref[...], axis=0, keepdims=True)
    sums = jnp.concatenate([sums[:, k * probes : (k + 1) * probes] for k in range(4)] * 2, axis=0).T
    rr, side_rho, rho_rho, rho_image = (sums[:, k : k + 1] for k in range(4))
    curve = (rr - side_rho) / STEP
    alpha = rr / curve
    turn = alpha / STEP
    rest = 1.0 - turn
    rr_next = rest * rest * rr + 2.0 * rest * turn * side_rho + turn * turn * rho_rho
    gain = rest + rr_next / rr
    cross = (side_rho - rho_rho) / STEP
    curve = gain * gain * curve + 2.0 * gain * turn * cross + turn * turn * rho_image
    alpha_next = rr_next / curve
    direction = gain * side + turn * rho
    field_ref[...] = alpha * side + alpha_next * direction
    residual_ref[...] = rest * side + turn * rho - alpha_next * (gain / STEP * (side - rho) + turn * image)


def finish(side, rho, image, sums):
    return pl.pallas_call(
        finish_kernel,
        out_shape=[jax.ShapeDtypeStruct(side.shape, jnp.float32)] * 2,
        compiler_params=pltpu.CompilerParams(vmem_limit_bytes=4 << 20),
        name="finish",
    )(side, rho, image, sums)


def on_device(states, offsets, right_side):
    own, probes = right_side.shape
    side = right_side.T
    points = lax.dynamic_slice_in_dim(states, offsets[0], own, 0)
    with jax.named_scope("fetch_points"):
        message = pack(points, side.astype(jnp.bfloat16))
        rows = [points] + [swap(points, offset) for offset in ROWS[1:3]]
        cols = [message] + [swap(message, offset) for offset in SQUARE[1:]]
        first = [message, swap_core(message)]
        tile_a, image_a, half_a = build([points], first, own, probes, side=side, weight=1)
        (rows[1], rows[2], again), image_a = lax.optimization_barrier(((rows[1], rows[2], points), image_a))
        rows.append(swap(again, ROWS[3]))
        tile_b, image_b, half_b = build(rows[1:3], first, own, probes, weight=1)
        half = [half_a, half_b]

    with jax.named_scope("build_tiles"):
        cols[2], image_b = lax.optimization_barrier((cols[2], image_b))
        tile_c, image = build(rows[:3], cols[2:3], own, probes, half, [image_a, image_b])
        other_z = swap_core(cols[2])
        cols[1], image = lax.optimization_barrier((cols[1], image))
        tile_d, image = build(rows[:3], cols[1:2], own, probes, half, [image])
        other_y = swap_core(cols[1])
        others = [other_y, other_z]
        tile_e, image = build(rows[:3], [other_z], own, probes, half, [image])
        other_y, image = lax.optimization_barrier((other_y, image))
        tile_i, image = build(rows[:3], [other_y], own, probes, half, [image])
        rows[3], image = lax.optimization_barrier((rows[3], image))
        tile_f, image_far, half_far = build([rows[3]], first + cols[1:3] + others, own, probes)
        cols[3], image_far = lax.optimization_barrier((cols[3], image_far))
        last = swap_core(cols[3])
        half.append(half_far)
        tile_g, image = build(rows, [cols[3]], own, probes, half, [image, image_far])
        tile_h, image = build(rows, [last], own, probes, half, [image])
        tiles = [
            (tile_a, 0, 0),
            (tile_b, own, 0),
            (tile_d, 0, 2 * own),
            (tile_c, 0, 3 * own),
            (tile_i, 0, 4 * own),
            (tile_e, 0, 5 * own),
            (tile_f, 3 * own, 0),
            (tile_g, 0, 6 * own),
            (tile_h, 0, 7 * own),
        ]

    with jax.named_scope("sum_over_rows"):
        parts = [image] + swap_each(share(image, own), ROWS[1:])

    rho, narrow = sum_rows(parts, own)
    other = second_product(tiles, narrow, own, 1)
    narrow, other = lax.optimization_barrier((narrow, other))
    mine = second_product(tiles, narrow, own, 0)

    with jax.named_scope("sum_over_columns"):
        blocks = merge(mine, swap_core(other), own)
        shares = [blocks[0]] + swap_each(blocks[:0:-1], SQUARE[:0:-1])

    with jax.named_scope("final_sums"):
        image, sums = local_sums(side, rho, shares)
        sums = jnp.broadcast_to(sums, (NY * NZ * NC, LANES))
        sums = lax.all_to_all(sums, ("y", "z", "c"), 0, 0, tiled=True)

    field, residual = finish(side, rho, image, sums)
    return field.T, residual.T


def solution(mesh):
    fine = Mesh(mesh.devices.reshape(NY, NZ, NC, NX), ("y", "z", "c", "x"))
    rows = ("y", "z", "c")
    in_specs = (P(rows, None), P(rows), P(rows, "x"))
    out_specs = (P(rows, "x"), P(rows, "x"))
    return jax.shard_map(on_device, mesh=fine, in_specs=in_specs, out_specs=out_specs, check_vma=False)
```
